512 devices in a mesh: tm: 16 (over z_lo, x), space: 32 (over z_hi, y, core).
Axes of the slice: x: 4, y: 4, z: 16 (z_hi: 4, z_lo: 4; z = z_hi * 4 + z_lo), core: 2. Of those that a mesh axis runs over, the one named last changes fastest.
Arguments:
- end_state: float32 [16, 64, 512, 128], P('tm', 'space'), may hold values from -8 to 8, as said below
- cond: float32 [64, 512, 128], P('space'), may hold values from 0.2 to 2
- receivers: int32 [16, 256], P('tm'), may hold values from 0 to 4194303
- residuals: float32 [16, 256], P('tm'), may hold values from -6 to 6
Outputs:
- corrected: float32 [16, 64, 512, 128], P('tm', 'space')
The draws below stay inside these ranges and needn't reach their ends.
Inputs may be any that keep to these rules, and one draw needn't show every extreme that they name: `end_state`: each slice's field is a rough part plus a part that varies slowly over the grid.
All inputs are finite; a program needn't handle non-finite values.
Results may differ from the reference program's by a relative error of at most 0.00002.
Values sent between devices are 32-bit elements; how exact they have to be, the bound alone decides.
No kernel may reach another device: no remote copies, remote signals or barrier semaphores. Data moves between devices by JAX's collectives and lax.ppermute only.
A program may use at most 64 MiB of HBM per device.

```python
import math
import jax
import jax.numpy as jnp
from jax import lax

NY = 512
NZ = 128
NREC = 256
FINE_STEPS = 2
SWEEPS = 2
SLICES = 16
NX = 64


def draw_end_state(key, part):
    rough_key, scale_key = jax.random.split(key)
    shape_full = (SLICES, NX, NY, NZ)
    rough_part = jnp.clip(jax.random.normal(rough_key, shape_full, jnp.float32), -5.0, 5.0)
    height = 2.0
    amplitude = jax.random.uniform(scale_key, (SLICES, 1, 1, 1), jnp.float32, 0.5, 1.5)
    along_x = jnp.sin(math.pi * (jnp.arange(NX, dtype=jnp.float32) + 0.5) / NX)
    along_y = jnp.sin(math.pi * (jnp.arange(NY, dtype=jnp.float32) + 0.5) / NY)
    along_z = jnp.sin(math.pi * (jnp.arange(NZ, dtype=jnp.float32) + 0.5) / NZ)
    smooth = along_x[:, None, None] * along_y[None, :, None] * along_z[None, None, :]
    return 0.7 * rough_part + height * amplitude * smooth[None]


def touch_ends(entries, key, smallest, top_value):
    place = [jax.random.randint(jax.random.fold_in(key, axis), (), 0, length) for axis, length in enumerate(entries.shape)]
    longest = entries.shape.index(max(entries.shape))
    neighbour = place[:longest] + [(place[longest] + 1) % entries.shape[longest]] + place[longest + 1:]
    return entries.at[tuple(place)].set(smallest).at[tuple(neighbour)].set(top_value)


def levels(own_key, dims, cuts, smallest, high):
    factor_of = 1.0
    for dim, shards_of in cuts:
        heights = jax.random.uniform(jax.random.fold_in(jax.random.fold_in(own_key, 6), dim), (shards_of,), jnp.float32, smallest / len(cuts), high / len(cuts))
        factor_of = factor_of * jnp.repeat(jnp.exp(heights), dims[dim] // shards_of).reshape((-1,) + (1,) * (len(dims) - 1 - dim))
    return factor_of


def noise(key, dims, width, reach, cuts=(), kind=jnp.bfloat16):
    result = width * jax.random.normal(key, dims, jnp.float32)
    if cuts:
        result = result * levels(key, dims, cuts, -0.22, 0.18)
    return jnp.clip(result, -reach, reach).astype(kind)


def setup_inputs(seed: int = 0) -> dict:
    streams_of = jax.random.split(jax.random.key(seed), 5)
    return {
        "end_state": draw_end_state(jax.random.fold_in(streams_of[4], 71), 0),
        "cond": jnp.clip(jnp.exp(math.log(2.0) - 2.3025851 * jax.random.uniform(streams_of[1], (NX, NY, NZ), jnp.float32) ** levels(streams_of[1], (NX, NY, NZ), ((0, 32),), -0.2, 0.2)), 0.2, 2.0),
        "receivers": touch_ends(jax.random.randint(streams_of[2], (SLICES, NREC), 0, NX * NY * NZ), jax.random.fold_in(streams_of[2], 1), 0, (NX * NY * NZ) - 1).astype(jnp.int32),
        "residuals": noise(streams_of[3], (SLICES, NREC), 1.0, 6.0, ((0, 16),), jnp.float32),
    }


def neighbors(padded):
    center = padded[1:-1]
    beside_all = padded[2:] + padded[:-2]
    planes = jnp.pad(center, ((0, 0), (1, 1), (1, 1)))
    beside_all = beside_all + planes[:, 2:, 1:-1] + planes[:, :-2, 1:-1]
    beside_all = beside_all + planes[:, 1:-1, 2:] + planes[:, 1:-1, :-2]
    return beside_all


def full_neighbors(field):
    return neighbors(jnp.pad(field, ((1, 1), (0, 0), (0, 0))))


def restrict(field):
    blocks = field.reshape(field.shape[0] // 2, 2, field.shape[1] // 2, 2, field.shape[2] // 2, 2)
    return blocks.mean(axis=(1, 3, 5))


def prolong(coarse):
    return jnp.repeat(jnp.repeat(jnp.repeat(coarse, 2, axis=0), 2, axis=1), 2, axis=2)


def fine_propagate(field_now, cond, source):
    diagonal = cond + 6.0
    for step_index in range(FINE_STEPS):
        rhs_term = cond * field_now + source
        for sweep_index in range(SWEEPS):
            field_now = (rhs_term + full_neighbors(field_now)) / diagonal
    return field_now


def coarse_propagate(field_now, coarse_cond):
    diagonal = coarse_cond + 1.5
    rhs_term = coarse_cond * field_now
    for sweep_index in range(SWEEPS):
        field_now = (rhs_term + 0.25 * full_neighbors(field_now)) / diagonal
    return field_now


def reference(end_state, cond, receivers, residuals):
    coarse_cond = restrict(cond) / FINE_STEPS

    def slice_terms(packed):
        start_field, cell_ids, values = packed
        source = jnp.zeros((NX * NY * NZ,), jnp.float32).at[cell_ids].add(values).reshape(NX, NY, NZ)
        fine_state = fine_propagate(start_field, cond, source)
        correction = fine_state - prolong(coarse_propagate(restrict(start_field), coarse_cond))
        return correction, restrict(correction)

    corrections, coarse_terms = lax.map(slice_terms, (end_state, receivers, residuals))
    start_coarse = restrict(end_state[SLICES - 1])

    def backward(incoming, packed):
        correction, coarse_term = packed
        propagated = coarse_propagate(incoming, coarse_cond)
        return coarse_term + propagated, prolong(propagated) + correction

    final_carry, corrected = lax.scan(backward, start_coarse, (corrections, coarse_terms), reverse=True)
    return corrected
```

```python
import jax
import jax.numpy as jnp
from jax import lax
from jax.experimental import pallas as pl
from jax.experimental.pallas import tpu as pltpu
from jax.sharding import PartitionSpec as P

FINE_STEPS = 2
SWEEPS = 2
SLABS = 32
SLICES = 16
PLANE = 128
BLOCK = 4
EXACT = lax.Precision.HIGHEST


def params():
    return pltpu.CompilerParams(vmem_limit_bytes=40 * 1024 * 1024)


def halving(half):
    row = lax.broadcasted_iota(jnp.int32, (128, 128), 0)
    lane = lax.broadcasted_iota(jnp.int32, (128, 128), 1)
    return jnp.where(lane == row // 2 + 64 * half, 0.125, 0.0).astype(jnp.float32)


def restrict_kernel(field_ref, out_ref):
    total = jnp.zeros((PLANE, 128), jnp.float32)
    for half in range(2):
        rows = None
        for plane in range(2):
            for r in range(2):
                part = field_ref[plane, pl.ds(2 * half + r, PLANE, stride=4), :]
                rows = part if rows is None else rows + part
        total = total + jnp.dot(rows, halving(half), precision=EXACT, preferred_element_type=jnp.float32)
    out_ref[...] = total


def restrict(field):
    return pl.pallas_call(
        restrict_kernel,
        out_shape=jax.ShapeDtypeStruct((PLANE, 128), jnp.float32),
        compiler_params=params(),
    )(field)


def prolong_add_kernel(delta_ref, field_ref, out_ref):
    row = lax.broadcasted_iota(jnp.int32, (128, 128), 0)
    lane = lax.broadcasted_iota(jnp.int32, (128, 128), 1)
    delta = delta_ref[...]
    for half in range(2):
        spread = jnp.where(row == lane // 2 + 64 * half, 1.0, 0.0).astype(jnp.float32)
        wide = jnp.dot(delta, spread, precision=EXACT, preferred_element_type=jnp.float32)
        for plane in range(2):
            for r in range(2):
                rows = pl.ds(2 * half + r, PLANE, stride=4)
                out_ref[plane, rows, :] = field_ref[plane, rows, :] + wide


def prolong_add(delta, field):
    return pl.pallas_call(
        prolong_add_kernel,
        out_shape=jax.ShapeDtypeStruct(field.shape, jnp.float32),
        compiler_params=params(),
    )(delta, field)


def lanes_of(shape):
    lane = lax.broadcasted_iota(jnp.int32, shape, len(shape) - 1)
    return lane < 64, lane % 64


def beside_z(value, z):
    before = jnp.where(z == 0, 0.0, pltpu.roll(value, 1, 1))
    after = jnp.where(z == 63, 0.0, pltpu.roll(value, 127, 1))
    return before + after


def plane_sweep_kernel(state_ref, start_ref, before_ref, after_ref, keep_ref, spread_ref, out_ref):
    value = state_ref[...]
    low, z = lanes_of(value.shape)
    row = lax.broadcasted_iota(jnp.int32, value.shape, 0)
    swapped = pltpu.roll(value, 64, 1)
    earlier = jnp.where(row == 0, 0.0, pltpu.roll(swapped, 1, 0))
    later = jnp.where(row == PLANE - 1, 0.0, pltpu.roll(swapped, PLANE - 1, 0))
    total = before_ref[...] + after_ref[...] + swapped + jnp.where(low, earlier, later) + beside_z(value, z)
    out_ref[...] = keep_ref[...] * start_ref[...] + spread_ref[...] * total


def plane_sweep(state, start, before, after, keep, spread):
    return pl.pallas_call(
        plane_sweep_kernel,
        out_shape=jax.ShapeDtypeStruct(state.shape, jnp.float32),
        compiler_params=params(),
    )(state, start, before, after, keep, spread)


def sweep_rows(source, start, keep, spread, target, first, last, low_end, high_end):
    shape = (SLABS, 128)
    low, z = lanes_of(shape)
    x = lax.broadcasted_iota(jnp.int32, shape, 0)
    zero = jnp.zeros(shape, jnp.float32)

    def swapped(q):
        return pltpu.roll(source[q], 64, 1) if low_end <= q < high_end else zero

    earlier, here = swapped(first - 1), swapped(first)
    for q in range(first, last):
        later = swapped(q + 1)
        value = source[q]
        total = here + jnp.where(low, earlier, later) + beside_z(value, z)
        total = total + jnp.where(x == 0, 0.0, pltpu.roll(value, 1, 0))
        total = total + jnp.where(x == SLABS - 1, 0.0, pltpu.roll(value, SLABS - 1, 0))
        target[q] = keep[q] * start[q] + spread[q] * total
        earlier, here = here, later


def coarse_step(fields, keep, spread, at, low_end, high_end):
    start, middle, result = fields.at[at], fields.at[2], fields.at[1 - at]
    sweep_rows(start, start, keep, spread, middle, low_end, high_end, low_end, high_end)
    sweep_rows(middle, start, keep, spread, result, low_end + 1, high_end - 1, low_end, high_end)
    return 1 - at


def first_links_kernel(c4_ref, c3_ref, c2_ref, c1_ref, keep_ref, spread_ref, out_ref, fields):
    rows = c4_ref.shape[0]
    fields[0] = c4_ref[...]
    at, low_end, high_end = 0, 0, rows
    for added in (c3_ref, c2_ref, c1_ref, None):
        at = coarse_step(fields, keep_ref, spread_ref, at, low_end, high_end)
        low_end, high_end = low_end + 1, high_end - 1
        if added is not None:
            for q in range(low_end, high_end):
                fields[at, q] = fields[at, q] + added[q - low_end]
    out_ref[...] = fields[at, low_end:high_end]


def power_kernel(links, window_ref, base_ref, keep_ref, spread_ref, out_ref, fields):
    rows = window_ref.shape[0]
    fields[0] = window_ref[...]
    at = 0
    for link in range(links):
        at = coarse_step(fields, keep_ref, spread_ref, at, link, rows - link)
    out_ref[...] = base_ref[...] + fields[at, links : rows - links]


def chain_call(kernel, rows, *operands):
    return pl.pallas_call(
        kernel,
        out_shape=jax.ShapeDtypeStruct((BLOCK, SLABS, 128), jnp.float32),
        scratch_shapes=[pltpu.VMEM((3, rows, SLABS, 128), jnp.float32)],
        compiler_params=params(),
    )(*operands)


def facing(distance, late):
    pairs = []
    for i in range(SLABS - distance):
        if (i // distance) % 2 == late:
            pairs += [(i, i + distance), (i + distance, i)]
    return pairs


def from_later(value, links, pairs):
    both = [((n + links) * SLABS + i, n * SLABS + j) for n in range(SLICES - links) for i, j in pairs]
    return lax.ppermute(value, ("tm", "space"), both)


def beside_later(value, links, distance, slab):
    one = from_later(value, links, facing(distance, 0))
    other = from_later(value, links, facing(distance, 1))
    upper = (slab // distance) % 2 == 1
    return jnp.where(upper, one, other), jnp.where(upper, other, one)


def windows(plane, reach):
    blocks = plane.reshape(SLABS, BLOCK, 128)
    padded = jnp.pad(blocks, ((reach, reach), (0, 0), (0, 0)))
    return jnp.concatenate([padded[i : i + SLABS] for i in range(2 * reach + 1)], axis=1)


def to_rows(plane, reach):
    arrived = lax.all_to_all(windows(plane, reach), "space", 0, 0)
    return jnp.transpose(arrived, (1, 0, 2))


def inside_planes(padded):
    center = padded[1:-1]
    beside_all = padded[2:] + padded[:-2]
    planes = jnp.pad(center, ((0, 0), (1, 1), (1, 1)))
    beside_all = beside_all + planes[:, 2:, 1:-1] + planes[:, :-2, 1:-1]
    beside_all = beside_all + planes[:, 1:-1, 2:] + planes[:, 1:-1, :-2]
    return beside_all


def per_device(end_state, cond, receivers, residuals):
    start_field = end_state[0]
    row_count, width_y, width_z = start_field.shape
    plane_size = width_y * width_z
    slab = lax.axis_index("space")
    slice_index = lax.axis_index("tm")
    odd = slab % 2 == 1
    is_final = slice_index == SLICES - 1

    def trade(first, last):
        across = lax.ppermute(jnp.where(odd, last, first), "space", facing(1, 1))
        along = lax.ppermute(jnp.where(odd, first, last), "space", facing(1, 0))
        return jnp.where(odd, along, across), jnp.where(odd, across, along)

    local_row = receivers[0] // plane_size - slab * row_count
    inside = (local_row >= 0) & (local_row < row_count)
    target = jnp.where(inside, local_row * plane_size + receivers[0] % plane_size, row_count * plane_size)
    flat_source = jnp.zeros((row_count * plane_size,), jnp.float32).at[target].add(residuals[0], mode="drop")
    source = flat_source.reshape(row_count, width_y, width_z)

    coarse_cond = restrict(cond) / FINE_STEPS
    plane_spread = 1.0 / (coarse_cond + 1.5)
    plane_keep = coarse_cond * plane_spread
    plane_spread = 0.25 * plane_spread
    row_cond = to_rows(coarse_cond, 2)
    place = (slab - 2) * BLOCK + lax.broadcasted_iota(jnp.int32, row_cond.shape, 0)
    within = (place >= 0) & (place < PLANE)
    row_spread = jnp.where(within, 1.0 / (row_cond + 1.5), 0.0)
    row_keep = row_cond * row_spread
    row_spread = 0.25 * row_spread

    diagonal = cond + 6.0
    field_now = start_field
    coarse_start = restrict(start_field)
    coarse_now = coarse_start
    sweep = 0
    for step_index in range(FINE_STEPS):
        rhs_term = cond * field_now + source
        for sweep_index in range(SWEEPS):
            first, last = field_now[0], field_now[1]
            if sweep in (1, 2):
                first = jnp.concatenate([first, coarse_now])
                last = jnp.concatenate([last, coarse_now])
            before, after = trade(first, last)
            padded = jnp.concatenate([before[None, :width_y], field_now, after[None, :width_y]])
            field_now = (rhs_term + inside_planes(padded)) / diagonal
            if sweep in (1, 2):
                coarse_now = plane_sweep(
                    coarse_now, coarse_start, before[width_y:], after[width_y:], plane_keep, plane_spread
                )
            sweep += 1
    direct = coarse_now

    term = restrict(field_now) - jnp.where(is_final, 0.0, direct)
    rows = to_rows(term, 1)
    later = [(i, i) for i in range(SLABS)]
    links = [from_later(rows[4 - k : 8 + k], k, later) for k in (4, 3, 2, 1)]
    inner = slice(BLOCK, 4 * BLOCK)
    total = chain_call(first_links_kernel, 12, *links, row_keep[inner], row_spread[inner])

    centre = from_later(total, 4, later)
    before, after = beside_later(total, 4, 1, slab)
    window = jnp.concatenate([before, centre, after])
    total = chain_call(
        lambda *refs: power_kernel(4, *refs), 12, window, total, row_keep[inner], row_spread[inner]
    )

    centre = from_later(total, 8, later)
    before, after = beside_later(total, 8, 1, slab)
    before_two, after_two = beside_later(total, 8, 2, slab)
    window = jnp.concatenate([before_two, before, centre, after, after_two])
    total = chain_call(lambda *refs: power_kernel(8, *refs), 20, window, total, row_keep, row_spread)

    back = lax.all_to_all(jnp.transpose(total, (1, 0, 2)), "space", 0, 0)
    propagated = jnp.where(is_final, direct, back.reshape(PLANE, 128))
    return prolong_add(propagated - direct, field_now)[None]


def solution(mesh):
    in_specs = (P("tm", "space", None, None), P("space", None, None), P("tm", None), P("tm", None))
    out_specs = P("tm", "space", None, None)
    return jax.shard_map(
        per_device, mesh=mesh, in_specs=in_specs, out_specs=out_specs, check_vma=False
    )
```

```python
import jax
import jax.numpy as jnp
from jax import lax
from jax.experimental import pallas as pl
from jax.experimental.pallas import tpu as pltpu
from jax.sharding import PartitionSpec as P

FINE_STEPS = 2
SWEEPS = 2
SLABS = 32
SLICES = 16
PLANE = 128
BLOCK = 4
EXACT = lax.Precision.HIGHEST


def params():
    return pltpu.CompilerParams(vmem_limit_bytes=40 * 1024 * 1024)


def halving(half):
    row = lax.broadcasted_iota(jnp.int32, (128, 128), 0)
    lane = lax.broadcasted_iota(jnp.int32, (128, 128), 1)
    return jnp.where(lane == row // 2 + 64 * half, 0.125, 0.0).astype(jnp.float32)


def restrict_kernel(field_ref, out_ref):
    total = jnp.zeros((PLANE, 128), jnp.float32)
    for half in range(2):
        rows = None
        for plane in range(2):
            for r in range(2):
                part = field_ref[plane, pl.ds(2 * half + r, PLANE, stride=4), :]
                rows = part if rows is None else rows + part
        total = total + jnp.dot(rows, halving(half), precision=EXACT, preferred_element_type=jnp.float32)
    out_ref[...] = total


def restrict(field):
    return pl.pallas_call(
        restrict_kernel,
        out_shape=jax.ShapeDtypeStruct((PLANE, 128), jnp.float32),
        compiler_params=params(),
    )(field)


def prolong_add_kernel(delta_ref, field_ref, out_ref):
    row = lax.broadcasted_iota(jnp.int32, (128, 128), 0)
    lane = lax.broadcasted_iota(jnp.int32, (128, 128), 1)
    delta = delta_ref[...]
    for half in range(2):
        spread = jnp.where(row == lane // 2 + 64 * half, 1.0, 0.0).astype(jnp.float32)
        wide = jnp.dot(delta, spread, precision=EXACT, preferred_element_type=jnp.float32)
        for plane in range(2):
            for r in range(2):
                rows = pl.ds(2 * half + r, PLANE, stride=4)
                out_ref[plane, rows, :] = field_ref[plane, rows, :] + wide


def prolong_add(delta, field):
    return pl.pallas_call(
        prolong_add_kernel,
        out_shape=jax.ShapeDtypeStruct(field.shape, jnp.float32),
        compiler_params=params(),
    )(delta, field)


def lanes_of(shape):
    lane = lax.broadcasted_iota(jnp.int32, shape, len(shape) - 1)
    return lane < 64, lane % 64


def beside_z(value, z):
    before = jnp.where(z == 0, 0.0, pltpu.roll(value, 1, 1))
    after = jnp.where(z == 63, 0.0, pltpu.roll(value, 127, 1))
    return before + after


def plane_sweep_kernel(state_ref, start_ref, before_ref, after_ref, keep_ref, spread_ref, out_ref):
    value = state_ref[...]
    low, z = lanes_of(value.shape)
    row = lax.broadcasted_iota(jnp.int32, value.shape, 0)
    swapped = pltpu.roll(value, 64, 1)
    earlier = jnp.where(row == 0, 0.0, pltpu.roll(swapped, 1, 0))
    later = jnp.where(row == PLANE - 1, 0.0, pltpu.roll(swapped, PLANE - 1, 0))
    total = before_ref[...] + after_ref[...] + swapped + jnp.where(low, earlier, later) + beside_z(value, z)
    out_ref[...] = keep_ref[...] * start_ref[...] + spread_ref[...] * total


def plane_sweep(state, start, before, after, keep, spread):
    return pl.pallas_call(
        plane_sweep_kernel,
        out_shape=jax.ShapeDtypeStruct(state.shape, jnp.float32),
        compiler_params=params(),
    )(state, start, before, after, keep, spread)


def sweep_rows(source, start, keep, spread, target, first, last, low_end, high_end):
    shape = (SLABS, 128)
    low, z = lanes_of(shape)
    x = lax.broadcasted_iota(jnp.int32, shape, 0)
    zero = jnp.zeros(shape, jnp.float32)

    def swapped(q):
        return pltpu.roll(source[q], 64, 1) if low_end <= q < high_end else zero

    earlier, here = swapped(first - 1), swapped(first)
    for q in range(first, last):
        later = swapped(q + 1)
        value = source[q]
        total = here + jnp.where(low, earlier, later) + beside_z(value, z)
        total = total + jnp.where(x == 0, 0.0, pltpu.roll(value, 1, 0))
        total = total + jnp.where(x == SLABS - 1, 0.0, pltpu.roll(value, SLABS - 1, 0))
        target[q] = keep[q] * start[q] + spread[q] * total
        earlier, here = here, later


def coarse_step(fields, keep, spread, at, low_end, high_end):
    start, middle, result = fields.at[at], fields.at[2], fields.at[1 - at]
    sweep_rows(start, start, keep, spread, middle, low_end, high_end, low_end, high_end)
    sweep_rows(middle, start, keep, spread, result, low_end + 1, high_end - 1, low_end, high_end)
    return 1 - at


def first_links_kernel(c4_ref, c3_ref, c2_ref, c1_ref, keep_ref, spread_ref, out_ref, fields):
    rows = c4_ref.shape[0]
    fields[0] = c4_ref[...]
    at, low_end, high_end = 0, 0, rows
    for added in (c3_ref, c2_ref, c1_ref, None):
        at = coarse_step(fields, keep_ref, spread_ref, at, low_end, high_end)
        low_end, high_end = low_end + 1, high_end - 1
        if added is not None:
            for q in range(low_end, high_end):
                fields[at, q] = fields[at, q] + added[q - low_end]
    out_ref[...] = fields[at, low_end:high_end]


def power_kernel(links, window_ref, base_ref, keep_ref, spread_ref, out_ref, fields):
    rows = window_ref.shape[0]
    fields[0] = window_ref[...]
    at = 0
    for link in range(links):
        at = coarse_step(fields, keep_ref, spread_ref, at, link, rows - link)
    out_ref[...] = base_ref[...] + fields[at, links : rows - links]


def chain_call(kernel, rows, *operands):
    return pl.pallas_call(
        kernel,
        out_shape=jax.ShapeDtypeStruct((BLOCK, SLABS, 128), jnp.float32),
        scratch_shapes=[pltpu.VMEM((3, rows, SLABS, 128), jnp.float32)],
        compiler_params=params(),
    )(*operands)


def facing(distance, late):
    pairs = []
    for i in range(SLABS - distance):
        if (i // distance) % 2 == late:
            pairs += [(i, i + distance), (i + distance, i)]
    return pairs


def from_later(value, links, pairs):
    both = [((n + links) * SLABS + i, n * SLABS + j) for n in range(SLICES - links) for i, j in pairs]
    return lax.ppermute(value, ("tm", "space"), both)


def beside_later(value, links, distance, slab):
    one = from_later(value, links, facing(distance, 0))
    other = from_later(value, links, facing(distance, 1))
    upper = (slab // distance) % 2 == 1
    return jnp.where(upper, one, other), jnp.where(upper, other, one)


def windows(plane, reach):
    blocks = plane.reshape(SLABS, BLOCK, 128)
    padded = jnp.pad(blocks, ((reach, reach), (0, 0), (0, 0)))
    return jnp.concatenate([padded[i : i + SLABS] for i in range(2 * reach + 1)], axis=1)


def to_rows(plane, reach):
    arrived = lax.all_to_all(windows(plane, reach), "space", 0, 0)
    return jnp.transpose(arrived, (1, 0, 2))


def inside_planes(padded):
    center = padded[1:-1]
    beside_all = padded[2:] + padded[:-2]
    planes = jnp.pad(center, ((0, 0), (1, 1), (1, 1)))
    beside_all = beside_all + planes[:, 2:, 1:-1] + planes[:, :-2, 1:-1]
    beside_all = beside_all + planes[:, 1:-1, 2:] + planes[:, 1:-1, :-2]
    return beside_all


def per_device(end_state, cond, receivers, residuals):
    start_field = end_state[0]
    row_count, width_y, width_z = start_field.shape
    plane_size = width_y * width_z
    slab = lax.axis_index("space")
    slice_index = lax.axis_index("tm")
    odd = slab % 2 == 1
    is_final = slice_index == SLICES - 1

    def trade(first, last):
        across = lax.ppermute(jnp.where(odd, last, first), "space", facing(1, 1))
        along = lax.ppermute(jnp.where(odd, first, last), "space", facing(1, 0))
        return jnp.where(odd, along, across), jnp.where(odd, across, along)

    local_row = receivers[0] // plane_size - slab * row_count
    inside = (local_row >= 0) & (local_row < row_count)
    target = jnp.where(inside, local_row * plane_size + receivers[0] % plane_size, row_count * plane_size)
    flat_source = jnp.zeros((row_count * plane_size,), jnp.float32).at[target].add(residuals[0], mode="drop")
    source = flat_source.reshape(row_count, width_y, width_z)

    coarse_cond = restrict(cond) / FINE_STEPS
    plane_spread = 1.0 / (coarse_cond + 1.5)
    plane_keep = coarse_cond * plane_spread
    plane_spread = 0.25 * plane_spread
    diagonal = cond + 6.0
    field_now = start_field
    coarse_start = restrict(start_field)
    coarse_now = coarse_start
    sweep = 0
    for step_index in range(FINE_STEPS):
        rhs_term = cond * field_now + source
        for sweep_index in range(SWEEPS):
            first, last = field_now[0], field_now[1]
            if sweep in (1, 2):
                first = jnp.concatenate([first, coarse_now])
                last = jnp.concatenate([last, coarse_now])
            before, after = trade(first, last)
            padded = jnp.concatenate([before[None, :width_y], field_now, after[None, :width_y]])
            field_now = (rhs_term + inside_planes(padded)) / diagonal
            if sweep in (1, 2):
                coarse_now = plane_sweep(
                    coarse_now, coarse_start, before[width_y:], after[width_y:], plane_keep, plane_spread
                )
            sweep += 1
            if sweep == 1:
                coarse_cond, field_now = lax.optimization_barrier((coarse_cond, field_now))
                row_cond = to_rows(coarse_cond, 2)
            if sweep == 3:
                row_cond, field_now = lax.optimization_barrier((row_cond, field_now))
    direct = coarse_now

    place = (slab - 2) * BLOCK + lax.broadcasted_iota(jnp.int32, row_cond.shape, 0)
    within = (place >= 0) & (place < PLANE)
    row_spread = jnp.where(within, 1.0 / (row_cond + 1.5), 0.0)
    row_keep = row_cond * row_spread
    row_spread = 0.25 * row_spread

    term = restrict(field_now) - jnp.where(is_final, 0.0, direct)
    rows = to_rows(term, 1)
    later = [(i, i) for i in range(SLABS)]
    links = [from_later(rows[4 - k : 8 + k], k, later) for k in (4, 3, 2, 1)]
    inner = slice(BLOCK, 4 * BLOCK)
    total = chain_call(first_links_kernel, 12, *links, row_keep[inner], row_spread[inner])

    centre = from_later(total, 4, later)
    before, after = beside_later(total, 4, 1, slab)
    window = jnp.concatenate([before, centre, after])
    total = chain_call(
        lambda *refs: power_kernel(4, *refs), 12, window, total, row_keep[inner], row_spread[inner]
    )

    centre = from_later(total, 8, later)
    before, after = beside_later(total, 8, 1, slab)
    before_two, after_two = beside_later(total, 8, 2, slab)
    window = jnp.concatenate([before_two, before, centre, after, after_two])
    total = chain_call(lambda *refs: power_kernel(8, *refs), 20, window, total, row_keep, row_spread)

    back = lax.all_to_all(jnp.transpose(total, (1, 0, 2)), "space", 0, 0)
    propagated = jnp.where(is_final, direct, back.reshape(PLANE, 128))
    return prolong_add(propagated - direct, field_now)[None]


def solution(mesh):
    in_specs = (P("tm", "space", None, None), P("space", None, None), P("tm", None), P("tm", None))
    out_specs = P("tm", "space", None, None)
    return jax.shard_map(
        per_device, mesh=mesh, in_specs=in_specs, out_specs=out_specs, check_vma=False
    )
```

```python
import jax
import jax.numpy as jnp
from jax import lax
from jax.experimental import pallas as pl
from jax.experimental.pallas import tpu as pltpu
from jax.sharding import PartitionSpec as P

FINE_STEPS = 2
SWEEPS = 2
SLABS = 32
SLICES = 16
PLANE = 128
BLOCK = 4
EXACT = lax.Precision.HIGHEST


def params():
    return pltpu.CompilerParams(vmem_limit_bytes=40 * 1024 * 1024)


def halving(half):
    row = lax.broadcasted_iota(jnp.int32, (128, 128), 0)
    lane = lax.broadcasted_iota(jnp.int32, (128, 128), 1)
    return jnp.where(lane == row // 2 + 64 * half, 0.125, 0.0).astype(jnp.float32)


def restrict_kernel(field_ref, out_ref):
    total = jnp.zeros((PLANE, 128), jnp.float32)
    for half in range(2):
        rows = None
        for plane in range(2):
            for r in range(2):
                part = field_ref[plane, pl.ds(2 * half + r, PLANE, stride=4), :]
                rows = part if rows is None else rows + part
        total = total + jnp.dot(rows, halving(half), precision=EXACT, preferred_element_type=jnp.float32)
    out_ref[...] = total


def restrict(field):
    return pl.pallas_call(
        restrict_kernel,
        out_shape=jax.ShapeDtypeStruct((PLANE, 128), jnp.float32),
        compiler_params=params(),
    )(field)


def prolong_add_kernel(delta_ref, field_ref, out_ref):
    row = lax.broadcasted_iota(jnp.int32, (128, 128), 0)
    lane = lax.broadcasted_iota(jnp.int32, (128, 128), 1)
    delta = delta_ref[...]
    for half in range(2):
        spread = jnp.where(row == lane // 2 + 64 * half, 1.0, 0.0).astype(jnp.float32)
        wide = jnp.dot(delta, spread, precision=EXACT, preferred_element_type=jnp.float32)
        for plane in range(2):
            for r in range(2):
                rows = pl.ds(2 * half + r, PLANE, stride=4)
                out_ref[plane, rows, :] = field_ref[plane, rows, :] + wide


def prolong_add(delta, field):
    return pl.pallas_call(
        prolong_add_kernel,
        out_shape=jax.ShapeDtypeStruct(field.shape, jnp.float32),
        compiler_params=params(),
    )(delta, field)


def lanes_of(shape):
    lane = lax.broadcasted_iota(jnp.int32, shape, len(shape) - 1)
    return lane < 64, lane % 64


def beside_z(value, z):
    before = jnp.where(z == 0, 0.0, pltpu.roll(value, 1, 1))
    after = jnp.where(z == 63, 0.0, pltpu.roll(value, 127, 1))
    return before + after


def plane_sweep_kernel(state_ref, start_ref, before_ref, after_ref, keep_ref, spread_ref, out_ref):
    value = state_ref[...]
    low, z = lanes_of(value.shape)
    row = lax.broadcasted_iota(jnp.int32, value.shape, 0)
    swapped = pltpu.roll(value, 64, 1)
    earlier = jnp.where(row == 0, 0.0, pltpu.roll(swapped, 1, 0))
    later = jnp.where(row == PLANE - 1, 0.0, pltpu.roll(swapped, PLANE - 1, 0))
    total = before_ref[...] + after_ref[...] + swapped + jnp.where(low, earlier, later) + beside_z(value, z)
    out_ref[...] = keep_ref[...] * start_ref[...] + spread_ref[...] * total


def plane_sweep(state, start, before, after, keep, spread):
    return pl.pallas_call(
        plane_sweep_kernel,
        out_shape=jax.ShapeDtypeStruct(state.shape, jnp.float32),
        compiler_params=params(),
    )(state, start, before, after, keep, spread)


def sweep_rows(source, start, keep, spread, target, first, last, low_end, high_end):
    shape = (SLABS, 128)
    low, z = lanes_of(shape)
    x = lax.broadcasted_iota(jnp.int32, shape, 0)
    zero = jnp.zeros(shape, jnp.float32)

    def swapped(q):
        return pltpu.roll(source[q], 64, 1) if low_end <= q < high_end else zero

    earlier, here = swapped(first - 1), swapped(first)
    for q in range(first, last):
        later = swapped(q + 1)
        value = source[q]
        total = here + jnp.where(low, earlier, later) + beside_z(value, z)
        total = total + jnp.where(x == 0, 0.0, pltpu.roll(value, 1, 0))
        total = total + jnp.where(x == SLABS - 1, 0.0, pltpu.roll(value, SLABS - 1, 0))
        target[q] = keep[q] * start[q] + spread[q] * total
        earlier, here = here, later


def coarse_step(fields, keep, spread, at, low_end, high_end):
    start, middle, result = fields.at[at], fields.at[2], fields.at[1 - at]
    sweep_rows(start, start, keep, spread, middle, low_end, high_end, low_end, high_end)
    sweep_rows(middle, start, keep, spread, result, low_end + 1, high_end - 1, low_end, high_end)
    return 1 - at


def first_links_kernel(c4_ref, c3_ref, c2_ref, c1_ref, keep_ref, spread_ref, out_ref, fields):
    rows = c4_ref.shape[0]
    fields[0] = c4_ref[...]
    at, low_end, high_end = 0, 0, rows
    for added in (c3_ref, c2_ref, c1_ref, None):
        at = coarse_step(fields, keep_ref, spread_ref, at, low_end, high_end)
        low_end, high_end = low_end + 1, high_end - 1
        if added is not None:
            for q in range(low_end, high_end):
                fields[at, q] = fields[at, q] + added[q - low_end]
    out_ref[...] = fields[at, low_end:high_end]


def power_kernel(links, window_ref, base_ref, keep_ref, spread_ref, out_ref, fields):
    rows = window_ref.shape[0]
    fields[0] = window_ref[...]
    at = 0
    for link in range(links):
        at = coarse_step(fields, keep_ref, spread_ref, at, link, rows - link)
    out_ref[...] = base_ref[...] + fields[at, links : rows - links]


def chain_call(kernel, rows, *operands):
    return pl.pallas_call(
        kernel,
        out_shape=jax.ShapeDtypeStruct((BLOCK, SLABS, 128), jnp.float32),
        scratch_shapes=[pltpu.VMEM((3, rows, SLABS, 128), jnp.float32)],
        compiler_params=params(),
    )(*operands)


def facing(distance, late):
    pairs = []
    for i in range(SLABS - distance):
        if (i // distance) % 2 == late:
            pairs += [(i, i + distance), (i + distance, i)]
    return pairs


def from_later(value, links, pairs):
    both = [((n + links) * SLABS + i, n * SLABS + j) for n in range(SLICES - links) for i, j in pairs]
    return lax.ppermute(value, ("tm", "space"), both)


def beside_later(value, links, distance, slab):
    one = from_later(value, links, facing(distance, 0))
    other = from_later(value, links, facing(distance, 1))
    upper = (slab // distance) % 2 == 1
    return jnp.where(upper, one, other), jnp.where(upper, other, one)


def windows(plane, reach):
    blocks = plane.reshape(SLABS, BLOCK, 128)
    padded = jnp.pad(blocks, ((reach, reach), (0, 0), (0, 0)))
    return jnp.concatenate([padded[i : i + SLABS] for i in range(2 * reach + 1)], axis=1)


def to_rows(parts):
    arrived = lax.all_to_all(parts, "space", 0, 0)
    return jnp.transpose(arrived, (1, 0, 2))


def inside_planes(padded):
    center = padded[1:-1]
    beside_all = padded[2:] + padded[:-2]
    planes = jnp.pad(center, ((0, 0), (1, 1), (1, 1)))
    beside_all = beside_all + planes[:, 2:, 1:-1] + planes[:, :-2, 1:-1]
    beside_all = beside_all + planes[:, 1:-1, 2:] + planes[:, 1:-1, :-2]
    return beside_all


def per_device(end_state, cond, receivers, residuals):
    start_field = end_state[0]
    row_count, width_y, width_z = start_field.shape
    plane_size = width_y * width_z
    slab = lax.axis_index("space")
    slice_index = lax.axis_index("tm")
    odd = slab % 2 == 1
    is_final = slice_index == SLICES - 1

    def trade(to_before, to_after):
        across = lax.ppermute(jnp.where(odd, to_after, to_before), "space", facing(1, 1))
        along = lax.ppermute(jnp.where(odd, to_before, to_after), "space", facing(1, 0))
        return jnp.where(odd, along, across), jnp.where(odd, across, along)

    ring = slice_index % 4
    quarter = width_y // 4
    share = lax.dynamic_slice_in_dim(cond, ring * quarter, quarter, axis=1)
    share = jnp.stack(trade(share[0], share[1]))
    for bit in (1, 2):
        upper = (ring // bit) % 2 == 1
        other = lax.ppermute(share, "tm", [(n, n ^ bit) for n in range(SLICES)])
        share = jnp.concatenate([jnp.where(upper, other, share), jnp.where(upper, share, other)], axis=1)
    wide_cond = jnp.concatenate([share[:1], cond, share[1:]])

    local_row = receivers[0] // plane_size - slab * row_count + 1
    inside = (local_row >= 0) & (local_row < row_count + 2)
    wide_size = (row_count + 2) * plane_size
    target = jnp.where(inside, local_row * plane_size + receivers[0] % plane_size, wide_size)
    flat_source = jnp.zeros((wide_size,), jnp.float32).at[target].add(residuals[0], mode="drop")
    wide_source = flat_source.reshape(row_count + 2, width_y, width_z)
    plane_place = slab * row_count - 1 + jnp.arange(row_count + 2)
    in_grid = ((plane_place >= 0) & (plane_place < SLABS * row_count))[:, None, None]

    coarse_cond = restrict(cond) / FINE_STEPS
    plane_spread = 1.0 / (coarse_cond + 1.5)
    plane_keep = coarse_cond * plane_spread
    plane_spread = 0.25 * plane_spread
    coarse_start = restrict(start_field)

    def two_sweeps(padded):
        wide = padded[1:-1]
        rhs_term = wide_cond * wide + wide_source
        diagonal = wide_cond + 6.0
        wide = jnp.where(in_grid, (rhs_term + inside_planes(padded)) / diagonal, 0.0)
        return (rhs_term[1:-1] + inside_planes(wide)) / diagonal[1:-1]

    before, after = trade(start_field, start_field)
    coarse_now = plane_sweep(
        coarse_start, coarse_start, restrict(before), restrict(after), plane_keep, plane_spread
    )
    field_now = two_sweeps(jnp.concatenate([before, start_field, after]))
    slab_rows = row_count * width_y
    sent = jnp.concatenate([field_now.reshape(slab_rows, width_z), coarse_now])
    before, after = trade(sent, sent)
    direct = plane_sweep(
        coarse_now, coarse_start, before[slab_rows:], after[slab_rows:], plane_keep, plane_spread
    )
    before = before[:slab_rows].reshape(start_field.shape)
    after = after[:slab_rows].reshape(start_field.shape)
    field_now = two_sweeps(jnp.concatenate([before, field_now, after]))

    term = restrict(field_now) - jnp.where(is_final, 0.0, direct)
    second_half = slice_index % 2 == 1
    cond_windows = windows(coarse_cond, 2)
    cond_windows = jnp.where(second_half, cond_windows[:, 10:], cond_windows[:, :10])
    arrived = to_rows(jnp.concatenate([windows(term, 1), cond_windows], axis=1))
    rows, own_cond = arrived[:12], arrived[12:]
    other_cond = lax.ppermute(own_cond, "tm", [(n, n ^ 1) for n in range(SLICES)])
    row_cond = jnp.concatenate(
        [jnp.where(second_half, other_cond, own_cond), jnp.where(second_half, own_cond, other_cond)]
    )
    place = (slab - 2) * BLOCK + lax.broadcasted_iota(jnp.int32, row_cond.shape, 0)
    within = (place >= 0) & (place < PLANE)
    row_spread = jnp.where(within, 1.0 / (row_cond + 1.5), 0.0)
    row_keep = row_cond * row_spread
    row_spread = 0.25 * row_spread

    later = [(i, i) for i in range(SLABS)]
    links = [from_later(rows[4 - k : 8 + k], k, later) for k in (4, 3, 2, 1)]
    inner = slice(BLOCK, 4 * BLOCK)
    total = chain_call(first_links_kernel, 12, *links, row_keep[inner], row_spread[inner])

    centre = from_later(total, 4, later)
    before, after = beside_later(total, 4, 1, slab)
    window = jnp.concatenate([before, centre, after])
    total = chain_call(
        lambda *refs: power_kernel(4, *refs), 12, window, total, row_keep[inner], row_spread[inner]
    )

    centre = from_later(total, 8, later)
    before, after = beside_later(total, 8, 1, slab)
    before_two, after_two = beside_later(total, 8, 2, slab)
    window = jnp.concatenate([before_two, before, centre, after, after_two])
    total = chain_call(lambda *refs: power_kernel(8, *refs), 20, window, total, row_keep, row_spread)

    back = lax.all_to_all(jnp.transpose(total, (1, 0, 2)), "space", 0, 0)
    propagated = jnp.where(is_final, direct, back.reshape(PLANE, 128))
    return prolong_add(propagated - direct, field_now)[None]


def solution(mesh):
    in_specs = (P("tm", "space", None, None), P("space", None, None), P("tm", None), P("tm", None))
    out_specs = P("tm", "space", None, None)
    return jax.shard_map(
        per_device, mesh=mesh, in_specs=in_specs, out_specs=out_specs, check_vma=False
    )
```

```python
import jax
import jax.numpy as jnp
from jax import lax
from jax.experimental import pallas as pl
from jax.experimental.pallas import tpu as pltpu
from jax.sharding import PartitionSpec as P

FINE_STEPS = 2
SWEEPS = 2
SLABS = 32
SLICES = 16
PLANE = 128
BLOCK = 4
EXACT = lax.Precision.HIGHEST


def params():
    return pltpu.CompilerParams(vmem_limit_bytes=40 * 1024 * 1024)


def halving(half):
    row = lax.broadcasted_iota(jnp.int32, (128, 128), 0)
    lane = lax.broadcasted_iota(jnp.int32, (128, 128), 1)
    return jnp.where(lane == row // 2 + 64 * half, 0.125, 0.0).astype(jnp.float32)


def restrict_kernel(field_ref, out_ref):
    total = jnp.zeros((PLANE, 128), jnp.float32)
    for half in range(2):
        rows = None
        for plane in range(2):
            for r in range(2):
                part = field_ref[plane, pl.ds(2 * half + r, PLANE, stride=4), :]
                rows = part if rows is None else rows + part
        total = total + jnp.dot(rows, halving(half), precision=EXACT, preferred_element_type=jnp.float32)
    out_ref[...] = total


def restrict(field):
    return pl.pallas_call(
        restrict_kernel,
        out_shape=jax.ShapeDtypeStruct((PLANE, 128), jnp.float32),
        compiler_params=params(),
    )(field)


def prolong_add_kernel(delta_ref, field_ref, out_ref):
    row = lax.broadcasted_iota(jnp.int32, (128, 128), 0)
    lane = lax.broadcasted_iota(jnp.int32, (128, 128), 1)
    delta = delta_ref[...]
    for half in range(2):
        spread = jnp.where(row == lane // 2 + 64 * half, 1.0, 0.0).astype(jnp.float32)
        wide = jnp.dot(delta, spread, precision=EXACT, preferred_element_type=jnp.float32)
        for plane in range(2):
            for r in range(2):
                rows = pl.ds(2 * half + r, PLANE, stride=4)
                out_ref[plane, rows, :] = field_ref[plane, rows, :] + wide


def prolong_add(delta, field):
    return pl.pallas_call(
        prolong_add_kernel,
        out_shape=jax.ShapeDtypeStruct(field.shape, jnp.float32),
        compiler_params=params(),
    )(delta, field)


def lanes_of(shape):
    lane = lax.broadcasted_iota(jnp.int32, shape, len(shape) - 1)
    return lane < 64, lane % 64


def beside_z(value, z):
    before = jnp.where(z == 0, 0.0, pltpu.roll(value, 1, 1))
    after = jnp.where(z == 63, 0.0, pltpu.roll(value, 127, 1))
    return before + after


def plane_sweep_kernel(state_ref, start_ref, before_ref, after_ref, keep_ref, spread_ref, out_ref):
    value = state_ref[...]
    low, z = lanes_of(value.shape)
    row = lax.broadcasted_iota(jnp.int32, value.shape, 0)
    swapped = pltpu.roll(value, 64, 1)
    earlier = jnp.where(row == 0, 0.0, pltpu.roll(swapped, 1, 0))
    later = jnp.where(row == PLANE - 1, 0.0, pltpu.roll(swapped, PLANE - 1, 0))
    total = before_ref[...] + after_ref[...] + swapped + jnp.where(low, earlier, later) + beside_z(value, z)
    out_ref[...] = keep_ref[...] * start_ref[...] + spread_ref[...] * total


def plane_sweep(state, start, before, after, keep, spread):
    return pl.pallas_call(
        plane_sweep_kernel,
        out_shape=jax.ShapeDtypeStruct(state.shape, jnp.float32),
        compiler_params=params(),
    )(state, start, before, after, keep, spread)


def sweep_rows(source, start, keep, spread, target, first, last, low_end, high_end):
    shape = (SLABS, 128)
    low, z = lanes_of(shape)
    x = lax.broadcasted_iota(jnp.int32, shape, 0)
    zero = jnp.zeros(shape, jnp.float32)

    def swapped(q):
        return pltpu.roll(source[q], 64, 1) if low_end <= q < high_end else zero

    earlier, here = swapped(first - 1), swapped(first)
    for q in range(first, last):
        later = swapped(q + 1)
        value = source[q]
        total = here + jnp.where(low, earlier, later) + beside_z(value, z)
        total = total + jnp.where(x == 0, 0.0, pltpu.roll(value, 1, 0))
        total = total + jnp.where(x == SLABS - 1, 0.0, pltpu.roll(value, SLABS - 1, 0))
        target[q] = keep[q] * start[q] + spread[q] * total
        earlier, here = here, later


def coarse_step(fields, keep, spread, at, low_end, high_end):
    start, middle, result = fields.at[at], fields.at[2], fields.at[1 - at]
    sweep_rows(start, start, keep, spread, middle, low_end, high_end, low_end, high_end)
    sweep_rows(middle, start, keep, spread, result, low_end + 1, high_end - 1, low_end, high_end)
    return 1 - at


def first_links_kernel(c4_ref, c3_ref, c2_ref, c1_ref, keep_ref, spread_ref, out_ref, fields):
    rows = c4_ref.shape[0]
    fields[0] = c4_ref[...]
    at, low_end, high_end = 0, 0, rows
    for added in (c3_ref, c2_ref, c1_ref, None):
        at = coarse_step(fields, keep_ref, spread_ref, at, low_end, high_end)
        low_end, high_end = low_end + 1, high_end - 1
        if added is not None:
            for q in range(low_end, high_end):
                fields[at, q] = fields[at, q] + added[q - low_end]
    out_ref[...] = fields[at, low_end:high_end]


def power_kernel(links, window_ref, base_ref, keep_ref, spread_ref, out_ref, fields):
    rows = window_ref.shape[0]
    fields[0] = window_ref[...]
    at = 0
    for link in range(links):
        at = coarse_step(fields, keep_ref, spread_ref, at, link, rows - link)
    out_ref[...] = base_ref[...] + fields[at, links : rows - links]


def chain_call(kernel, rows, *operands):
    return pl.pallas_call(
        kernel,
        out_shape=jax.ShapeDtypeStruct((BLOCK, SLABS, 128), jnp.float32),
        scratch_shapes=[pltpu.VMEM((3, rows, SLABS, 128), jnp.float32)],
        compiler_params=params(),
    )(*operands)


def facing(distance, late):
    pairs = []
    for i in range(SLABS - distance):
        if (i // distance) % 2 == late:
            pairs += [(i, i + distance), (i + distance, i)]
    return pairs


def from_later(value, links, pairs):
    both = [((n + links) * SLABS + i, n * SLABS + j) for n in range(SLICES - links) for i, j in pairs]
    return lax.ppermute(value, ("tm", "space"), both)


def beside_later(value, links, distance, slab):
    one = from_later(value, links, facing(distance, 0))
    other = from_later(value, links, facing(distance, 1))
    upper = (slab // distance) % 2 == 1
    return jnp.where(upper, one, other), jnp.where(upper, other, one)


def windows(plane, reach):
    blocks = plane.reshape(SLABS, BLOCK, 128)
    padded = jnp.pad(blocks, ((reach, reach), (0, 0), (0, 0)))
    return jnp.concatenate([padded[i : i + SLABS] for i in range(2 * reach + 1)], axis=1)


def to_rows(parts):
    arrived = lax.all_to_all(parts, "space", 0, 0)
    return jnp.transpose(arrived, (1, 0, 2))


def inside_planes(padded):
    center = padded[1:-1]
    beside_all = padded[2:] + padded[:-2]
    planes = jnp.pad(center, ((0, 0), (1, 1), (1, 1)))
    beside_all = beside_all + planes[:, 2:, 1:-1] + planes[:, :-2, 1:-1]
    beside_all = beside_all + planes[:, 1:-1, 2:] + planes[:, 1:-1, :-2]
    return beside_all


def per_device(end_state, cond, receivers, residuals):
    start_field = end_state[0]
    row_count, width_y, width_z = start_field.shape
    plane_size = width_y * width_z
    slab = lax.axis_index("space")
    slice_index = lax.axis_index("tm")
    odd = slab % 2 == 1
    is_final = slice_index == SLICES - 1

    def trade(to_before, to_after):
        across = lax.ppermute(jnp.where(odd, to_after, to_before), "space", facing(1, 1))
        along = lax.ppermute(jnp.where(odd, to_before, to_after), "space", facing(1, 0))
        return jnp.where(odd, along, across), jnp.where(odd, across, along)

    ring = slice_index % 4
    quarter = width_y // 4
    share = lax.dynamic_slice_in_dim(cond, ring * quarter, quarter, axis=1)
    share = jnp.stack(trade(share[0], share[1]))
    for bit in (1, 2):
        upper = (ring // bit) % 2 == 1
        other = lax.ppermute(share, "tm", [(n, n ^ bit) for n in range(SLICES)])
        share = jnp.concatenate([jnp.where(upper, other, share), jnp.where(upper, share, other)], axis=1)
    wide_cond = jnp.concatenate([share[:1], cond, share[1:]])

    local_row = receivers[0] // plane_size - slab * row_count + 1
    inside = (local_row >= 0) & (local_row < row_count + 2)
    wide_size = (row_count + 2) * plane_size
    target = jnp.where(inside, local_row * plane_size + receivers[0] % plane_size, wide_size)
    flat_source = jnp.zeros((wide_size,), jnp.float32).at[target].add(residuals[0], mode="drop")
    wide_source = flat_source.reshape(row_count + 2, width_y, width_z)
    plane_place = slab * row_count - 1 + jnp.arange(row_count + 2)
    in_grid = ((plane_place >= 0) & (plane_place < SLABS * row_count))[:, None, None]

    coarse_cond = restrict(cond) / FINE_STEPS
    plane_spread = 1.0 / (coarse_cond + 1.5)
    plane_keep = coarse_cond * plane_spread
    plane_spread = 0.25 * plane_spread
    coarse_start = restrict(start_field)

    def two_sweeps(padded):
        wide = padded[1:-1]
        rhs_term = wide_cond * wide + wide_source
        diagonal = wide_cond + 6.0
        wide = jnp.where(in_grid, (rhs_term + inside_planes(padded)) / diagonal, 0.0)
        return (rhs_term[1:-1] + inside_planes(wide)) / diagonal[1:-1]

    before, after = trade(start_field, start_field)

    tall = jnp.pad(coarse_cond, ((2 * BLOCK, 2 * BLOCK), (0, 0)))
    shares = []
    for i in range(2):
        at = (slab - 2 * slice_index - i) % SLABS
        window = lax.dynamic_slice_in_dim(tall, at * BLOCK, 5 * BLOCK, axis=0)
        pairs = [
            (n * SLABS + j, n * SLABS + (j - 2 * n - i) % SLABS) for n in range(SLICES) for j in range(SLABS)
        ]
        shares.append(lax.ppermute(window, ("tm", "space"), pairs))
    gathered = jnp.stack(shares)
    for bit in (1, 2, 4, 8):
        upper = (slice_index // bit) % 2 == 1
        other = lax.ppermute(gathered, "tm", [(n, n ^ bit) for n in range(SLICES)])
        gathered = jnp.concatenate([jnp.where(upper, other, gathered), jnp.where(upper, gathered, other)])
    turned = lax.dynamic_slice_in_dim(
        jnp.concatenate([gathered, gathered]), (SLABS - slab) % SLABS, SLABS, axis=0
    )
    row_cond = jnp.transpose(turned, (1, 0, 2))

    coarse_now = plane_sweep(
        coarse_start, coarse_start, restrict(before), restrict(after), plane_keep, plane_spread
    )
    field_now = two_sweeps(jnp.concatenate([before, start_field, after]))
    slab_rows = row_count * width_y
    sent = jnp.concatenate([field_now.reshape(slab_rows, width_z), coarse_now])
    before, after = trade(sent, sent)
    direct = plane_sweep(
        coarse_now, coarse_start, before[slab_rows:], after[slab_rows:], plane_keep, plane_spread
    )
    before = before[:slab_rows].reshape(start_field.shape)
    after = after[:slab_rows].reshape(start_field.shape)
    field_now = two_sweeps(jnp.concatenate([before, field_now, after]))

    term = restrict(field_now) - jnp.where(is_final, 0.0, direct)
    rows = to_rows(windows(term, 1))
    place = (slab - 2) * BLOCK + lax.broadcasted_iota(jnp.int32, row_cond.shape, 0)
    within = (place >= 0) & (place < PLANE)
    row_spread = jnp.where(within, 1.0 / (row_cond + 1.5), 0.0)
    row_keep = row_cond * row_spread
    row_spread = 0.25 * row_spread

    later = [(i, i) for i in range(SLABS)]
    links = [from_later(rows[4 - k : 8 + k], k, later) for k in (4, 3, 2, 1)]
    inner = slice(BLOCK, 4 * BLOCK)
    total = chain_call(first_links_kernel, 12, *links, row_keep[inner], row_spread[inner])

    centre = from_later(total, 4, later)
    before, after = beside_later(total, 4, 1, slab)
    window = jnp.concatenate([before, centre, after])
    total = chain_call(
        lambda *refs: power_kernel(4, *refs), 12, window, total, row_keep[inner], row_spread[inner]
    )

    centre = from_later(total, 8, later)
    near = from_later(total, 8, facing(1, 1))
    outward = [(j - 2, j) for j in range(2, SLABS, 2)] + [(j + 2, j) for j in range(1, SLABS - 2, 2)]
    far = from_later(total, 8, outward)
    swapped = lax.ppermute(jnp.stack([centre, near]), "space", facing(1, 0))
    window = jnp.where(
        odd,
        jnp.concatenate([swapped[1], swapped[0], centre, near, far]),
        jnp.concatenate([far, near, centre, swapped[0], swapped[1]]),
    )
    total = chain_call(lambda *refs: power_kernel(8, *refs), 20, window, total, row_keep, row_spread)

    back = lax.all_to_all(jnp.transpose(total, (1, 0, 2)), "space", 0, 0)
    propagated = jnp.where(is_final, direct, back.reshape(PLANE, 128))
    return prolong_add(propagated - direct, field_now)[None]


def solution(mesh):
    in_specs = (P("tm", "space", None, None), P("space", None, None), P("tm", None), P("tm", None))
    out_specs = P("tm", "space", None, None)
    return jax.shard_map(
        per_device, mesh=mesh, in_specs=in_specs, out_specs=out_specs, check_vma=False
    )
```

```python
import jax
import jax.numpy as jnp
from jax import lax
from jax.experimental import pallas as pl
from jax.experimental.pallas import tpu as pltpu
from jax.sharding import PartitionSpec as P

FINE_STEPS = 2
SWEEPS = 2
SLABS = 32
SLICES = 16
PLANE = 128
BLOCK = 4
EXACT = lax.Precision.HIGHEST


def params():
    return pltpu.CompilerParams(vmem_limit_bytes=12 * 1024 * 1024)


def halving(half):
    row = lax.broadcasted_iota(jnp.int32, (128, 128), 0)
    lane = lax.broadcasted_iota(jnp.int32, (128, 128), 1)
    return jnp.where(lane == row // 2 + 64 * half, 0.125, 0.0).astype(jnp.float32)


def restrict_kernel(field_ref, out_ref):
    total = jnp.zeros((PLANE, 128), jnp.float32)
    for half in range(2):
        rows = None
        for plane in range(2):
            for r in range(2):
                part = field_ref[plane, pl.ds(2 * half + r, PLANE, stride=4), :]
                rows = part if rows is None else rows + part
        total = total + jnp.dot(rows, halving(half), precision=EXACT, preferred_element_type=jnp.float32)
    out_ref[...] = total


def restrict(field):
    return pl.pallas_call(
        restrict_kernel,
        out_shape=jax.ShapeDtypeStruct((PLANE, 128), jnp.float32),
        compiler_params=params(),
    )(field)


def prolong_add_kernel(delta_ref, field_ref, out_ref):
    row = lax.broadcasted_iota(jnp.int32, (128, 128), 0)
    lane = lax.broadcasted_iota(jnp.int32, (128, 128), 1)
    delta = delta_ref[...]
    for half in range(2):
        spread = jnp.where(row == lane // 2 + 64 * half, 1.0, 0.0).astype(jnp.float32)
        wide = jnp.dot(delta, spread, precision=EXACT, preferred_element_type=jnp.float32)
        for plane in range(2):
            for r in range(2):
                rows = pl.ds(2 * half + r, PLANE, stride=4)
                out_ref[plane, rows, :] = field_ref[plane, rows, :] + wide


def prolong_add(delta, field):
    return pl.pallas_call(
        prolong_add_kernel,
        out_shape=jax.ShapeDtypeStruct(field.shape, jnp.float32),
        compiler_params=params(),
    )(delta, field)


def lanes_of(shape):
    lane = lax.broadcasted_iota(jnp.int32, shape, len(shape) - 1)
    return lane < 64, lane % 64


def beside_z(value, z):
    before = jnp.where(z == 0, 0.0, pltpu.roll(value, 1, 1))
    after = jnp.where(z == 63, 0.0, pltpu.roll(value, 127, 1))
    return before + after


def beside_in_plane(value):
    rows = value.shape[0]
    row = lax.broadcasted_iota(jnp.int32, value.shape, 0)
    lane = lax.broadcasted_iota(jnp.int32, value.shape, 1)
    above = jnp.where(row == 0, 0.0, pltpu.roll(value, 1, 0))
    below = jnp.where(row == rows - 1, 0.0, pltpu.roll(value, rows - 1, 0))
    before = jnp.where(lane == 0, 0.0, pltpu.roll(value, 1, 1))
    after = jnp.where(lane == 127, 0.0, pltpu.roll(value, 127, 1))
    return above + below + before + after


def step_kernel(place_ref, across_ref, along_ref, field_ref, share_ref, cond_ref, source_ref, out_ref):
    odd = place_ref[0] == 1
    planes = [jnp.where(odd, along_ref[p], across_ref[p]) for p in range(2)]
    planes += [field_ref[p] for p in range(2)]
    planes += [jnp.where(odd, across_ref[p], along_ref[p]) for p in range(2)]
    conds = [share_ref[0], cond_ref[0], cond_ref[1], share_ref[1]]
    terms, diagonals, wide = [], [], []
    for i in range(4):
        value = planes[i + 1]
        terms.append(conds[i] * value + source_ref[i])
        diagonals.append(conds[i] + 6.0)
        total = planes[i] + planes[i + 2] + beside_in_plane(value)
        wide.append((terms[i] + total) / diagonals[i])
    wide[0] = jnp.where(place_ref[1] == 1, wide[0], 0.0)
    wide[3] = jnp.where(place_ref[2] == 1, wide[3], 0.0)
    for p in range(2):
        total = wide[p] + wide[p + 2] + beside_in_plane(wide[p + 1])
        out_ref[p] = (terms[p + 1] + total) / diagonals[p + 1]


def fine_step(place, *operands):
    in_vmem = pl.BlockSpec(memory_space=pltpu.VMEM)
    return pl.pallas_call(
        step_kernel,
        out_shape=jax.ShapeDtypeStruct(operands[2].shape, jnp.float32),
        in_specs=[pl.BlockSpec(memory_space=pltpu.SMEM)] + [in_vmem] * len(operands),
        out_specs=in_vmem,
        compiler_params=params(),
    )(place, *operands)


def plane_sweep_kernel(state_ref, start_ref, before_ref, after_ref, keep_ref, spread_ref, out_ref):
    value = state_ref[...]
    low, z = lanes_of(value.shape)
    row = lax.broadcasted_iota(jnp.int32, value.shape, 0)
    swapped = pltpu.roll(value, 64, 1)
    earlier = jnp.where(row == 0, 0.0, pltpu.roll(swapped, 1, 0))
    later = jnp.where(row == PLANE - 1, 0.0, pltpu.roll(swapped, PLANE - 1, 0))
    total = before_ref[...] + after_ref[...] + swapped + jnp.where(low, earlier, later) + beside_z(value, z)
    out_ref[...] = keep_ref[...] * start_ref[...] + spread_ref[...] * total


def plane_sweep(state, start, before, after, keep, spread):
    return pl.pallas_call(
        plane_sweep_kernel,
        out_shape=jax.ShapeDtypeStruct(state.shape, jnp.float32),
        compiler_params=params(),
    )(state, start, before, after, keep, spread)


def sweep_rows(source, start, keep, spread, target, first, last, low_end, high_end):
    shape = (SLABS, 128)
    low, z = lanes_of(shape)
    x = lax.broadcasted_iota(jnp.int32, shape, 0)
    zero = jnp.zeros(shape, jnp.float32)

    def swapped(q):
        return pltpu.roll(source[q], 64, 1) if low_end <= q < high_end else zero

    earlier, here = swapped(first - 1), swapped(first)
    for q in range(first, last):
        later = swapped(q + 1)
        value = source[q]
        total = here + jnp.where(low, earlier, later) + beside_z(value, z)
        total = total + jnp.where(x == 0, 0.0, pltpu.roll(value, 1, 0))
        total = total + jnp.where(x == SLABS - 1, 0.0, pltpu.roll(value, SLABS - 1, 0))
        target[q] = keep[q] * start[q] + spread[q] * total
        earlier, here = here, later


def coarse_step(fields, keep, spread, at, low_end, high_end):
    start, middle, result = fields.at[at], fields.at[2], fields.at[1 - at]
    sweep_rows(start, start, keep, spread, middle, low_end, high_end, low_end, high_end)
    sweep_rows(middle, start, keep, spread, result, low_end + 1, high_end - 1, low_end, high_end)
    return 1 - at


def first_links_kernel(c4_ref, c3_ref, c2_ref, c1_ref, keep_ref, spread_ref, out_ref, fields):
    rows = c4_ref.shape[0]
    fields[0] = c4_ref[...]
    at, low_end, high_end = 0, 0, rows
    for added in (c3_ref, c2_ref, c1_ref, None):
        at = coarse_step(fields, keep_ref, spread_ref, at, low_end, high_end)
        low_end, high_end = low_end + 1, high_end - 1
        if added is not None:
            for q in range(low_end, high_end):
                fields[at, q] = fields[at, q] + added[q - low_end]
    out_ref[...] = fields[at, low_end:high_end]


def power_kernel(links, window_ref, base_ref, keep_ref, spread_ref, out_ref, fields):
    rows = window_ref.shape[0]
    fields[0] = window_ref[...]
    at = 0
    for link in range(links):
        at = coarse_step(fields, keep_ref, spread_ref, at, link, rows - link)
    out_ref[...] = base_ref[...] + fields[at, links : rows - links]


def chain_call(kernel, rows, *operands):
    return pl.pallas_call(
        kernel,
        out_shape=jax.ShapeDtypeStruct((BLOCK, SLABS, 128), jnp.float32),
        scratch_shapes=[pltpu.VMEM((3, rows, SLABS, 128), jnp.float32)],
        compiler_params=params(),
    )(*operands)


def facing(distance, late):
    pairs = []
    for i in range(SLABS - distance):
        if (i // distance) % 2 == late:
            pairs += [(i, i + distance), (i + distance, i)]
    return pairs


def from_later(value, links, pairs):
    both = [((n + links) * SLABS + i, n * SLABS + j) for n in range(SLICES - links) for i, j in pairs]
    return lax.ppermute(value, ("tm", "space"), both)


def beside_later(value, links, distance, slab):
    one = from_later(value, links, facing(distance, 0))
    other = from_later(value, links, facing(distance, 1))
    upper = (slab // distance) % 2 == 1
    return jnp.where(upper, one, other), jnp.where(upper, other, one)


def windows(plane, reach):
    blocks = plane.reshape(SLABS, BLOCK, 128)
    padded = jnp.pad(blocks, ((reach, reach), (0, 0), (0, 0)))
    return jnp.concatenate([padded[i : i + SLABS] for i in range(2 * reach + 1)], axis=1)


def to_rows(parts):
    arrived = lax.all_to_all(parts, "space", 0, 0)
    return jnp.transpose(arrived, (1, 0, 2))


def per_device(end_state, cond, receivers, residuals):
    start_field = end_state[0]
    row_count, width_y, width_z = start_field.shape
    plane_size = width_y * width_z
    slab = lax.axis_index("space")
    slice_index = lax.axis_index("tm")
    odd = slab % 2 == 1
    is_final = slice_index == SLICES - 1

    def across_chips(value):
        return lax.ppermute(value, "space", facing(1, 1))

    def in_chip(value):
        return lax.ppermute(value, "space", facing(1, 0))

    def by_side(along, across):
        return jnp.where(odd, along, across), jnp.where(odd, across, along)

    ring = slice_index % 4
    quarter = width_y // 4
    share = lax.dynamic_slice_in_dim(cond, ring * quarter, quarter, axis=1)
    across = across_chips(jnp.where(odd, share[1], share[0]))
    along = in_chip(jnp.where(odd, share[0], share[1]))
    share = jnp.stack(by_side(along, across))
    for bit in (1, 2):
        upper = (ring // bit) % 2 == 1
        other = lax.ppermute(share, "tm", [(n, n ^ bit) for n in range(SLICES)])
        share = jnp.concatenate([jnp.where(upper, other, share), jnp.where(upper, share, other)], axis=1)

    local_row = receivers[0] // plane_size - slab * row_count + 1
    inside = (local_row >= 0) & (local_row < row_count + 2)
    wide_size = (row_count + 2) * plane_size
    target = jnp.where(inside, local_row * plane_size + receivers[0] % plane_size, wide_size)
    flat_source = jnp.zeros((wide_size,), jnp.float32).at[target].add(residuals[0], mode="drop")
    wide_source = flat_source.reshape(row_count + 2, width_y, width_z)
    place = jnp.stack([odd, slab > 0, slab < SLABS - 1]).astype(jnp.int32)

    coarse_cond = restrict(cond) / FINE_STEPS
    plane_spread = 1.0 / (coarse_cond + 1.5)
    plane_keep = coarse_cond * plane_spread
    plane_spread = 0.25 * plane_spread
    coarse_start = restrict(start_field)

    across, along = across_chips(start_field), in_chip(start_field)
    coarse_now = plane_sweep(
        coarse_start, coarse_start, *by_side(restrict(along), restrict(across)), plane_keep, plane_spread
    )
    field_now = fine_step(place, across, along, start_field, share, cond, wide_source)

    sent = jnp.concatenate([field_now.reshape(row_count * width_y, width_z), coarse_now])
    across, along = across_chips(sent), in_chip(sent)
    direct = plane_sweep(
        coarse_now, coarse_start, *by_side(along[-PLANE:], across[-PLANE:]), plane_keep, plane_spread
    )
    across, along = (value[:-PLANE].reshape(start_field.shape) for value in (across, along))
    field_now = fine_step(place, across, along, field_now, share, cond, wide_source)

    term = restrict(field_now) - jnp.where(is_final, 0.0, direct)
    second_half = slice_index % 2 == 1
    cond_windows = windows(coarse_cond, 2)
    cond_windows = jnp.where(second_half, cond_windows[:, 10:], cond_windows[:, :10])
    arrived = to_rows(jnp.concatenate([windows(term, 1), cond_windows], axis=1))
    rows, own_cond = arrived[:12], arrived[12:]
    other_cond = lax.ppermute(own_cond, "tm", [(n, n ^ 1) for n in range(SLICES)])
    row_cond = jnp.concatenate(
        [jnp.where(second_half, other_cond, own_cond), jnp.where(second_half, own_cond, other_cond)]
    )
    row_place = (slab - 2) * BLOCK + lax.broadcasted_iota(jnp.int32, row_cond.shape, 0)
    within = (row_place >= 0) & (row_place < PLANE)
    row_spread = jnp.where(within, 1.0 / (row_cond + 1.5), 0.0)
    row_keep = row_cond * row_spread
    row_spread = 0.25 * row_spread

    later = [(i, i) for i in range(SLABS)]
    links = [from_later(rows[4 - k : 8 + k], k, later) for k in (4, 3, 2, 1)]
    inner = slice(BLOCK, 4 * BLOCK)
    total = chain_call(first_links_kernel, 12, *links, row_keep[inner], row_spread[inner])

    centre = from_later(total, 4, later)
    before, after = beside_later(total, 4, 1, slab)
    window = jnp.concatenate([before, centre, after])
    total = chain_call(
        lambda *refs: power_kernel(4, *refs), 12, window, total, row_keep[inner], row_spread[inner]
    )

    centre = from_later(total, 8, later)
    near = from_later(total, 8, facing(1, 1))
    outward = [(j - 2, j) for j in range(2, SLABS, 2)] + [(j + 2, j) for j in range(1, SLABS - 2, 2)]
    far = from_later(total, 8, outward)
    swapped = lax.ppermute(jnp.stack([centre, near]), "space", facing(1, 0))
    window = jnp.where(
        odd,
        jnp.concatenate([swapped[1], swapped[0], centre, near, far]),
        jnp.concatenate([far, near, centre, swapped[0], swapped[1]]),
    )
    total = chain_call(lambda *refs: power_kernel(8, *refs), 20, window, total, row_keep, row_spread)

    back = lax.all_to_all(jnp.transpose(total, (1, 0, 2)), "space", 0, 0)
    propagated = jnp.where(is_final, direct, back.reshape(PLANE, 128))
    return prolong_add(propagated - direct, field_now)[None]


def solution(mesh):
    in_specs = (P("tm", "space", None, None), P("space", None, None), P("tm", None), P("tm", None))
    out_specs = P("tm", "space", None, None)
    return jax.shard_map(
        per_device, mesh=mesh, in_specs=in_specs, out_specs=out_specs, check_vma=False
    )
```

```python
import jax
import jax.numpy as jnp
from jax import lax
from jax.experimental import pallas as pl
from jax.experimental.pallas import tpu as pltpu
from jax.sharding import PartitionSpec as P

FINE_STEPS = 2
SWEEPS = 2
SLABS = 32
SLICES = 16
PLANE = 128
BLOCK = 4
EXACT = lax.Precision.HIGHEST


def params():
    return pltpu.CompilerParams(vmem_limit_bytes=16 * 1024 * 1024)


def halving(half):
    row = lax.broadcasted_iota(jnp.int32, (128, 128), 0)
    lane = lax.broadcasted_iota(jnp.int32, (128, 128), 1)
    return jnp.where(lane == row // 2 + 64 * half, 0.125, 0.0).astype(jnp.float32)


def restricted(ref, rows):
    total = jnp.zeros((PLANE, 128), jnp.float32)
    for half in range(2):
        parts = [ref[pl.ds(p * rows + 2 * half + r, PLANE, stride=4), :] for p in range(2) for r in range(2)]
        summed = (parts[0] + parts[1]) + (parts[2] + parts[3])
        total = total + jnp.dot(summed, halving(half), precision=EXACT, preferred_element_type=jnp.float32)
    return total


def restrict_kernel(field_ref, out_ref):
    out_ref[...] = restricted(field_ref, field_ref.shape[0] // 2)


def restrict(field):
    return pl.pallas_call(
        restrict_kernel,
        out_shape=jax.ShapeDtypeStruct((PLANE, 128), jnp.float32),
        compiler_params=params(),
    )(field.reshape(-1, 128))


def prolong_add_kernel(delta_ref, field_ref, out_ref):
    row = lax.broadcasted_iota(jnp.int32, (128, 128), 0)
    lane = lax.broadcasted_iota(jnp.int32, (128, 128), 1)
    delta = delta_ref[...]
    for half in range(2):
        spread = jnp.where(row == lane // 2 + 64 * half, 1.0, 0.0).astype(jnp.float32)
        wide = jnp.dot(delta, spread, precision=EXACT, preferred_element_type=jnp.float32)
        for plane in range(2):
            for r in range(2):
                rows = pl.ds(2 * half + r, PLANE, stride=4)
                out_ref[plane, rows, :] = field_ref[plane, rows, :] + wide


def prolong_add(delta, field):
    return pl.pallas_call(
        prolong_add_kernel,
        out_shape=jax.ShapeDtypeStruct(field.shape, jnp.float32),
        compiler_params=params(),
    )(delta, field)


def lanes_of(shape):
    lane = lax.broadcasted_iota(jnp.int32, shape, len(shape) - 1)
    return lane < 64, lane % 64


def beside_z(value, z):
    before = jnp.where(z == 0, 0.0, pltpu.roll(value, 1, 1))
    after = jnp.where(z == 63, 0.0, pltpu.roll(value, 127, 1))
    return before + after


def beside_in_plane(value):
    rows = value.shape[0]
    row = lax.broadcasted_iota(jnp.int32, value.shape, 0)
    lane = lax.broadcasted_iota(jnp.int32, value.shape, 1)
    above = jnp.where(row == 0, 0.0, pltpu.roll(value, 1, 0))
    below = jnp.where(row == rows - 1, 0.0, pltpu.roll(value, rows - 1, 0))
    before = jnp.where(lane == 0, 0.0, pltpu.roll(value, 1, 1))
    after = jnp.where(lane == 127, 0.0, pltpu.roll(value, 127, 1))
    return above + below + before + after


def two_sweeps(place_ref, across_ref, along_ref, field_ref, share_ref, cond_ref, source_ref):
    odd = place_ref[0] == 1
    rows = cond_ref.shape[1]

    def plane(ref, p):
        return ref[p * rows : (p + 1) * rows, :]

    planes = [jnp.where(odd, plane(along_ref, p), plane(across_ref, p)) for p in range(2)]
    planes += [plane(field_ref, p) for p in range(2)]
    planes += [jnp.where(odd, plane(across_ref, p), plane(along_ref, p)) for p in range(2)]
    conds = [share_ref[0], cond_ref[0], cond_ref[1], share_ref[1]]
    terms, diagonals, wide = [], [], []
    for i in range(4):
        value = planes[i + 1]
        terms.append(conds[i] * value + source_ref[i])
        diagonals.append(conds[i] + 6.0)
        total = planes[i] + planes[i + 2] + beside_in_plane(value)
        wide.append((terms[i] + total) / diagonals[i])
    wide[0] = jnp.where(place_ref[1] == 1, wide[0], 0.0)
    wide[3] = jnp.where(place_ref[2] == 1, wide[3], 0.0)
    swept = []
    for p in range(2):
        total = wide[p] + wide[p + 2] + beside_in_plane(wide[p + 1])
        swept.append((terms[p + 1] + total) / diagonals[p + 1])
    return swept


def plane_sweep(value, start, beside, keep, spread):
    low, z = lanes_of(value.shape)
    row = lax.broadcasted_iota(jnp.int32, value.shape, 0)
    swapped = pltpu.roll(value, 64, 1)
    earlier = jnp.where(row == 0, 0.0, pltpu.roll(swapped, 1, 0))
    later = jnp.where(row == PLANE - 1, 0.0, pltpu.roll(swapped, PLANE - 1, 0))
    total = beside + swapped + jnp.where(low, earlier, later) + beside_z(value, z)
    return keep * start + spread * total


def first_step_kernel(*refs):
    start_ref, keep_ref, spread_ref, out_ref = refs[7:]
    across_ref, along_ref, cond_ref = refs[1], refs[2], refs[5]
    rows = cond_ref.shape[1]
    for p, value in enumerate(two_sweeps(*refs[:7])):
        out_ref[p * rows : (p + 1) * rows, :] = value
    beside = restricted(across_ref, rows) + restricted(along_ref, rows)
    start = start_ref[...]
    out_ref[2 * rows :, :] = plane_sweep(start, start, beside, keep_ref[...], spread_ref[...])


def second_step_kernel(*refs):
    start_ref, keep_ref, spread_ref, field_ref, term_ref, direct_ref = refs[7:]
    place_ref, across_ref, along_ref, sent_ref, cond_ref = refs[0], refs[1], refs[2], refs[3], refs[5]
    rows = cond_ref.shape[1]
    for p, value in enumerate(two_sweeps(*refs[:7])):
        field_ref[p * rows : (p + 1) * rows, :] = value
    tail = slice(2 * rows, 2 * rows + PLANE)
    beside = across_ref[tail, :] + along_ref[tail, :]
    direct = plane_sweep(sent_ref[tail, :], start_ref[...], beside, keep_ref[...], spread_ref[...])
    direct_ref[...] = direct
    term_ref[...] = restricted(field_ref, rows) - jnp.where(place_ref[3] == 1, 0.0, direct)


def step_call(kernel, shapes, place, *operands):
    in_vmem = pl.BlockSpec(memory_space=pltpu.VMEM)
    return pl.pallas_call(
        kernel,
        out_shape=[jax.ShapeDtypeStruct(shape, jnp.float32) for shape in shapes],
        in_specs=[pl.BlockSpec(memory_space=pltpu.SMEM)] + [in_vmem] * len(operands),
        out_specs=[in_vmem] * len(shapes),
        compiler_params=params(),
    )(place, *operands)


def sweep_rows(source, start, keep, spread, target, first, last, low_end, high_end):
    shape = (SLABS, 128)
    low, z = lanes_of(shape)
    x = lax.broadcasted_iota(jnp.int32, shape, 0)
    zero = jnp.zeros(shape, jnp.float32)

    def swapped(q):
        return pltpu.roll(source[q], 64, 1) if low_end <= q < high_end else zero

    earlier, here = swapped(first - 1), swapped(first)
    for q in range(first, last):
        later = swapped(q + 1)
        value = source[q]
        total = here + jnp.where(low, earlier, later) + beside_z(value, z)
        total = total + jnp.where(x == 0, 0.0, pltpu.roll(value, 1, 0))
        total = total + jnp.where(x == SLABS - 1, 0.0, pltpu.roll(value, SLABS - 1, 0))
        target[q] = keep[q] * start[q] + spread[q] * total
        earlier, here = here, later


def coarse_step(fields, keep, spread, at, low_end, high_end):
    start, middle, result = fields.at[at], fields.at[2], fields.at[1 - at]
    sweep_rows(start, start, keep, spread, middle, low_end, high_end, low_end, high_end)
    sweep_rows(middle, start, keep, spread, result, low_end + 1, high_end - 1, low_end, high_end)
    return 1 - at


def first_links_kernel(left_ref, c4_ref, c3_ref, c2_ref, c1_ref, keep_ref, spread_ref, out_ref, fields):
    rows = keep_ref.shape[0]
    for q in range(rows):
        fields[0, q] = jnp.where(left_ref[0] >= 4, c4_ref[q], 0.0)
    at, low_end, high_end = 0, 0, rows
    for link, added in ((3, c3_ref), (2, c2_ref), (1, c1_ref), (0, None)):
        at = coarse_step(fields, keep_ref, spread_ref, at, low_end, high_end)
        low_end, high_end = low_end + 1, high_end - 1
        if added is not None:
            for q in range(low_end, high_end):
                fields[at, q] = fields[at, q] + jnp.where(left_ref[0] >= link, added[q - low_end], 0.0)
    out_ref[...] = fields[at, low_end:high_end]


def power_kernel(links, window_ref, base_ref, keep_ref, spread_ref, out_ref, fields):
    rows = window_ref.shape[0]
    fields[0] = window_ref[...]
    at = 0
    for link in range(links):
        at = coarse_step(fields, keep_ref, spread_ref, at, link, rows - link)
    out_ref[...] = base_ref[...] + fields[at, links : rows - links]


def chain_call(kernel, rows, *operands, scalars=0):
    spaces = [pltpu.SMEM] * scalars + [pltpu.VMEM] * (len(operands) - scalars)
    return pl.pallas_call(
        kernel,
        in_specs=[pl.BlockSpec(memory_space=space) for space in spaces],
        out_shape=jax.ShapeDtypeStruct((BLOCK, SLABS, 128), jnp.float32),
        scratch_shapes=[pltpu.VMEM((3, rows, SLABS, 128), jnp.float32)],
        compiler_params=params(),
    )(*operands)


def facing(distance, late):
    pairs = []
    for i in range(SLABS - distance):
        if (i // distance) % 2 == late:
            pairs += [(i, i + distance), (i + distance, i)]
    return pairs


def from_later(value, links, pairs):
    both = [((n + links) * SLABS + i, n * SLABS + j) for n in range(SLICES - links) for i, j in pairs]
    return lax.ppermute(value, ("tm", "space"), both)


def beside_later(value, links, distance, slab):
    one = from_later(value, links, facing(distance, 0))
    other = from_later(value, links, facing(distance, 1))
    upper = (slab // distance) % 2 == 1
    return jnp.where(upper, one, other), jnp.where(upper, other, one)


def windows(plane, reach):
    blocks = plane.reshape(SLABS, BLOCK, 128)
    padded = jnp.pad(blocks, ((reach, reach), (0, 0), (0, 0)))
    return jnp.concatenate([padded[i : i + SLABS] for i in range(2 * reach + 1)], axis=1)


def to_rows(parts):
    arrived = lax.all_to_all(parts, "space", 0, 0)
    return jnp.transpose(arrived, (1, 0, 2))


def per_device(end_state, cond, receivers, residuals):
    start_field = end_state[0]
    row_count, width_y, width_z = start_field.shape
    plane_size = width_y * width_z
    slab = lax.axis_index("space")
    slice_index = lax.axis_index("tm")
    odd = slab % 2 == 1
    is_final = slice_index == SLICES - 1

    def across_chips(value):
        return lax.ppermute(value, "space", facing(1, 1))

    def in_chip(value):
        return lax.ppermute(value, "space", facing(1, 0))

    def by_side(along, across):
        return jnp.where(odd, along, across), jnp.where(odd, across, along)

    ring = slice_index % 4
    quarter = width_y // 4
    share = lax.dynamic_slice_in_dim(cond, ring * quarter, quarter, axis=1)
    across = across_chips(jnp.where(odd, share[1], share[0]))
    along = in_chip(jnp.where(odd, share[0], share[1]))
    share = jnp.stack(by_side(along, across))
    for bit in (1, 2):
        upper = (ring // bit) % 2 == 1
        other = lax.ppermute(share, "tm", [(n, n ^ bit) for n in range(SLICES)])
        share = jnp.concatenate([jnp.where(upper, other, share), jnp.where(upper, share, other)], axis=1)

    local_row = receivers[0] // plane_size - slab * row_count + 1
    inside = (local_row >= 0) & (local_row < row_count + 2)
    wide_size = (row_count + 2) * plane_size
    target = jnp.where(inside, local_row * plane_size + receivers[0] % plane_size, wide_size)
    flat_source = jnp.zeros((wide_size,), jnp.float32).at[target].add(residuals[0], mode="drop")
    wide_source = flat_source.reshape(row_count + 2, width_y, width_z)
    place = jnp.stack([odd, slab > 0, slab < SLABS - 1, is_final]).astype(jnp.int32)

    coarse_cond = restrict(cond) / FINE_STEPS
    plane_spread = 1.0 / (coarse_cond + 1.5)
    plane_keep = coarse_cond * plane_spread
    plane_spread = 0.25 * plane_spread
    coarse_start = restrict(start_field)

    slab_rows = row_count * width_y
    start_rows = start_field.reshape(slab_rows, width_z)
    around = (share, cond, wide_source, coarse_start, plane_keep, plane_spread)
    across, along = across_chips(start_rows), in_chip(start_rows)
    sent, = step_call(
        first_step_kernel, [(slab_rows + PLANE, 128)], place, across, along, start_rows, *around
    )
    across, along = across_chips(sent), in_chip(sent)
    field_now, term, direct = step_call(
        second_step_kernel, [(slab_rows, 128), (PLANE, 128), (PLANE, 128)], place, across, along, sent, *around
    )
    field_now = field_now.reshape(start_field.shape)

    turn = slice_index % 5
    cond_block = lax.dynamic_slice_in_dim(windows(coarse_cond, 2), turn * BLOCK, BLOCK, axis=1)
    arrived = to_rows(jnp.concatenate([windows(term, 1), cond_block], axis=1))
    links, blocks = {}, [arrived[12:]]
    for k in (1, 2, 3, 4):
        pairs = [((n + k if n + k < SLICES else n + k - 15), n) for n in range(SLICES - 1)]
        links[k] = lax.ppermute(jnp.concatenate([arrived[4 - k : 8 + k], arrived[12:]]), "tm", pairs)
        blocks.append(links[k][-BLOCK:])
    row_cond = jnp.concatenate(blocks + blocks[:-1])
    row_cond = lax.dynamic_slice_in_dim(row_cond, (5 - turn) % 5 * BLOCK, 5 * BLOCK, axis=0)
    row_place = (slab - 2) * BLOCK + lax.broadcasted_iota(jnp.int32, row_cond.shape, 0)
    within = (row_place >= 0) & (row_place < PLANE)
    row_spread = jnp.where(within, 1.0 / (row_cond + 1.5), 0.0)
    row_keep = row_cond * row_spread
    row_spread = 0.25 * row_spread

    later = [(i, i) for i in range(SLABS)]
    inner = slice(BLOCK, 4 * BLOCK)
    left = (SLICES - 1 - slice_index)[None].astype(jnp.int32)
    total = chain_call(
        first_links_kernel, 12, left, *(links[k] for k in (4, 3, 2, 1)), row_keep[inner], row_spread[inner], scalars=1
    )

    centre = from_later(total, 4, later)
    before, after = beside_later(total, 4, 1, slab)
    window = jnp.concatenate([before, centre, after])
    total = chain_call(
        lambda *refs: power_kernel(4, *refs), 12, window, total, row_keep[inner], row_spread[inner]
    )

    centre = from_later(total, 8, later)
    near = from_later(total, 8, facing(1, 1))
    outward = [(j - 2, j) for j in range(2, SLABS, 2)] + [(j + 2, j) for j in range(1, SLABS - 2, 2)]
    far = from_later(total, 8, outward)
    swapped = lax.ppermute(jnp.stack([centre, near]), "space", facing(1, 0))
    window = jnp.where(
        odd,
        jnp.concatenate([swapped[1], swapped[0], centre, near, far]),
        jnp.concatenate([far, near, centre, swapped[0], swapped[1]]),
    )
    total = chain_call(lambda *refs: power_kernel(8, *refs), 20, window, total, row_keep, row_spread)

    back = lax.all_to_all(jnp.transpose(total, (1, 0, 2)), "space", 0, 0)
    propagated = jnp.where(is_final, direct, back.reshape(PLANE, 128))
    return prolong_add(propagated - direct, field_now)[None]


def solution(mesh):
    in_specs = (P("tm", "space", None, None), P("space", None, None), P("tm", None), P("tm", None))
    out_specs = P("tm", "space", None, None)
    return jax.shard_map(
        per_device, mesh=mesh, in_specs=in_specs, out_specs=out_specs, check_vma=False
    )
```

```python
import jax
import jax.numpy as jnp
from jax import lax
from jax.experimental import pallas as pl
from jax.experimental.pallas import tpu as pltpu
from jax.sharding import PartitionSpec as P

FINE_STEPS = 2
SWEEPS = 2
SLABS = 32
SLICES = 16
PLANE = 128
BLOCK = 4
EXACT = lax.Precision.HIGHEST


def params():
    return pltpu.CompilerParams(vmem_limit_bytes=16 * 1024 * 1024)


def halving(half):
    row = lax.broadcasted_iota(jnp.int32, (128, 128), 0)
    lane = lax.broadcasted_iota(jnp.int32, (128, 128), 1)
    return jnp.where(lane == row // 2 + 64 * half, 0.125, 0.0).astype(jnp.float32)


def restricted(ref, rows):
    total = jnp.zeros((PLANE, 128), jnp.float32)
    for half in range(2):
        parts = [ref[pl.ds(p * rows + 2 * half + r, PLANE, stride=4), :] for p in range(2) for r in range(2)]
        summed = (parts[0] + parts[1]) + (parts[2] + parts[3])
        total = total + jnp.dot(summed, halving(half), precision=EXACT, preferred_element_type=jnp.float32)
    return total


def restrict_kernel(field_ref, out_ref):
    out_ref[...] = restricted(field_ref, field_ref.shape[0] // 2)


def restrict(field):
    return pl.pallas_call(
        restrict_kernel,
        out_shape=jax.ShapeDtypeStruct((PLANE, 128), jnp.float32),
        compiler_params=params(),
    )(field.reshape(-1, 128))


def prolong_add_kernel(delta_ref, field_ref, out_ref):
    row = lax.broadcasted_iota(jnp.int32, (128, 128), 0)
    lane = lax.broadcasted_iota(jnp.int32, (128, 128), 1)
    delta = delta_ref[...]
    for half in range(2):
        spread = jnp.where(row == lane // 2 + 64 * half, 1.0, 0.0).astype(jnp.float32)
        wide = jnp.dot(delta, spread, precision=EXACT, preferred_element_type=jnp.float32)
        for plane in range(2):
            for r in range(2):
                rows = pl.ds(2 * half + r, PLANE, stride=4)
                out_ref[plane, rows, :] = field_ref[plane, rows, :] + wide


def prolong_add(delta, field):
    return pl.pallas_call(
        prolong_add_kernel,
        out_shape=jax.ShapeDtypeStruct(field.shape, jnp.float32),
        compiler_params=params(),
    )(delta, field)


def lanes_of(shape):
    lane = lax.broadcasted_iota(jnp.int32, shape, len(shape) - 1)
    return lane < 64, lane % 64


def beside_z(value, z):
    before = jnp.where(z == 0, 0.0, pltpu.roll(value, 1, 1))
    after = jnp.where(z == 63, 0.0, pltpu.roll(value, 127, 1))
    return before + after


def beside_in_plane(value):
    rows = value.shape[0]
    row = lax.broadcasted_iota(jnp.int32, value.shape, 0)
    lane = lax.broadcasted_iota(jnp.int32, value.shape, 1)
    above = jnp.where(row == 0, 0.0, pltpu.roll(value, 1, 0))
    below = jnp.where(row == rows - 1, 0.0, pltpu.roll(value, rows - 1, 0))
    before = jnp.where(lane == 0, 0.0, pltpu.roll(value, 1, 1))
    after = jnp.where(lane == 127, 0.0, pltpu.roll(value, 127, 1))
    return above + below + before + after


def two_sweeps(place_ref, across_ref, along_ref, field_ref, share_ref, cond_ref, source_ref):
    odd = place_ref[0] == 1
    rows = cond_ref.shape[1]

    def plane(ref, p):
        return ref[p * rows : (p + 1) * rows, :]

    planes = [jnp.where(odd, plane(along_ref, p), plane(across_ref, p)) for p in range(2)]
    planes += [plane(field_ref, p) for p in range(2)]
    planes += [jnp.where(odd, plane(across_ref, p), plane(along_ref, p)) for p in range(2)]
    conds = [share_ref[0], cond_ref[0], cond_ref[1], share_ref[1]]
    terms, diagonals, wide = [], [], []
    for i in range(4):
        value = planes[i + 1]
        terms.append(conds[i] * value + source_ref[i])
        diagonals.append(conds[i] + 6.0)
        total = planes[i] + planes[i + 2] + beside_in_plane(value)
        wide.append((terms[i] + total) / diagonals[i])
    wide[0] = jnp.where(place_ref[1] == 1, wide[0], 0.0)
    wide[3] = jnp.where(place_ref[2] == 1, wide[3], 0.0)
    swept = []
    for p in range(2):
        total = wide[p] + wide[p + 2] + beside_in_plane(wide[p + 1])
        swept.append((terms[p + 1] + total) / diagonals[p + 1])
    return swept


def plane_sweep(value, start, beside, keep, spread):
    low, z = lanes_of(value.shape)
    row = lax.broadcasted_iota(jnp.int32, value.shape, 0)
    swapped = pltpu.roll(value, 64, 1)
    earlier = jnp.where(row == 0, 0.0, pltpu.roll(swapped, 1, 0))
    later = jnp.where(row == PLANE - 1, 0.0, pltpu.roll(swapped, PLANE - 1, 0))
    total = beside + swapped + jnp.where(low, earlier, later) + beside_z(value, z)
    return keep * start + spread * total


def first_step_kernel(*refs):
    start_ref, keep_ref, spread_ref, out_ref = refs[7:]
    across_ref, along_ref, cond_ref = refs[1], refs[2], refs[5]
    rows = cond_ref.shape[1]
    for p, value in enumerate(two_sweeps(*refs[:7])):
        out_ref[p * rows : (p + 1) * rows, :] = value
    beside = restricted(across_ref, rows) + restricted(along_ref, rows)
    start = start_ref[...]
    out_ref[2 * rows :, :] = plane_sweep(start, start, beside, keep_ref[...], spread_ref[...])


def second_step_kernel(*refs):
    start_ref, keep_ref, spread_ref, field_ref, term_ref, direct_ref = refs[7:]
    place_ref, across_ref, along_ref, sent_ref, cond_ref = refs[0], refs[1], refs[2], refs[3], refs[5]
    rows = cond_ref.shape[1]
    for p, value in enumerate(two_sweeps(*refs[:7])):
        field_ref[p * rows : (p + 1) * rows, :] = value
    tail = slice(2 * rows, 2 * rows + PLANE)
    beside = across_ref[tail, :] + along_ref[tail, :]
    direct = plane_sweep(sent_ref[tail, :], start_ref[...], beside, keep_ref[...], spread_ref[...])
    direct_ref[...] = direct
    term_ref[...] = restricted(field_ref, rows) - jnp.where(place_ref[3] == 1, 0.0, direct)


def step_call(kernel, shapes, place, *operands):
    in_vmem = pl.BlockSpec(memory_space=pltpu.VMEM)
    return pl.pallas_call(
        kernel,
        out_shape=[jax.ShapeDtypeStruct(shape, jnp.float32) for shape in shapes],
        in_specs=[pl.BlockSpec(memory_space=pltpu.SMEM)] + [in_vmem] * len(operands),
        out_specs=[in_vmem] * len(shapes),
        compiler_params=params(),
    )(place, *operands)


def sweep_rows(source, start, keep, spread, target, first, last, low_end, high_end):
    shape = (SLABS, 128)
    low, z = lanes_of(shape)
    x = lax.broadcasted_iota(jnp.int32, shape, 0)
    zero = jnp.zeros(shape, jnp.float32)

    def swapped(q):
        return pltpu.roll(source[q], 64, 1) if low_end <= q < high_end else zero

    earlier, here = swapped(first - 1), swapped(first)
    for q in range(first, last):
        later = swapped(q + 1)
        value = source[q]
        total = here + jnp.where(low, earlier, later) + beside_z(value, z)
        total = total + jnp.where(x == 0, 0.0, pltpu.roll(value, 1, 0))
        total = total + jnp.where(x == SLABS - 1, 0.0, pltpu.roll(value, SLABS - 1, 0))
        target[q] = keep[q] * start[q] + spread[q] * total
        earlier, here = here, later


def coarse_step(fields, keep, spread, at, low_end, high_end):
    start, middle, result = fields.at[at], fields.at[2], fields.at[1 - at]
    sweep_rows(start, start, keep, spread, middle, low_end, high_end, low_end, high_end)
    sweep_rows(middle, start, keep, spread, result, low_end + 1, high_end - 1, low_end, high_end)
    return 1 - at


def first_links_kernel(c4_ref, c3_ref, c2_ref, c1_ref, keep_ref, spread_ref, out_ref, fields):
    rows = c4_ref.shape[0]
    fields[0] = c4_ref[...]
    at, low_end, high_end = 0, 0, rows
    for added in (c3_ref, c2_ref, c1_ref, None):
        at = coarse_step(fields, keep_ref, spread_ref, at, low_end, high_end)
        low_end, high_end = low_end + 1, high_end - 1
        if added is not None:
            for q in range(low_end, high_end):
                fields[at, q] = fields[at, q] + added[q - low_end]
    out_ref[...] = fields[at, low_end:high_end]


def power_kernel(links, window_ref, base_ref, keep_ref, spread_ref, out_ref, fields):
    rows = window_ref.shape[0]
    fields[0] = window_ref[...]
    at = 0
    for link in range(links):
        at = coarse_step(fields, keep_ref, spread_ref, at, link, rows - link)
    out_ref[...] = base_ref[...] + fields[at, links : rows - links]


def chain_call(kernel, rows, *operands):
    return pl.pallas_call(
        kernel,
        out_shape=jax.ShapeDtypeStruct((BLOCK, SLABS, 128), jnp.float32),
        scratch_shapes=[pltpu.VMEM((3, rows, SLABS, 128), jnp.float32)],
        compiler_params=params(),
    )(*operands)


def facing(distance, late):
    pairs = []
    for i in range(SLABS - distance):
        if (i // distance) % 2 == late:
            pairs += [(i, i + distance), (i + distance, i)]
    return pairs


def from_later(value, links, pairs):
    both = [((n + links) * SLABS + i, n * SLABS + j) for n in range(SLICES - links) for i, j in pairs]
    return lax.ppermute(value, ("tm", "space"), both)


def beside_later(value, links, distance, slab):
    one = from_later(value, links, facing(distance, 0))
    other = from_later(value, links, facing(distance, 1))
    upper = (slab // distance) % 2 == 1
    return jnp.where(upper, one, other), jnp.where(upper, other, one)


def windows(plane, reach):
    blocks = plane.reshape(SLABS, BLOCK, 128)
    padded = jnp.pad(blocks, ((reach, reach), (0, 0), (0, 0)))
    return jnp.concatenate([padded[i : i + SLABS] for i in range(2 * reach + 1)], axis=1)


def to_rows(parts):
    arrived = lax.all_to_all(parts, "space", 0, 0)
    return jnp.transpose(arrived, (1, 0, 2))


def per_device(end_state, cond, receivers, residuals):
    start_field = end_state[0]
    row_count, width_y, width_z = start_field.shape
    plane_size = width_y * width_z
    slab = lax.axis_index("space")
    slice_index = lax.axis_index("tm")
    odd = slab % 2 == 1
    is_final = slice_index == SLICES - 1

    def across_chips(value):
        return lax.ppermute(value, "space", facing(1, 1))

    def in_chip(value):
        return lax.ppermute(value, "space", facing(1, 0))

    def by_side(along, across):
        return jnp.where(odd, along, across), jnp.where(odd, across, along)

    ring = slice_index % 4
    quarter = width_y // 4
    share = lax.dynamic_slice_in_dim(cond, ring * quarter, quarter, axis=1)
    across = across_chips(jnp.where(odd, share[1], share[0]))
    along = in_chip(jnp.where(odd, share[0], share[1]))
    share = jnp.stack(by_side(along, across))
    for bit in (1, 2):
        upper = (ring // bit) % 2 == 1
        other = lax.ppermute(share, "tm", [(n, n ^ bit) for n in range(SLICES)])
        share = jnp.concatenate([jnp.where(upper, other, share), jnp.where(upper, share, other)], axis=1)

    local_row = receivers[0] // plane_size - slab * row_count + 1
    inside = (local_row >= 0) & (local_row < row_count + 2)
    wide_size = (row_count + 2) * plane_size
    target = jnp.where(inside, local_row * plane_size + receivers[0] % plane_size, wide_size)
    flat_source = jnp.zeros((wide_size,), jnp.float32).at[target].add(residuals[0], mode="drop")
    wide_source = flat_source.reshape(row_count + 2, width_y, width_z)
    place = jnp.stack([odd, slab > 0, slab < SLABS - 1, is_final]).astype(jnp.int32)

    coarse_cond = restrict(cond) / FINE_STEPS
    plane_spread = 1.0 / (coarse_cond + 1.5)
    plane_keep = coarse_cond * plane_spread
    plane_spread = 0.25 * plane_spread
    coarse_start = restrict(start_field)

    slab_rows = row_count * width_y
    start_rows = start_field.reshape(slab_rows, width_z)
    around = (share, cond, wide_source, coarse_start, plane_keep, plane_spread)
    across, along = across_chips(start_rows), in_chip(start_rows)
    sent, = step_call(
        first_step_kernel, [(slab_rows + PLANE, 128)], place, across, along, start_rows, *around
    )
    across, along = across_chips(sent), in_chip(sent)
    field_now, term, direct = step_call(
        second_step_kernel, [(slab_rows, 128), (PLANE, 128), (PLANE, 128)], place, across, along, sent, *around
    )
    field_now = field_now.reshape(start_field.shape)

    tall = jnp.pad(coarse_cond, ((2 * BLOCK, 2 * BLOCK), (0, 0)))
    backwards = sum((slice_index // bit) % 2 * (SLICES // 2 // bit) for bit in (1, 2, 4, 8))
    shares = []
    for i in range(2):
        at = (slab - 2 * backwards - i) % SLABS
        window = lax.dynamic_slice_in_dim(tall, at * BLOCK, 5 * BLOCK, axis=0)
        pairs = []
        for n in range(SLICES):
            turned = sum((n // bit) % 2 * (SLICES // 2 // bit) for bit in (1, 2, 4, 8))
            pairs += [(n * SLABS + j, n * SLABS + (j - 2 * turned - i) % SLABS) for j in range(SLABS)]
        shares.append(lax.ppermute(window, ("tm", "space"), pairs))
    gathered = jnp.stack(shares)
    for bit in (8, 4, 2, 1):
        upper = (slice_index // bit) % 2 == 1
        other = lax.ppermute(gathered, "tm", [(n, n ^ bit) for n in range(SLICES)])
        gathered = jnp.concatenate([jnp.where(upper, other, gathered), jnp.where(upper, gathered, other)])
    turned = lax.dynamic_slice_in_dim(
        jnp.concatenate([gathered, gathered]), (SLABS - slab) % SLABS, SLABS, axis=0
    )
    row_cond = jnp.transpose(turned, (1, 0, 2))

    rows = to_rows(windows(term, 1))
    later = [(i, i) for i in range(SLABS)]
    links = {k: from_later(rows[4 - k : 8 + k], k, later) for k in (1, 2, 3, 4)}
    row_place = (slab - 2) * BLOCK + lax.broadcasted_iota(jnp.int32, row_cond.shape, 0)
    within = (row_place >= 0) & (row_place < PLANE)
    row_spread = jnp.where(within, 1.0 / (row_cond + 1.5), 0.0)
    row_keep = row_cond * row_spread
    row_spread = 0.25 * row_spread

    inner = slice(BLOCK, 4 * BLOCK)
    total = chain_call(
        first_links_kernel, 12, *(links[k] for k in (4, 3, 2, 1)), row_keep[inner], row_spread[inner]
    )

    centre = from_later(total, 4, later)
    before, after = beside_later(total, 4, 1, slab)
    window = jnp.concatenate([before, centre, after])
    total = chain_call(
        lambda *refs: power_kernel(4, *refs), 12, window, total, row_keep[inner], row_spread[inner]
    )

    centre = from_later(total, 8, later)
    near = from_later(total, 8, facing(1, 1))
    outward = [(j - 2, j) for j in range(2, SLABS, 2)] + [(j + 2, j) for j in range(1, SLABS - 2, 2)]
    far = from_later(total, 8, outward)
    swapped = lax.ppermute(jnp.stack([centre, near]), "space", facing(1, 0))
    window = jnp.where(
        odd,
        jnp.concatenate([swapped[1], swapped[0], centre, near, far]),
        jnp.concatenate([far, near, centre, swapped[0], swapped[1]]),
    )
    total = chain_call(lambda *refs: power_kernel(8, *refs), 20, window, total, row_keep, row_spread)

    back = lax.all_to_all(jnp.transpose(total, (1, 0, 2)), "space", 0, 0)
    propagated = jnp.where(is_final, direct, back.reshape(PLANE, 128))
    return prolong_add(propagated - direct, field_now)[None]


def solution(mesh):
    in_specs = (P("tm", "space", None, None), P("space", None, None), P("tm", None), P("tm", None))
    out_specs = P("tm", "space", None, None)
    return jax.shard_map(
        per_device, mesh=mesh, in_specs=in_specs, out_specs=out_specs, check_vma=False
    )
```

```python
import jax
import jax.numpy as jnp
from jax import lax
from jax.experimental import pallas as pl
from jax.experimental.pallas import tpu as pltpu
from jax.sharding import PartitionSpec as P

FINE_STEPS = 2
SWEEPS = 2
SLABS = 32
SLICES = 16
PLANE = 128
BLOCK = 4
EXACT = lax.Precision.HIGHEST


def params():
    return pltpu.CompilerParams(vmem_limit_bytes=16 * 1024 * 1024)


def halving(half):
    row = lax.broadcasted_iota(jnp.int32, (128, 128), 0)
    lane = lax.broadcasted_iota(jnp.int32, (128, 128), 1)
    return jnp.where(lane == row // 2 + 64 * half, 0.125, 0.0).astype(jnp.float32)


def restricted(ref, rows):
    total = jnp.zeros((PLANE, 128), jnp.float32)
    for half in range(2):
        parts = [ref[pl.ds(p * rows + 2 * half + r, PLANE, stride=4), :] for p in range(2) for r in range(2)]
        summed = (parts[0] + parts[1]) + (parts[2] + parts[3])
        total = total + jnp.dot(summed, halving(half), precision=EXACT, preferred_element_type=jnp.float32)
    return total


def restrict_kernel(field_ref, out_ref):
    out_ref[...] = restricted(field_ref, field_ref.shape[0] // 2)


def restrict(field):
    return pl.pallas_call(
        restrict_kernel,
        out_shape=jax.ShapeDtypeStruct((PLANE, 128), jnp.float32),
        compiler_params=params(),
    )(field.reshape(-1, 128))


def prolong_add_kernel(delta_ref, field_ref, out_ref):
    row = lax.broadcasted_iota(jnp.int32, (128, 128), 0)
    lane = lax.broadcasted_iota(jnp.int32, (128, 128), 1)
    delta = delta_ref[...]
    for half in range(2):
        spread = jnp.where(row == lane // 2 + 64 * half, 1.0, 0.0).astype(jnp.float32)
        wide = jnp.dot(delta, spread, precision=EXACT, preferred_element_type=jnp.float32)
        for plane in range(2):
            for r in range(2):
                rows = pl.ds(2 * half + r, PLANE, stride=4)
                out_ref[plane, rows, :] = field_ref[plane, rows, :] + wide


def prolong_add(delta, field):
    return pl.pallas_call(
        prolong_add_kernel,
        out_shape=jax.ShapeDtypeStruct(field.shape, jnp.float32),
        compiler_params=params(),
    )(delta, field)


def lanes_of(shape):
    lane = lax.broadcasted_iota(jnp.int32, shape, len(shape) - 1)
    return lane < 64, lane % 64


def beside_z(value, z):
    before = jnp.where(z == 0, 0.0, pltpu.roll(value, 1, 1))
    after = jnp.where(z == 63, 0.0, pltpu.roll(value, 127, 1))
    return before + after


def beside_in_plane(value):
    rows = value.shape[0]
    row = lax.broadcasted_iota(jnp.int32, value.shape, 0)
    lane = lax.broadcasted_iota(jnp.int32, value.shape, 1)
    above = jnp.where(row == 0, 0.0, pltpu.roll(value, 1, 0))
    below = jnp.where(row == rows - 1, 0.0, pltpu.roll(value, rows - 1, 0))
    before = jnp.where(lane == 0, 0.0, pltpu.roll(value, 1, 1))
    after = jnp.where(lane == 127, 0.0, pltpu.roll(value, 127, 1))
    return above + below + before + after


def two_sweeps(place_ref, across_ref, along_ref, field_ref, share_ref, cond_ref, source_ref):
    odd = place_ref[0] == 1
    rows = cond_ref.shape[1]

    def plane(ref, p):
        return ref[p * rows : (p + 1) * rows, :]

    planes = [jnp.where(odd, plane(along_ref, p), plane(across_ref, p)) for p in range(2)]
    planes += [plane(field_ref, p) for p in range(2)]
    planes += [jnp.where(odd, plane(across_ref, p), plane(along_ref, p)) for p in range(2)]
    conds = [share_ref[0], cond_ref[0], cond_ref[1], share_ref[1]]
    terms, diagonals, wide = [], [], []
    for i in range(4):
        value = planes[i + 1]
        terms.append(conds[i] * value + source_ref[i])
        diagonals.append(conds[i] + 6.0)
        total = planes[i] + planes[i + 2] + beside_in_plane(value)
        wide.append((terms[i] + total) / diagonals[i])
    wide[0] = jnp.where(place_ref[1] == 1, wide[0], 0.0)
    wide[3] = jnp.where(place_ref[2] == 1, wide[3], 0.0)
    swept = []
    for p in range(2):
        total = wide[p] + wide[p + 2] + beside_in_plane(wide[p + 1])
        swept.append((terms[p + 1] + total) / diagonals[p + 1])
    return swept


def plane_sweep(value, start, beside, keep, spread):
    low, z = lanes_of(value.shape)
    row = lax.broadcasted_iota(jnp.int32, value.shape, 0)
    swapped = pltpu.roll(value, 64, 1)
    earlier = jnp.where(row == 0, 0.0, pltpu.roll(swapped, 1, 0))
    later = jnp.where(row == PLANE - 1, 0.0, pltpu.roll(swapped, PLANE - 1, 0))
    total = beside + swapped + jnp.where(low, earlier, later) + beside_z(value, z)
    return keep * start + spread * total


def first_step_kernel(*refs):
    start_ref, keep_ref, spread_ref, out_ref = refs[7:]
    across_ref, along_ref, cond_ref = refs[1], refs[2], refs[5]
    rows = cond_ref.shape[1]
    for p, value in enumerate(two_sweeps(*refs[:7])):
        out_ref[p * rows : (p + 1) * rows, :] = value
    beside = restricted(across_ref, rows) + restricted(along_ref, rows)
    start = start_ref[...]
    out_ref[2 * rows :, :] = plane_sweep(start, start, beside, keep_ref[...], spread_ref[...])


def second_step_kernel(*refs):
    start_ref, keep_ref, spread_ref, field_ref, term_ref, direct_ref = refs[7:]
    place_ref, across_ref, along_ref, sent_ref, cond_ref = refs[0], refs[1], refs[2], refs[3], refs[5]
    rows = cond_ref.shape[1]
    for p, value in enumerate(two_sweeps(*refs[:7])):
        field_ref[p * rows : (p + 1) * rows, :] = value
    tail = slice(2 * rows, 2 * rows + PLANE)
    beside = across_ref[tail, :] + along_ref[tail, :]
    direct = plane_sweep(sent_ref[tail, :], start_ref[...], beside, keep_ref[...], spread_ref[...])
    direct_ref[...] = direct
    term_ref[...] = restricted(field_ref, rows) - jnp.where(place_ref[3] == 1, 0.0, direct)


def step_call(kernel, shapes, place, *operands):
    in_vmem = pl.BlockSpec(memory_space=pltpu.VMEM)
    return pl.pallas_call(
        kernel,
        out_shape=[jax.ShapeDtypeStruct(shape, jnp.float32) for shape in shapes],
        in_specs=[pl.BlockSpec(memory_space=pltpu.SMEM)] + [in_vmem] * len(operands),
        out_specs=[in_vmem] * len(shapes),
        compiler_params=params(),
    )(place, *operands)


def sweep_rows(source, start, keep, spread, target, first, last, low_end, high_end):
    shape = (SLABS, 128)
    low, z = lanes_of(shape)
    x = lax.broadcasted_iota(jnp.int32, shape, 0)
    zero = jnp.zeros(shape, jnp.float32)

    def swapped(q):
        return pltpu.roll(source[q], 64, 1) if low_end <= q < high_end else zero

    earlier, here = swapped(first - 1), swapped(first)
    for q in range(first, last):
        later = swapped(q + 1)
        value = source[q]
        total = here + jnp.where(low, earlier, later) + beside_z(value, z)
        total = total + jnp.where(x == 0, 0.0, pltpu.roll(value, 1, 0))
        total = total + jnp.where(x == SLABS - 1, 0.0, pltpu.roll(value, SLABS - 1, 0))
        target[q] = keep[q] * start[q] + spread[q] * total
        earlier, here = here, later


def coarse_step(fields, keep, spread, at, low_end, high_end):
    start, middle, result = fields.at[at], fields.at[2], fields.at[1 - at]
    sweep_rows(start, start, keep, spread, middle, low_end, high_end, low_end, high_end)
    sweep_rows(middle, start, keep, spread, result, low_end + 1, high_end - 1, low_end, high_end)
    return 1 - at


def first_links_kernel(c4_ref, c3_ref, c2_ref, c1_ref, keep_ref, spread_ref, out_ref, fields):
    rows = c4_ref.shape[0]
    fields[0] = c4_ref[...]
    at, low_end, high_end = 0, 0, rows
    for added in (c3_ref, c2_ref, c1_ref, None):
        at = coarse_step(fields, keep_ref, spread_ref, at, low_end, high_end)
        low_end, high_end = low_end + 1, high_end - 1
        if added is not None:
            for q in range(low_end, high_end):
                fields[at, q] = fields[at, q] + added[q - low_end]
    out_ref[...] = fields[at, low_end:high_end]


def power_kernel(links, window_ref, base_ref, keep_ref, spread_ref, out_ref, fields):
    rows = window_ref.shape[0]
    fields[0] = window_ref[...]
    at = 0
    for link in range(links):
        at = coarse_step(fields, keep_ref, spread_ref, at, link, rows - link)
    out_ref[...] = base_ref[...] + fields[at, links : rows - links]


def chain_call(kernel, rows, *operands):
    return pl.pallas_call(
        kernel,
        out_shape=jax.ShapeDtypeStruct((BLOCK, SLABS, 128), jnp.float32),
        scratch_shapes=[pltpu.VMEM((3, rows, SLABS, 128), jnp.float32)],
        compiler_params=params(),
    )(*operands)


def facing(distance, late):
    pairs = []
    for i in range(SLABS - distance):
        if (i // distance) % 2 == late:
            pairs += [(i, i + distance), (i + distance, i)]
    return pairs


def from_later(value, links, pairs):
    both = [((n + links) * SLABS + i, n * SLABS + j) for n in range(SLICES - links) for i, j in pairs]
    return lax.ppermute(value, ("tm", "space"), both)


def beside_later(value, links, distance, slab):
    one = from_later(value, links, facing(distance, 0))
    other = from_later(value, links, facing(distance, 1))
    upper = (slab // distance) % 2 == 1
    return jnp.where(upper, one, other), jnp.where(upper, other, one)


def windows(plane, reach):
    blocks = plane.reshape(SLABS, BLOCK, 128)
    padded = jnp.pad(blocks, ((reach, reach), (0, 0), (0, 0)))
    return jnp.concatenate([padded[i : i + SLABS] for i in range(2 * reach + 1)], axis=1)


def to_rows(parts):
    arrived = lax.all_to_all(parts, "space", 0, 0)
    return jnp.transpose(arrived, (1, 0, 2))


def per_device(end_state, cond, receivers, residuals):
    start_field = end_state[0]
    row_count, width_y, width_z = start_field.shape
    plane_size = width_y * width_z
    slab = lax.axis_index("space")
    slice_index = lax.axis_index("tm")
    odd = slab % 2 == 1
    is_final = slice_index == SLICES - 1

    def across_chips(value):
        return lax.ppermute(value, "space", facing(1, 1))

    def in_chip(value):
        return lax.ppermute(value, "space", facing(1, 0))

    def by_side(along, across):
        return jnp.where(odd, along, across), jnp.where(odd, across, along)

    ring = slice_index % 4
    quarter = width_y // 4
    share = lax.dynamic_slice_in_dim(cond, ring * quarter, quarter, axis=1)
    across = across_chips(jnp.where(odd, share[1], share[0]))
    along = in_chip(jnp.where(odd, share[0], share[1]))
    share = jnp.stack(by_side(along, across))
    for bit in (1, 2):
        upper = (ring // bit) % 2 == 1
        other = lax.ppermute(share, "tm", [(n, n ^ bit) for n in range(SLICES)])
        share = jnp.concatenate([jnp.where(upper, other, share), jnp.where(upper, share, other)], axis=1)

    local_row = receivers[0] // plane_size - slab * row_count + 1
    inside = (local_row >= 0) & (local_row < row_count + 2)
    wide_size = (row_count + 2) * plane_size
    target = jnp.where(inside, local_row * plane_size + receivers[0] % plane_size, wide_size)
    flat_source = jnp.zeros((wide_size,), jnp.float32).at[target].add(residuals[0], mode="drop")
    wide_source = flat_source.reshape(row_count + 2, width_y, width_z)
    place = jnp.stack([odd, slab > 0, slab < SLABS - 1, is_final]).astype(jnp.int32)

    coarse_cond = restrict(cond) / FINE_STEPS
    plane_spread = 1.0 / (coarse_cond + 1.5)
    plane_keep = coarse_cond * plane_spread
    plane_spread = 0.25 * plane_spread
    coarse_start = restrict(start_field)

    slab_rows = row_count * width_y
    start_rows = start_field.reshape(slab_rows, width_z)
    tall = jnp.pad(coarse_cond, ((2 * BLOCK, 2 * BLOCK), (0, 0)))
    tall, share = lax.optimization_barrier((tall, share))
    shares = []
    for i in range(2):
        at = (slab - 2 * (ring * 4 + slice_index // 4) - i) % SLABS
        window = lax.dynamic_slice_in_dim(tall, at * BLOCK, 5 * BLOCK, axis=0)
        pairs = []
        for n in range(SLICES):
            away = 2 * (n % 4 * 4 + n // 4) + i
            pairs += [(n * SLABS + j, n * SLABS + (j - away) % SLABS) for j in range(SLABS)]
        shares.append(lax.ppermute(window, ("tm", "space"), pairs))
    gathered = jnp.stack(shares)
    for unit in (4, 1):
        count = gathered.shape[0]
        parts = [gathered]
        for k in (1, 2, 3):
            pairs = [(n - n // unit % 4 * unit + (n // unit + k) % 4 * unit, n) for n in range(SLICES)]
            parts.append(lax.ppermute(gathered, "tm", pairs))
        first = (4 - slice_index // unit % 4) % 4
        gathered = lax.dynamic_slice_in_dim(jnp.concatenate(parts + parts[:3]), first * count, 4 * count)
    turned = lax.dynamic_slice_in_dim(
        jnp.concatenate([gathered, gathered]), (SLABS - slab) % SLABS, SLABS, axis=0
    )
    row_cond = jnp.transpose(turned, (1, 0, 2))

    around = (share, cond, wide_source, coarse_start, plane_keep, plane_spread)
    across, along = across_chips(start_rows), in_chip(start_rows)
    sent, = step_call(
        first_step_kernel, [(slab_rows + PLANE, 128)], place, across, along, start_rows, *around
    )
    across, along = across_chips(sent), in_chip(sent)
    field_now, term, direct = step_call(
        second_step_kernel, [(slab_rows, 128), (PLANE, 128), (PLANE, 128)], place, across, along, sent, *around
    )
    field_now = field_now.reshape(start_field.shape)

    rows = to_rows(windows(term, 1))
    later = [(i, i) for i in range(SLABS)]
    links = {k: from_later(rows[4 - k : 8 + k], k, later) for k in (1, 2, 3, 4)}
    row_place = (slab - 2) * BLOCK + lax.broadcasted_iota(jnp.int32, row_cond.shape, 0)
    within = (row_place >= 0) & (row_place < PLANE)
    row_spread = jnp.where(within, 1.0 / (row_cond + 1.5), 0.0)
    row_keep = row_cond * row_spread
    row_spread = 0.25 * row_spread

    inner = slice(BLOCK, 4 * BLOCK)
    total = chain_call(
        first_links_kernel, 12, *(links[k] for k in (4, 3, 2, 1)), row_keep[inner], row_spread[inner]
    )

    centre = from_later(total, 4, later)
    before, after = beside_later(total, 4, 1, slab)
    window = jnp.concatenate([before, centre, after])
    total = chain_call(
        lambda *refs: power_kernel(4, *refs), 12, window, total, row_keep[inner], row_spread[inner]
    )

    centre = from_later(total, 8, later)
    near = from_later(total, 8, facing(1, 1))
    outward = [(j - 2, j) for j in range(2, SLABS, 2)] + [(j + 2, j) for j in range(1, SLABS - 2, 2)]
    far = from_later(total, 8, outward)
    swapped = lax.ppermute(jnp.stack([centre, near]), "space", facing(1, 0))
    window = jnp.where(
        odd,
        jnp.concatenate([swapped[1], swapped[0], centre, near, far]),
        jnp.concatenate([far, near, centre, swapped[0], swapped[1]]),
    )
    total = chain_call(lambda *refs: power_kernel(8, *refs), 20, window, total, row_keep, row_spread)

    back = lax.all_to_all(jnp.transpose(total, (1, 0, 2)), "space", 0, 0)
    propagated = jnp.where(is_final, direct, back.reshape(PLANE, 128))
    return prolong_add(propagated - direct, field_now)[None]


def solution(mesh):
    in_specs = (P("tm", "space", None, None), P("space", None, None), P("tm", None), P("tm", None))
    out_specs = P("tm", "space", None, None)
    return jax.shard_map(
        per_device, mesh=mesh, in_specs=in_specs, out_specs=out_specs, check_vma=False
    )
```

```python
import jax
import jax.numpy as jnp
from jax import lax
from jax.experimental import pallas as pl
from jax.experimental.pallas import tpu as pltpu
from jax.sharding import PartitionSpec as P

FINE_STEPS = 2
SWEEPS = 2
SLABS = 32
SLICES = 16
PLANE = 128
BLOCK = 4
EXACT = lax.Precision.HIGHEST


def params():
    return pltpu.CompilerParams(vmem_limit_bytes=16 * 1024 * 1024)


def halving(half):
    row = lax.broadcasted_iota(jnp.int32, (128, 128), 0)
    lane = lax.broadcasted_iota(jnp.int32, (128, 128), 1)
    return jnp.where(lane == row // 2 + 64 * half, 0.125, 0.0).astype(jnp.float32)


def restricted(ref, rows):
    total = jnp.zeros((PLANE, 128), jnp.float32)
    for half in range(2):
        parts = [ref[pl.ds(p * rows + 2 * half + r, PLANE, stride=4), :] for p in range(2) for r in range(2)]
        summed = (parts[0] + parts[1]) + (parts[2] + parts[3])
        total = total + jnp.dot(summed, halving(half), precision=EXACT, preferred_element_type=jnp.float32)
    return total


def restrict_kernel(field_ref, out_ref):
    out_ref[...] = restricted(field_ref, field_ref.shape[0] // 2)


def restrict(field):
    return pl.pallas_call(
        restrict_kernel,
        out_shape=jax.ShapeDtypeStruct((PLANE, 128), jnp.float32),
        compiler_params=params(),
    )(field.reshape(-1, 128))


def prolong_add_kernel(delta_ref, field_ref, out_ref):
    row = lax.broadcasted_iota(jnp.int32, (128, 128), 0)
    lane = lax.broadcasted_iota(jnp.int32, (128, 128), 1)
    delta = delta_ref[...]
    for half in range(2):
        spread = jnp.where(row == lane // 2 + 64 * half, 1.0, 0.0).astype(jnp.float32)
        wide = jnp.dot(delta, spread, precision=EXACT, preferred_element_type=jnp.float32)
        for plane in range(2):
            for r in range(2):
                rows = pl.ds(2 * half + r, PLANE, stride=4)
                out_ref[plane, rows, :] = field_ref[plane, rows, :] + wide


def prolong_add(delta, field):
    return pl.pallas_call(
        prolong_add_kernel,
        out_shape=jax.ShapeDtypeStruct(field.shape, jnp.float32),
        compiler_params=params(),
    )(delta, field)


def lanes_of(shape):
    lane = lax.broadcasted_iota(jnp.int32, shape, len(shape) - 1)
    return lane < 64, lane % 64


def beside_z(value, z):
    before = jnp.where(z == 0, 0.0, pltpu.roll(value, 1, 1))
    after = jnp.where(z == 63, 0.0, pltpu.roll(value, 127, 1))
    return before + after


def beside_in_plane(value):
    rows = value.shape[0]
    row = lax.broadcasted_iota(jnp.int32, value.shape, 0)
    lane = lax.broadcasted_iota(jnp.int32, value.shape, 1)
    above = jnp.where(row == 0, 0.0, pltpu.roll(value, 1, 0))
    below = jnp.where(row == rows - 1, 0.0, pltpu.roll(value, rows - 1, 0))
    before = jnp.where(lane == 0, 0.0, pltpu.roll(value, 1, 1))
    after = jnp.where(lane == 127, 0.0, pltpu.roll(value, 127, 1))
    return above + below + before + after


def two_sweeps(place_ref, across_ref, along_ref, field_ref, share_ref, cond_ref, source_ref):
    odd = place_ref[0] == 1
    rows = cond_ref.shape[1]

    def plane(ref, p):
        return ref[p * rows : (p + 1) * rows, :]

    planes = [jnp.where(odd, plane(along_ref, p), plane(across_ref, p)) for p in range(2)]
    planes += [plane(field_ref, p) for p in range(2)]
    planes += [jnp.where(odd, plane(across_ref, p), plane(along_ref, p)) for p in range(2)]
    conds = [share_ref[0], cond_ref[0], cond_ref[1], share_ref[1]]
    terms, diagonals, wide = [], [], []
    for i in range(4):
        value = planes[i + 1]
        terms.append(conds[i] * value + source_ref[i])
        diagonals.append(conds[i] + 6.0)
        total = planes[i] + planes[i + 2] + beside_in_plane(value)
        wide.append((terms[i] + total) / diagonals[i])
    wide[0] = jnp.where(place_ref[1] == 1, wide[0], 0.0)
    wide[3] = jnp.where(place_ref[2] == 1, wide[3], 0.0)
    swept = []
    for p in range(2):
        total = wide[p] + wide[p + 2] + beside_in_plane(wide[p + 1])
        swept.append((terms[p + 1] + total) / diagonals[p + 1])
    return swept


def plane_sweep(value, start, beside, keep, spread):
    low, z = lanes_of(value.shape)
    row = lax.broadcasted_iota(jnp.int32, value.shape, 0)
    swapped = pltpu.roll(value, 64, 1)
    earlier = jnp.where(row == 0, 0.0, pltpu.roll(swapped, 1, 0))
    later = jnp.where(row == PLANE - 1, 0.0, pltpu.roll(swapped, PLANE - 1, 0))
    total = beside + swapped + jnp.where(low, earlier, later) + beside_z(value, z)
    return keep * start + spread * total


def first_step_kernel(*refs):
    start_ref, keep_ref, spread_ref, out_ref = refs[7:]
    across_ref, along_ref, cond_ref = refs[1], refs[2], refs[5]
    rows = cond_ref.shape[1]
    for p, value in enumerate(two_sweeps(*refs[:7])):
        out_ref[p * rows : (p + 1) * rows, :] = value
    beside = restricted(across_ref, rows) + restricted(along_ref, rows)
    start = start_ref[...]
    out_ref[2 * rows :, :] = plane_sweep(start, start, beside, keep_ref[...], spread_ref[...])


def second_step_kernel(*refs):
    start_ref, keep_ref, spread_ref, field_ref, term_ref, direct_ref = refs[7:]
    place_ref, across_ref, along_ref, sent_ref, cond_ref = refs[0], refs[1], refs[2], refs[3], refs[5]
    rows = cond_ref.shape[1]
    for p, value in enumerate(two_sweeps(*refs[:7])):
        field_ref[p * rows : (p + 1) * rows, :] = value
    tail = slice(2 * rows, 2 * rows + PLANE)
    beside = across_ref[tail, :] + along_ref[tail, :]
    direct = plane_sweep(sent_ref[tail, :], start_ref[...], beside, keep_ref[...], spread_ref[...])
    direct_ref[...] = direct
    term_ref[...] = restricted(field_ref, rows) - jnp.where(place_ref[3] == 1, 0.0, direct)


def step_call(kernel, shapes, place, *operands):
    in_vmem = pl.BlockSpec(memory_space=pltpu.VMEM)
    return pl.pallas_call(
        kernel,
        out_shape=[jax.ShapeDtypeStruct(shape, jnp.float32) for shape in shapes],
        in_specs=[pl.BlockSpec(memory_space=pltpu.SMEM)] + [in_vmem] * len(operands),
        out_specs=[in_vmem] * len(shapes),
        compiler_params=params(),
    )(place, *operands)


def sweep_rows(source, start, keep, spread, target, first, last, low_end, high_end):
    shape = (SLABS, 128)
    low, z = lanes_of(shape)
    x = lax.broadcasted_iota(jnp.int32, shape, 0)
    zero = jnp.zeros(shape, jnp.float32)

    def swapped(q):
        return pltpu.roll(source[q], 64, 1) if low_end <= q < high_end else zero

    earlier, here = swapped(first - 1), swapped(first)
    for q in range(first, last):
        later = swapped(q + 1)
        value = source[q]
        total = here + jnp.where(low, earlier, later) + beside_z(value, z)
        total = total + jnp.where(x == 0, 0.0, pltpu.roll(value, 1, 0))
        total = total + jnp.where(x == SLABS - 1, 0.0, pltpu.roll(value, SLABS - 1, 0))
        target[q] = keep[q] * start[q] + spread[q] * total
        earlier, here = here, later


def coarse_step(fields, keep, spread, at, low_end, high_end):
    start, middle, result = fields.at[at], fields.at[2], fields.at[1 - at]
    sweep_rows(start, start, keep, spread, middle, low_end, high_end, low_end, high_end)
    sweep_rows(middle, start, keep, spread, result, low_end + 1, high_end - 1, low_end, high_end)
    return 1 - at


def first_links_kernel(c4_ref, c3_ref, c2_ref, c1_ref, keep_ref, spread_ref, out_ref, fields):
    rows = c4_ref.shape[0]
    fields[0] = c4_ref[...]
    at, low_end, high_end = 0, 0, rows
    for added in (c3_ref, c2_ref, c1_ref, None):
        at = coarse_step(fields, keep_ref, spread_ref, at, low_end, high_end)
        low_end, high_end = low_end + 1, high_end - 1
        if added is not None:
            for q in range(low_end, high_end):
                fields[at, q] = fields[at, q] + added[q - low_end]
    out_ref[...] = fields[at, low_end:high_end]


def power_kernel(links, window_ref, base_ref, keep_ref, spread_ref, out_ref, fields):
    rows = window_ref.shape[0]
    fields[0] = window_ref[...]
    at = 0
    for link in range(links):
        at = coarse_step(fields, keep_ref, spread_ref, at, link, rows - link)
    out_ref[...] = base_ref[...] + fields[at, links : rows - links]


def chain_call(kernel, rows, *operands):
    return pl.pallas_call(
        kernel,
        out_shape=jax.ShapeDtypeStruct((BLOCK, SLABS, 128), jnp.float32),
        scratch_shapes=[pltpu.VMEM((3, rows, SLABS, 128), jnp.float32)],
        compiler_params=params(),
    )(*operands)


def facing(distance, late):
    pairs = []
    for i in range(SLABS - distance):
        if (i // distance) % 2 == late:
            pairs += [(i, i + distance), (i + distance, i)]
    return pairs


def from_later(value, links, pairs):
    both = [((n + links) * SLABS + i, n * SLABS + j) for n in range(SLICES - links) for i, j in pairs]
    return lax.ppermute(value, ("tm", "space"), both)


def beside_later(value, links, distance, slab):
    one = from_later(value, links, facing(distance, 0))
    other = from_later(value, links, facing(distance, 1))
    upper = (slab // distance) % 2 == 1
    return jnp.where(upper, one, other), jnp.where(upper, other, one)


def windows(plane, reach):
    blocks = plane.reshape(SLABS, BLOCK, 128)
    padded = jnp.pad(blocks, ((reach, reach), (0, 0), (0, 0)))
    return jnp.concatenate([padded[i : i + SLABS] for i in range(2 * reach + 1)], axis=1)


def to_rows(parts):
    arrived = lax.all_to_all(parts, "space", 0, 0)
    return jnp.transpose(arrived, (1, 0, 2))


def per_device(end_state, cond, receivers, residuals):
    start_field = end_state[0]
    row_count, width_y, width_z = start_field.shape
    plane_size = width_y * width_z
    slab = lax.axis_index("space")
    slice_index = lax.axis_index("tm")
    odd = slab % 2 == 1
    is_final = slice_index == SLICES - 1

    def across_chips(value):
        return lax.ppermute(value, "space", facing(1, 1))

    def in_chip(value):
        return lax.ppermute(value, "space", facing(1, 0))

    def by_side(along, across):
        return jnp.where(odd, along, across), jnp.where(odd, across, along)

    ring = slice_index % 4
    quarter = width_y // 4
    share = lax.dynamic_slice_in_dim(cond, ring * quarter, quarter, axis=1)
    across = across_chips(jnp.where(odd, share[1], share[0]))
    along = in_chip(jnp.where(odd, share[0], share[1]))
    share = jnp.stack(by_side(along, across))
    for bit in (1, 2):
        upper = (ring // bit) % 2 == 1
        other = lax.ppermute(share, "tm", [(n, n ^ bit) for n in range(SLICES)])
        share = jnp.concatenate([jnp.where(upper, other, share), jnp.where(upper, share, other)], axis=1)

    local_row = receivers[0] // plane_size - slab * row_count + 1
    inside = (local_row >= 0) & (local_row < row_count + 2)
    wide_size = (row_count + 2) * plane_size
    target = jnp.where(inside, local_row * plane_size + receivers[0] % plane_size, wide_size)
    flat_source = jnp.zeros((wide_size,), jnp.float32).at[target].add(residuals[0], mode="drop")
    wide_source = flat_source.reshape(row_count + 2, width_y, width_z)
    place = jnp.stack([odd, slab > 0, slab < SLABS - 1, is_final]).astype(jnp.int32)

    coarse_cond = restrict(cond) / FINE_STEPS
    plane_spread = 1.0 / (coarse_cond + 1.5)
    plane_keep = coarse_cond * plane_spread
    plane_spread = 0.25 * plane_spread
    coarse_start = restrict(start_field)

    slab_rows = row_count * width_y
    start_rows = start_field.reshape(slab_rows, width_z)
    around = (share, cond, wide_source, coarse_start, plane_keep, plane_spread)
    across, along = across_chips(start_rows), in_chip(start_rows)
    sent, = step_call(
        first_step_kernel, [(slab_rows + PLANE, 128)], place, across, along, start_rows, *around
    )
    across, along = across_chips(sent), in_chip(sent)
    field_now, term, direct = step_call(
        second_step_kernel, [(slab_rows, 128), (PLANE, 128), (PLANE, 128)], place, across, along, sent, *around
    )
    field_now = field_now.reshape(start_field.shape)

    second_half = slice_index % 2 == 1
    cond_windows = windows(coarse_cond, 2)
    cond_windows = jnp.where(second_half, cond_windows[:, 10:], cond_windows[:, :10])
    arrived = to_rows(jnp.concatenate([windows(term, 1), cond_windows], axis=1))
    rows, own_cond = arrived[:12], arrived[12:]
    other_cond = lax.ppermute(own_cond, "tm", [(n, n ^ 1) for n in range(SLICES)])
    row_cond = jnp.concatenate(
        [jnp.where(second_half, other_cond, own_cond), jnp.where(second_half, own_cond, other_cond)]
    )
    later = [(i, i) for i in range(SLABS)]
    links = {k: from_later(rows[4 - k : 8 + k], k, later) for k in (1, 2, 3, 4)}
    row_place = (slab - 2) * BLOCK + lax.broadcasted_iota(jnp.int32, row_cond.shape, 0)
    within = (row_place >= 0) & (row_place < PLANE)
    row_spread = jnp.where(within, 1.0 / (row_cond + 1.5), 0.0)
    row_keep = row_cond * row_spread
    row_spread = 0.25 * row_spread

    inner = slice(BLOCK, 4 * BLOCK)
    total = chain_call(
        first_links_kernel, 12, *(links[k] for k in (4, 3, 2, 1)), row_keep[inner], row_spread[inner]
    )

    centre = from_later(total, 4, later)
    before, after = beside_later(total, 4, 1, slab)
    window = jnp.concatenate([before, centre, after])
    total = chain_call(
        lambda *refs: power_kernel(4, *refs), 12, window, total, row_keep[inner], row_spread[inner]
    )

    centre = from_later(total, 8, later)
    near = from_later(total, 8, facing(1, 1))
    outward = [(j - 2, j) for j in range(2, SLABS, 2)] + [(j + 2, j) for j in range(1, SLABS - 2, 2)]
    far = from_later(total, 8, outward)
    swapped = lax.ppermute(jnp.stack([centre, near]), "space", facing(1, 0))
    window = jnp.where(
        odd,
        jnp.concatenate([swapped[1], swapped[0], centre, near, far]),
        jnp.concatenate([far, near, centre, swapped[0], swapped[1]]),
    )
    total = chain_call(lambda *refs: power_kernel(8, *refs), 20, window, total, row_keep, row_spread)

    back = lax.all_to_all(jnp.transpose(total, (1, 0, 2)), "space", 0, 0)
    propagated = jnp.where(is_final, direct, back.reshape(PLANE, 128))
    return prolong_add(propagated - direct, field_now)[None]


def solution(mesh):
    in_specs = (P("tm", "space", None, None), P("space", None, None), P("tm", None), P("tm", None))
    out_specs = P("tm", "space", None, None)
    return jax.shard_map(
        per_device, mesh=mesh, in_specs=in_specs, out_specs=out_specs, check_vma=False
    )
```

```python
import jax
import jax.numpy as jnp
from jax import lax
from jax.experimental import pallas as pl
from jax.experimental.pallas import tpu as pltpu
from jax.sharding import PartitionSpec as P

FINE_STEPS = 2
SWEEPS = 2
SLABS = 32
SLICES = 16
PLANE = 128
BLOCK = 4
EXACT = lax.Precision.HIGHEST


def params():
    return pltpu.CompilerParams(vmem_limit_bytes=16 * 1024 * 1024)


def halving(half):
    row = lax.broadcasted_iota(jnp.int32, (128, 128), 0)
    lane = lax.broadcasted_iota(jnp.int32, (128, 128), 1)
    return jnp.where(lane == row // 2 + 64 * half, 0.125, 0.0).astype(jnp.float32)


def restricted(ref, rows):
    total = jnp.zeros((PLANE, 128), jnp.float32)
    for half in range(2):
        parts = [ref[pl.ds(p * rows + 2 * half + r, PLANE, stride=4), :] for p in range(2) for r in range(2)]
        summed = (parts[0] + parts[1]) + (parts[2] + parts[3])
        total = total + jnp.dot(summed, halving(half), precision=EXACT, preferred_element_type=jnp.float32)
    return total


def restrict_kernel(field_ref, out_ref):
    out_ref[...] = restricted(field_ref, field_ref.shape[0] // 2)


def restrict(field):
    return pl.pallas_call(
        restrict_kernel,
        out_shape=jax.ShapeDtypeStruct((PLANE, 128), jnp.float32),
        compiler_params=params(),
    )(field.reshape(-1, 128))


def prolong_add_kernel(delta_ref, field_ref, out_ref):
    row = lax.broadcasted_iota(jnp.int32, (128, 128), 0)
    lane = lax.broadcasted_iota(jnp.int32, (128, 128), 1)
    delta = delta_ref[...]
    for half in range(2):
        spread = jnp.where(row == lane // 2 + 64 * half, 1.0, 0.0).astype(jnp.float32)
        wide = jnp.dot(delta, spread, precision=EXACT, preferred_element_type=jnp.float32)
        for plane in range(2):
            for r in range(2):
                rows = pl.ds(2 * half + r, PLANE, stride=4)
                out_ref[plane, rows, :] = field_ref[plane, rows, :] + wide


def prolong_add(delta, field):
    return pl.pallas_call(
        prolong_add_kernel,
        out_shape=jax.ShapeDtypeStruct(field.shape, jnp.float32),
        compiler_params=params(),
    )(delta, field)


def lanes_of(shape):
    lane = lax.broadcasted_iota(jnp.int32, shape, len(shape) - 1)
    return lane < 64, lane % 64


def beside_z(value, z):
    before = jnp.where(z == 0, 0.0, pltpu.roll(value, 1, 1))
    after = jnp.where(z == 63, 0.0, pltpu.roll(value, 127, 1))
    return before + after


def beside_in_plane(value):
    rows = value.shape[0]
    row = lax.broadcasted_iota(jnp.int32, value.shape, 0)
    lane = lax.broadcasted_iota(jnp.int32, value.shape, 1)
    above = jnp.where(row == 0, 0.0, pltpu.roll(value, 1, 0))
    below = jnp.where(row == rows - 1, 0.0, pltpu.roll(value, rows - 1, 0))
    before = jnp.where(lane == 0, 0.0, pltpu.roll(value, 1, 1))
    after = jnp.where(lane == 127, 0.0, pltpu.roll(value, 127, 1))
    return above + below + before + after


def two_sweeps(place_ref, across_ref, along_ref, field_ref, share_ref, cond_ref, source_ref, inverses):
    odd = place_ref[0] == 1
    rows = cond_ref.shape[1]

    def plane(ref, p):
        return ref[p * rows : (p + 1) * rows, :]

    planes = [jnp.where(odd, plane(along_ref, p), plane(across_ref, p)) for p in range(2)]
    planes += [plane(field_ref, p) for p in range(2)]
    planes += [jnp.where(odd, plane(across_ref, p), plane(along_ref, p)) for p in range(2)]
    conds = [share_ref[0], cond_ref[0], cond_ref[1], share_ref[1]]
    terms, wide = [], []
    for i in range(4):
        value = planes[i + 1]
        terms.append(conds[i] * value + source_ref[i])
        total = planes[i] + planes[i + 2] + beside_in_plane(value)
        wide.append((terms[i] + total) * inverses[i])
    wide[0] = jnp.where(place_ref[1] == 1, wide[0], 0.0)
    wide[3] = jnp.where(place_ref[2] == 1, wide[3], 0.0)
    swept = []
    for p in range(2):
        total = wide[p] + wide[p + 2] + beside_in_plane(wide[p + 1])
        swept.append((terms[p + 1] + total) * inverses[p + 1])
    return swept


def plane_sweep(value, start, beside, keep, spread):
    low, z = lanes_of(value.shape)
    row = lax.broadcasted_iota(jnp.int32, value.shape, 0)
    swapped = pltpu.roll(value, 64, 1)
    earlier = jnp.where(row == 0, 0.0, pltpu.roll(swapped, 1, 0))
    later = jnp.where(row == PLANE - 1, 0.0, pltpu.roll(swapped, PLANE - 1, 0))
    total = beside + swapped + jnp.where(low, earlier, later) + beside_z(value, z)
    return keep * start + spread * total


def fetched_sweeps(across_from, along_from, across_ref, along_ref, arrived, place_ref, *refs):
    fetches = [
        pltpu.make_async_copy(across_from, across_ref, arrived.at[0]),
        pltpu.make_async_copy(along_from, along_ref, arrived.at[1]),
    ]
    for fetch in fetches:
        fetch.start()
    share_ref, cond_ref = refs[1], refs[2]
    inverses = [1.0 / (cond + 6.0) for cond in (share_ref[0], cond_ref[0], cond_ref[1], share_ref[1])]
    for fetch in fetches:
        fetch.wait()
    return two_sweeps(place_ref, across_ref, along_ref, *refs, inverses)


def first_step_kernel(
    place_ref, across_from, along_from, field_ref, share_ref, cond_ref, source_ref, start_ref, keep_ref, spread_ref,
    sent_ref, across_ref, along_ref, arrived
):
    rows = cond_ref.shape[1]
    traded = (across_from, along_from, across_ref, along_ref, arrived)
    for p, value in enumerate(fetched_sweeps(*traded, place_ref, field_ref, share_ref, cond_ref, source_ref)):
        sent_ref[p * rows : (p + 1) * rows, :] = value
    beside = restricted(across_ref, rows) + restricted(along_ref, rows)
    start = start_ref[...]
    sent_ref[2 * rows :, :] = plane_sweep(start, start, beside, keep_ref[...], spread_ref[...])


def second_step_kernel(
    place_ref, across_from, along_from, sent_ref, share_ref, cond_ref, source_ref, start_ref, keep_ref, spread_ref,
    field_ref, term_ref, direct_ref, across_ref, along_ref, arrived
):
    rows = cond_ref.shape[1]
    traded = (across_from, along_from, across_ref, along_ref, arrived)
    for p, value in enumerate(fetched_sweeps(*traded, place_ref, sent_ref, share_ref, cond_ref, source_ref)):
        field_ref[p * rows : (p + 1) * rows, :] = value
    tail = slice(2 * rows, 2 * rows + PLANE)
    beside = across_ref[tail, :] + along_ref[tail, :]
    direct = plane_sweep(sent_ref[tail, :], start_ref[...], beside, keep_ref[...], spread_ref[...])
    direct_ref[...] = direct
    term_ref[...] = restricted(field_ref, rows) - jnp.where(place_ref[3] == 1, 0.0, direct)


def step_call(kernel, shapes, place, traded, *operands):
    in_vmem = pl.BlockSpec(memory_space=pltpu.VMEM)
    in_hbm = pl.BlockSpec(memory_space=pltpu.HBM)
    scratch = [pltpu.VMEM(value.shape, jnp.float32) for value in traded]
    return pl.pallas_call(
        kernel,
        out_shape=[jax.ShapeDtypeStruct(shape, jnp.float32) for shape in shapes],
        in_specs=[pl.BlockSpec(memory_space=pltpu.SMEM)] + [in_hbm] * len(traded) + [in_vmem] * len(operands),
        out_specs=[in_vmem] * len(shapes),
        scratch_shapes=scratch + [pltpu.SemaphoreType.DMA((len(traded),))],
        compiler_params=params(),
    )(place, *traded, *operands)


def sweep_rows(source, start, keep, spread, target, first, last, low_end, high_end):
    shape = (SLABS, 128)
    low, z = lanes_of(shape)
    x = lax.broadcasted_iota(jnp.int32, shape, 0)
    zero = jnp.zeros(shape, jnp.float32)

    def swapped(q):
        return pltpu.roll(source[q], 64, 1) if low_end <= q < high_end else zero

    earlier, here = swapped(first - 1), swapped(first)
    for q in range(first, last):
        later = swapped(q + 1)
        value = source[q]
        total = here + jnp.where(low, earlier, later) + beside_z(value, z)
        total = total + jnp.where(x == 0, 0.0, pltpu.roll(value, 1, 0))
        total = total + jnp.where(x == SLABS - 1, 0.0, pltpu.roll(value, SLABS - 1, 0))
        target[q] = keep[q] * start[q] + spread[q] * total
        earlier, here = here, later


def coarse_step(fields, keep, spread, at, low_end, high_end):
    start, middle, result = fields.at[at], fields.at[2], fields.at[1 - at]
    sweep_rows(start, start, keep, spread, middle, low_end, high_end, low_end, high_end)
    sweep_rows(middle, start, keep, spread, result, low_end + 1, high_end - 1, low_end, high_end)
    return 1 - at


def first_links_kernel(c4_ref, c3_ref, c2_ref, c1_ref, keep_ref, spread_ref, out_ref, fields):
    rows = c4_ref.shape[0]
    fields[0] = c4_ref[...]
    at, low_end, high_end = 0, 0, rows
    for added in (c3_ref, c2_ref, c1_ref, None):
        at = coarse_step(fields, keep_ref, spread_ref, at, low_end, high_end)
        low_end, high_end = low_end + 1, high_end - 1
        if added is not None:
            for q in range(low_end, high_end):
                fields[at, q] = fields[at, q] + added[q - low_end]
    out_ref[...] = fields[at, low_end:high_end]


def power_kernel(links, window_ref, base_ref, keep_ref, spread_ref, out_ref, fields):
    rows = window_ref.shape[0]
    fields[0] = window_ref[...]
    at = 0
    for link in range(links):
        at = coarse_step(fields, keep_ref, spread_ref, at, link, rows - link)
    out_ref[...] = base_ref[...] + fields[at, links : rows - links]


def chain_call(kernel, rows, *operands):
    return pl.pallas_call(
        kernel,
        out_shape=jax.ShapeDtypeStruct((BLOCK, SLABS, 128), jnp.float32),
        scratch_shapes=[pltpu.VMEM((3, rows, SLABS, 128), jnp.float32)],
        compiler_params=params(),
    )(*operands)


def facing(distance, late):
    pairs = []
    for i in range(SLABS - distance):
        if (i // distance) % 2 == late:
            pairs += [(i, i + distance), (i + distance, i)]
    return pairs


def from_later(value, links, pairs):
    both = [((n + links) * SLABS + i, n * SLABS + j) for n in range(SLICES - links) for i, j in pairs]
    return lax.ppermute(value, ("tm", "space"), both)


def beside_later(value, links, distance, slab):
    one = from_later(value, links, facing(distance, 0))
    other = from_later(value, links, facing(distance, 1))
    upper = (slab // distance) % 2 == 1
    return jnp.where(upper, one, other), jnp.where(upper, other, one)


def windows(plane, reach):
    blocks = plane.reshape(SLABS, BLOCK, 128)
    padded = jnp.pad(blocks, ((reach, reach), (0, 0), (0, 0)))
    return jnp.concatenate([padded[i : i + SLABS] for i in range(2 * reach + 1)], axis=1)


def to_rows(parts):
    arrived = lax.all_to_all(parts, "space", 0, 0)
    return jnp.transpose(arrived, (1, 0, 2))


def per_device(end_state, cond, receivers, residuals):
    start_field = end_state[0]
    row_count, width_y, width_z = start_field.shape
    plane_size = width_y * width_z
    slab = lax.axis_index("space")
    slice_index = lax.axis_index("tm")
    odd = slab % 2 == 1
    is_final = slice_index == SLICES - 1

    def across_chips(value):
        return lax.ppermute(value, "space", facing(1, 1))

    def in_chip(value):
        return lax.ppermute(value, "space", facing(1, 0))

    def by_side(along, across):
        return jnp.where(odd, along, across), jnp.where(odd, across, along)

    ring = slice_index % 4
    quarter = width_y // 4
    share = lax.dynamic_slice_in_dim(cond, ring * quarter, quarter, axis=1)
    across = across_chips(jnp.where(odd, share[1], share[0]))
    along = in_chip(jnp.where(odd, share[0], share[1]))
    share = jnp.stack(by_side(along, across))
    for bit in (1, 2):
        upper = (ring // bit) % 2 == 1
        other = lax.ppermute(share, "tm", [(n, n ^ bit) for n in range(SLICES)])
        share = jnp.concatenate([jnp.where(upper, other, share), jnp.where(upper, share, other)], axis=1)

    local_row = receivers[0] // plane_size - slab * row_count + 1
    inside = (local_row >= 0) & (local_row < row_count + 2)
    wide_size = (row_count + 2) * plane_size
    target = jnp.where(inside, local_row * plane_size + receivers[0] % plane_size, wide_size)
    flat_source = jnp.zeros((wide_size,), jnp.float32).at[target].add(residuals[0], mode="drop")
    wide_source = flat_source.reshape(row_count + 2, width_y, width_z)
    place = jnp.stack([odd, slab > 0, slab < SLABS - 1, is_final]).astype(jnp.int32)

    coarse_cond = restrict(cond) / FINE_STEPS
    plane_spread = 1.0 / (coarse_cond + 1.5)
    plane_keep = coarse_cond * plane_spread
    plane_spread = 0.25 * plane_spread
    coarse_start = restrict(start_field)

    slab_rows = row_count * width_y
    start_rows = start_field.reshape(slab_rows, width_z)
    around = (share, cond, wide_source, coarse_start, plane_keep, plane_spread)
    across, along = across_chips(start_rows), in_chip(start_rows)
    sent, = step_call(first_step_kernel, [(slab_rows + PLANE, 128)], place, (across, along), start_rows, *around)
    across, along = across_chips(sent), in_chip(sent)
    shapes = [(slab_rows, 128), (PLANE, 128), (PLANE, 128)]
    field_now, term, direct = step_call(second_step_kernel, shapes, place, (across, along), sent, *around)
    field_now = field_now.reshape(start_field.shape)

    second_half = slice_index % 2 == 1
    cond_windows = windows(coarse_cond, 2)
    cond_windows = jnp.where(second_half, cond_windows[:, 10:], cond_windows[:, :10])
    arrived = to_rows(jnp.concatenate([windows(term, 1), cond_windows], axis=1))
    rows, own_cond = arrived[:12], arrived[12:]
    other_cond = lax.ppermute(own_cond, "tm", [(n, n ^ 1) for n in range(SLICES)])
    row_cond = jnp.concatenate(
        [jnp.where(second_half, other_cond, own_cond), jnp.where(second_half, own_cond, other_cond)]
    )
    later = [(i, i) for i in range(SLABS)]
    links = {k: from_later(rows[4 - k : 8 + k], k, later) for k in (1, 2, 3, 4)}
    row_place = (slab - 2) * BLOCK + lax.broadcasted_iota(jnp.int32, row_cond.shape, 0)
    within = (row_place >= 0) & (row_place < PLANE)
    row_spread = jnp.where(within, 1.0 / (row_cond + 1.5), 0.0)
    row_keep = row_cond * row_spread
    row_spread = 0.25 * row_spread

    inner = slice(BLOCK, 4 * BLOCK)
    total = chain_call(
        first_links_kernel, 12, *(links[k] for k in (4, 3, 2, 1)), row_keep[inner], row_spread[inner]
    )

    centre = from_later(total, 4, later)
    before, after = beside_later(total, 4, 1, slab)
    window = jnp.concatenate([before, centre, after])
    total = chain_call(
        lambda *refs: power_kernel(4, *refs), 12, window, total, row_keep[inner], row_spread[inner]
    )

    centre = from_later(total, 8, later)
    near = from_later(total, 8, facing(1, 1))
    outward = [(j - 2, j) for j in range(2, SLABS, 2)] + [(j + 2, j) for j in range(1, SLABS - 2, 2)]
    far = from_later(total, 8, outward)
    swapped = lax.ppermute(jnp.stack([centre, near]), "space", facing(1, 0))
    window = jnp.where(
        odd,
        jnp.concatenate([swapped[1], swapped[0], centre, near, far]),
        jnp.concatenate([far, near, centre, swapped[0], swapped[1]]),
    )
    total = chain_call(lambda *refs: power_kernel(8, *refs), 20, window, total, row_keep, row_spread)

    back = lax.all_to_all(jnp.transpose(total, (1, 0, 2)), "space", 0, 0)
    propagated = jnp.where(is_final, direct, back.reshape(PLANE, 128))
    return prolong_add(propagated - direct, field_now)[None]


def solution(mesh):
    in_specs = (P("tm", "space", None, None), P("space", None, None), P("tm", None), P("tm", None))
    out_specs = P("tm", "space", None, None)
    return jax.shard_map(
        per_device, mesh=mesh, in_specs=in_specs, out_specs=out_specs, check_vma=False
    )
```

```python
import jax
import jax.numpy as jnp
from jax import lax
from jax.experimental import pallas as pl
from jax.experimental.pallas import tpu as pltpu
from jax.sharding import PartitionSpec as P

FINE_STEPS = 2
SWEEPS = 2
SLABS = 32
SLICES = 16
PLANE = 128
BLOCK = 4
EXACT = lax.Precision.HIGHEST


def params():
    return pltpu.CompilerParams(vmem_limit_bytes=16 * 1024 * 1024)


def halving(half):
    row = lax.broadcasted_iota(jnp.int32, (128, 128), 0)
    lane = lax.broadcasted_iota(jnp.int32, (128, 128), 1)
    return jnp.where(lane == row // 2 + 64 * half, 0.125, 0.0).astype(jnp.float32)


def restricted(ref, rows):
    total = jnp.zeros((PLANE, 128), jnp.float32)
    for half in range(2):
        parts = [ref[pl.ds(p * rows + 2 * half + r, PLANE, stride=4), :] for p in range(2) for r in range(2)]
        summed = (parts[0] + parts[1]) + (parts[2] + parts[3])
        total = total + jnp.dot(summed, halving(half), precision=EXACT, preferred_element_type=jnp.float32)
    return total


def restrict_kernel(field_ref, out_ref):
    out_ref[...] = restricted(field_ref, field_ref.shape[0] // 2)


def restrict(field):
    return pl.pallas_call(
        restrict_kernel,
        out_shape=jax.ShapeDtypeStruct((PLANE, 128), jnp.float32),
        compiler_params=params(),
    )(field.reshape(-1, 128))


def prolong_add_kernel(delta_ref, field_ref, out_ref):
    row = lax.broadcasted_iota(jnp.int32, (128, 128), 0)
    lane = lax.broadcasted_iota(jnp.int32, (128, 128), 1)
    delta = delta_ref[...]
    for half in range(2):
        spread = jnp.where(row == lane // 2 + 64 * half, 1.0, 0.0).astype(jnp.float32)
        wide = jnp.dot(delta, spread, precision=EXACT, preferred_element_type=jnp.float32)
        for plane in range(2):
            for r in range(2):
                rows = pl.ds(2 * half + r, PLANE, stride=4)
                out_ref[plane, rows, :] = field_ref[plane, rows, :] + wide


def prolong_add(delta, field):
    return pl.pallas_call(
        prolong_add_kernel,
        out_shape=jax.ShapeDtypeStruct(field.shape, jnp.float32),
        compiler_params=params(),
    )(delta, field)


def lanes_of(shape):
    lane = lax.broadcasted_iota(jnp.int32, shape, len(shape) - 1)
    return lane < 64, lane % 64


def beside_z(value, z):
    before = jnp.where(z == 0, 0.0, pltpu.roll(value, 1, 1))
    after = jnp.where(z == 63, 0.0, pltpu.roll(value, 127, 1))
    return before + after


def beside_in_plane(value):
    rows = value.shape[0]
    row = lax.broadcasted_iota(jnp.int32, value.shape, 0)
    lane = lax.broadcasted_iota(jnp.int32, value.shape, 1)
    above = jnp.where(row == 0, 0.0, pltpu.roll(value, 1, 0))
    below = jnp.where(row == rows - 1, 0.0, pltpu.roll(value, rows - 1, 0))
    before = jnp.where(lane == 0, 0.0, pltpu.roll(value, 1, 1))
    after = jnp.where(lane == 127, 0.0, pltpu.roll(value, 127, 1))
    return above + below + before + after


def two_sweeps(place_ref, across_ref, along_ref, field_ref, share_ref, cond_ref, source_ref):
    odd = place_ref[0] == 1
    rows = cond_ref.shape[1]

    def plane(ref, p):
        return ref[p * rows : (p + 1) * rows, :]

    planes = [jnp.where(odd, plane(along_ref, p), plane(across_ref, p)) for p in range(2)]
    planes += [plane(field_ref, p) for p in range(2)]
    planes += [jnp.where(odd, plane(across_ref, p), plane(along_ref, p)) for p in range(2)]
    conds = [share_ref[0], cond_ref[0], cond_ref[1], share_ref[1]]
    terms, diagonals, wide = [], [], []
    for i in range(4):
        value = planes[i + 1]
        terms.append(conds[i] * value + source_ref[i])
        diagonals.append(conds[i] + 6.0)
        total = planes[i] + planes[i + 2] + beside_in_plane(value)
        wide.append((terms[i] + total) / diagonals[i])
    wide[0] = jnp.where(place_ref[1] == 1, wide[0], 0.0)
    wide[3] = jnp.where(place_ref[2] == 1, wide[3], 0.0)
    swept = []
    for p in range(2):
        total = wide[p] + wide[p + 2] + beside_in_plane(wide[p + 1])
        swept.append((terms[p + 1] + total) / diagonals[p + 1])
    return swept


def plane_sweep(value, start, beside, keep, spread):
    low, z = lanes_of(value.shape)
    row = lax.broadcasted_iota(jnp.int32, value.shape, 0)
    swapped = pltpu.roll(value, 64, 1)
    earlier = jnp.where(row == 0, 0.0, pltpu.roll(swapped, 1, 0))
    later = jnp.where(row == PLANE - 1, 0.0, pltpu.roll(swapped, PLANE - 1, 0))
    total = beside + swapped + jnp.where(low, earlier, later) + beside_z(value, z)
    return keep * start + spread * total


def first_step_kernel(*refs):
    start_ref, keep_ref, spread_ref, out_ref = refs[7:]
    across_ref, along_ref, cond_ref = refs[1], refs[2], refs[5]
    rows = cond_ref.shape[1]
    for p, value in enumerate(two_sweeps(*refs[:7])):
        out_ref[p * rows : (p + 1) * rows, :] = value
    beside = restricted(across_ref, rows) + restricted(along_ref, rows)
    start = start_ref[...]
    out_ref[2 * rows :, :] = plane_sweep(start, start, beside, keep_ref[...], spread_ref[...])


def second_step_kernel(*refs):
    start_ref, keep_ref, spread_ref, field_ref, term_ref, direct_ref = refs[7:]
    place_ref, across_ref, along_ref, sent_ref, cond_ref = refs[0], refs[1], refs[2], refs[3], refs[5]
    rows = cond_ref.shape[1]
    for p, value in enumerate(two_sweeps(*refs[:7])):
        field_ref[p * rows : (p + 1) * rows, :] = value
    tail = slice(2 * rows, 2 * rows + PLANE)
    beside = across_ref[tail, :] + along_ref[tail, :]
    direct = plane_sweep(sent_ref[tail, :], start_ref[...], beside, keep_ref[...], spread_ref[...])
    direct_ref[...] = direct
    term_ref[...] = restricted(field_ref, rows) - jnp.where(place_ref[3] == 1, 0.0, direct)


def step_call(kernel, shapes, place, *operands):
    in_vmem = pl.BlockSpec(memory_space=pltpu.VMEM)
    return pl.pallas_call(
        kernel,
        out_shape=[jax.ShapeDtypeStruct(shape, jnp.float32) for shape in shapes],
        in_specs=[pl.BlockSpec(memory_space=pltpu.SMEM)] + [in_vmem] * len(operands),
        out_specs=[in_vmem] * len(shapes),
        compiler_params=params(),
    )(place, *operands)


def sweep_rows(source, start, keep, spread, target, first, last, low_end, high_end):
    shape = (SLABS, 128)
    low, z = lanes_of(shape)
    x = lax.broadcasted_iota(jnp.int32, shape, 0)
    zero = jnp.zeros(shape, jnp.float32)

    def swapped(q):
        return pltpu.roll(source[q], 64, 1) if low_end <= q < high_end else zero

    earlier, here = swapped(first - 1), swapped(first)
    for q in range(first, last):
        later = swapped(q + 1)
        value = source[q]
        total = here + jnp.where(low, earlier, later) + beside_z(value, z)
        total = total + jnp.where(x == 0, 0.0, pltpu.roll(value, 1, 0))
        total = total + jnp.where(x == SLABS - 1, 0.0, pltpu.roll(value, SLABS - 1, 0))
        target[q] = keep[q] * start[q] + spread[q] * total
        earlier, here = here, later


def coarse_step(fields, keep, spread, at, low_end, high_end):
    start, middle, result = fields.at[at], fields.at[2], fields.at[1 - at]
    sweep_rows(start, start, keep, spread, middle, low_end, high_end, low_end, high_end)
    sweep_rows(middle, start, keep, spread, result, low_end + 1, high_end - 1, low_end, high_end)
    return 1 - at


def first_links_kernel(c4_ref, c3_ref, c2_ref, c1_ref, keep_ref, spread_ref, out_ref, fields):
    rows = c4_ref.shape[0]
    fields[0] = c4_ref[...]
    at, low_end, high_end = 0, 0, rows
    for added in (c3_ref, c2_ref, c1_ref, None):
        at = coarse_step(fields, keep_ref, spread_ref, at, low_end, high_end)
        low_end, high_end = low_end + 1, high_end - 1
        if added is not None:
            for q in range(low_end, high_end):
                fields[at, q] = fields[at, q] + added[q - low_end]
    out_ref[...] = fields[at, low_end:high_end]


def power_kernel(links, window_ref, base_ref, keep_ref, spread_ref, out_ref, fields):
    rows = window_ref.shape[0]
    fields[0] = window_ref[...]
    at = 0
    for link in range(links):
        at = coarse_step(fields, keep_ref, spread_ref, at, link, rows - link)
    out_ref[...] = base_ref[...] + fields[at, links : rows - links]


def chain_call(kernel, rows, *operands):
    return pl.pallas_call(
        kernel,
        out_shape=jax.ShapeDtypeStruct((BLOCK, SLABS, 128), jnp.float32),
        scratch_shapes=[pltpu.VMEM((3, rows, SLABS, 128), jnp.float32)],
        compiler_params=params(),
    )(*operands)


def snake(j):
    return j if j // 8 % 2 == 0 else j // 8 * 8 + 7 - j % 8


def snaked(value):
    return jnp.concatenate([jnp.flip(value[g : g + 8], 0) if g // 8 % 2 else value[g : g + 8] for g in range(0, SLABS, 8)])


def facing(distance, late):
    pairs = []
    for i in range(SLABS - distance):
        if (i // distance) % 2 == late:
            pairs += [(i, i + distance), (i + distance, i)]
    return pairs


def from_later(value, links, pairs):
    pairs = [(snake(i), snake(j)) for i, j in pairs]
    both = [((n + links) * SLABS + i, n * SLABS + j) for n in range(SLICES - links) for i, j in pairs]
    return lax.ppermute(value, ("tm", "space"), both)


def beside_later(value, links, distance, block):
    one = from_later(value, links, facing(distance, 0))
    other = from_later(value, links, facing(distance, 1))
    upper = (block // distance) % 2 == 1
    return jnp.where(upper, one, other), jnp.where(upper, other, one)


def windows(plane, reach):
    blocks = plane.reshape(SLABS, BLOCK, 128)
    padded = jnp.pad(blocks, ((reach, reach), (0, 0), (0, 0)))
    return jnp.concatenate([padded[i : i + SLABS] for i in range(2 * reach + 1)], axis=1)


def to_rows(parts):
    arrived = lax.all_to_all(parts, "space", 0, 0)
    return jnp.transpose(arrived, (1, 0, 2))


def per_device(end_state, cond, receivers, residuals):
    start_field = end_state[0]
    row_count, width_y, width_z = start_field.shape
    plane_size = width_y * width_z
    slab = lax.axis_index("space")
    slice_index = lax.axis_index("tm")
    odd = slab % 2 == 1
    is_final = slice_index == SLICES - 1

    def across_chips(value):
        return lax.ppermute(value, "space", facing(1, 1))

    def in_chip(value):
        return lax.ppermute(value, "space", facing(1, 0))

    def by_side(along, across):
        return jnp.where(odd, along, across), jnp.where(odd, across, along)

    ring = slice_index % 4
    quarter = width_y // 4
    share = lax.dynamic_slice_in_dim(cond, ring * quarter, quarter, axis=1)
    across = across_chips(jnp.where(odd, share[1], share[0]))
    along = in_chip(jnp.where(odd, share[0], share[1]))
    share = jnp.stack(by_side(along, across))
    for bit in (1, 2):
        upper = (ring // bit) % 2 == 1
        other = lax.ppermute(share, "tm", [(n, n ^ bit) for n in range(SLICES)])
        share = jnp.concatenate([jnp.where(upper, other, share), jnp.where(upper, share, other)], axis=1)

    local_row = receivers[0] // plane_size - slab * row_count + 1
    inside = (local_row >= 0) & (local_row < row_count + 2)
    wide_size = (row_count + 2) * plane_size
    target = jnp.where(inside, local_row * plane_size + receivers[0] % plane_size, wide_size)
    flat_source = jnp.zeros((wide_size,), jnp.float32).at[target].add(residuals[0], mode="drop")
    wide_source = flat_source.reshape(row_count + 2, width_y, width_z)
    place = jnp.stack([odd, slab > 0, slab < SLABS - 1, is_final]).astype(jnp.int32)

    coarse_cond = restrict(cond) / FINE_STEPS
    plane_spread = 1.0 / (coarse_cond + 1.5)
    plane_keep = coarse_cond * plane_spread
    plane_spread = 0.25 * plane_spread
    coarse_start = restrict(start_field)

    slab_rows = row_count * width_y
    start_rows = start_field.reshape(slab_rows, width_z)
    around = (share, cond, wide_source, coarse_start, plane_keep, plane_spread)
    across, along = across_chips(start_rows), in_chip(start_rows)
    sent, = step_call(
        first_step_kernel, [(slab_rows + PLANE, 128)], place, across, along, start_rows, *around
    )
    across, along = across_chips(sent), in_chip(sent)
    field_now, term, direct = step_call(
        second_step_kernel, [(slab_rows, 128), (PLANE, 128), (PLANE, 128)], place, across, along, sent, *around
    )
    field_now = field_now.reshape(start_field.shape)

    second_half = slice_index % 2 == 1
    cond_windows = windows(coarse_cond, 2)
    cond_windows = jnp.where(second_half, cond_windows[:, 10:], cond_windows[:, :10])
    arrived = to_rows(snaked(jnp.concatenate([windows(term, 1), cond_windows], axis=1)))
    rows, own_cond = arrived[:12], arrived[12:]
    other_cond = lax.ppermute(own_cond, "tm", [(n, n ^ 1) for n in range(SLICES)])
    row_cond = jnp.concatenate(
        [jnp.where(second_half, other_cond, own_cond), jnp.where(second_half, own_cond, other_cond)]
    )
    later = [(i, i) for i in range(SLABS)]
    links = {k: from_later(rows[4 - k : 8 + k], k, later) for k in (1, 2, 3, 4)}
    group = slab // 8
    block = jnp.where(group % 2 == 1, 16 * group + 7 - slab, slab)
    row_place = (block - 2) * BLOCK + lax.broadcasted_iota(jnp.int32, row_cond.shape, 0)
    within = (row_place >= 0) & (row_place < PLANE)
    row_spread = jnp.where(within, 1.0 / (row_cond + 1.5), 0.0)
    row_keep = row_cond * row_spread
    row_spread = 0.25 * row_spread

    inner = slice(BLOCK, 4 * BLOCK)
    total = chain_call(
        first_links_kernel, 12, *(links[k] for k in (4, 3, 2, 1)), row_keep[inner], row_spread[inner]
    )

    centre = from_later(total, 4, later)
    before, after = beside_later(total, 4, 1, block)
    window = jnp.concatenate([before, centre, after])
    total = chain_call(
        lambda *refs: power_kernel(4, *refs), 12, window, total, row_keep[inner], row_spread[inner]
    )

    centre = from_later(total, 8, later)
    near = from_later(total, 8, facing(1, 1))
    outward = [(j - 2, j) for j in range(2, SLABS, 2)] + [(j + 2, j) for j in range(1, SLABS - 2, 2)]
    far = from_later(total, 8, outward)
    swapped = from_later(jnp.stack([centre, near]), 0, facing(1, 0))
    window = jnp.where(
        block % 2 == 1,
        jnp.concatenate([swapped[1], swapped[0], centre, near, far]),
        jnp.concatenate([far, near, centre, swapped[0], swapped[1]]),
    )
    total = chain_call(lambda *refs: power_kernel(8, *refs), 20, window, total, row_keep, row_spread)

    back = lax.all_to_all(jnp.transpose(total, (1, 0, 2)), "space", 0, 0)
    propagated = jnp.where(is_final, direct, snaked(back).reshape(PLANE, 128))
    return prolong_add(propagated - direct, field_now)[None]


def solution(mesh):
    in_specs = (P("tm", "space", None, None), P("space", None, None), P("tm", None), P("tm", None))
    out_specs = P("tm", "space", None, None)
    return jax.shard_map(
        per_device, mesh=mesh, in_specs=in_specs, out_specs=out_specs, check_vma=False
    )
```

```python
import jax
import jax.numpy as jnp
from jax import lax
from jax.experimental import pallas as pl
from jax.experimental.pallas import tpu as pltpu
from jax.sharding import PartitionSpec as P

FINE_STEPS = 2
SWEEPS = 2
SLABS = 32
SLICES = 16
PLANE = 128
BLOCK = 4
EXACT = lax.Precision.HIGHEST


def params():
    return pltpu.CompilerParams(vmem_limit_bytes=16 * 1024 * 1024)


def halving(half):
    row = lax.broadcasted_iota(jnp.int32, (128, 128), 0)
    lane = lax.broadcasted_iota(jnp.int32, (128, 128), 1)
    return jnp.where(lane == row // 2 + 64 * half, 0.125, 0.0).astype(jnp.float32)


def restricted(ref, rows):
    total = jnp.zeros((PLANE, 128), jnp.float32)
    for half in range(2):
        parts = [ref[pl.ds(p * rows + 2 * half + r, PLANE, stride=4), :] for p in range(2) for r in range(2)]
        summed = (parts[0] + parts[1]) + (parts[2] + parts[3])
        total = total + jnp.dot(summed, halving(half), precision=EXACT, preferred_element_type=jnp.float32)
    return total


def restrict_kernel(field_ref, out_ref):
    out_ref[...] = restricted(field_ref, field_ref.shape[0] // 2)


def restrict(field):
    return pl.pallas_call(
        restrict_kernel,
        out_shape=jax.ShapeDtypeStruct((PLANE, 128), jnp.float32),
        compiler_params=params(),
    )(field.reshape(-1, 128))


def prolong_add_kernel(delta_ref, field_ref, out_ref):
    row = lax.broadcasted_iota(jnp.int32, (128, 128), 0)
    lane = lax.broadcasted_iota(jnp.int32, (128, 128), 1)
    delta = delta_ref[...]
    for half in range(2):
        spread = jnp.where(row == lane // 2 + 64 * half, 1.0, 0.0).astype(jnp.float32)
        wide = jnp.dot(delta, spread, precision=EXACT, preferred_element_type=jnp.float32)
        for plane in range(2):
            for r in range(2):
                rows = pl.ds(2 * half + r, PLANE, stride=4)
                out_ref[plane, rows, :] = field_ref[plane, rows, :] + wide


def prolong_add(delta, field):
    return pl.pallas_call(
        prolong_add_kernel,
        out_shape=jax.ShapeDtypeStruct(field.shape, jnp.float32),
        compiler_params=params(),
    )(delta, field)


def lanes_of(shape):
    lane = lax.broadcasted_iota(jnp.int32, shape, len(shape) - 1)
    return lane < 64, lane % 64


def beside_z(value, z):
    before = jnp.where(z == 0, 0.0, pltpu.roll(value, 1, 1))
    after = jnp.where(z == 63, 0.0, pltpu.roll(value, 127, 1))
    return before + after


def beside_in_plane(value):
    rows = value.shape[0]
    row = lax.broadcasted_iota(jnp.int32, value.shape, 0)
    lane = lax.broadcasted_iota(jnp.int32, value.shape, 1)
    above = jnp.where(row == 0, 0.0, pltpu.roll(value, 1, 0))
    below = jnp.where(row == rows - 1, 0.0, pltpu.roll(value, rows - 1, 0))
    before = jnp.where(lane == 0, 0.0, pltpu.roll(value, 1, 1))
    after = jnp.where(lane == 127, 0.0, pltpu.roll(value, 127, 1))
    return above + below + before + after


def two_sweeps(place_ref, across_ref, along_ref, field_ref, share_ref, cond_ref, source_ref):
    odd = place_ref[0] == 1
    rows = cond_ref.shape[1]

    def plane(ref, p):
        return ref[p * rows : (p + 1) * rows, :]

    planes = [jnp.where(odd, plane(along_ref, p), plane(across_ref, p)) for p in range(2)]
    planes += [plane(field_ref, p) for p in range(2)]
    planes += [jnp.where(odd, plane(across_ref, p), plane(along_ref, p)) for p in range(2)]
    conds = [share_ref[0], cond_ref[0], cond_ref[1], share_ref[1]]
    terms, diagonals, wide = [], [], []
    for i in range(4):
        value = planes[i + 1]
        terms.append(conds[i] * value + source_ref[i])
        diagonals.append(conds[i] + 6.0)
        total = planes[i] + planes[i + 2] + beside_in_plane(value)
        wide.append((terms[i] + total) / diagonals[i])
    wide[0] = jnp.where(place_ref[1] == 1, wide[0], 0.0)
    wide[3] = jnp.where(place_ref[2] == 1, wide[3], 0.0)
    swept = []
    for p in range(2):
        total = wide[p] + wide[p + 2] + beside_in_plane(wide[p + 1])
        swept.append((terms[p + 1] + total) / diagonals[p + 1])
    return swept


def plane_sweep(value, start, beside, keep, spread):
    low, z = lanes_of(value.shape)
    row = lax.broadcasted_iota(jnp.int32, value.shape, 0)
    swapped = pltpu.roll(value, 64, 1)
    earlier = jnp.where(row == 0, 0.0, pltpu.roll(swapped, 1, 0))
    later = jnp.where(row == PLANE - 1, 0.0, pltpu.roll(swapped, PLANE - 1, 0))
    total = beside + swapped + jnp.where(low, earlier, later) + beside_z(value, z)
    return keep * start + spread * total


def first_step_kernel(*refs):
    start_ref, keep_ref, spread_ref, out_ref = refs[7:]
    across_ref, along_ref, cond_ref = refs[1], refs[2], refs[5]
    rows = cond_ref.shape[1]
    for p, value in enumerate(two_sweeps(*refs[:7])):
        out_ref[p * rows : (p + 1) * rows, :] = value
    beside = restricted(across_ref, rows) + restricted(along_ref, rows)
    start = start_ref[...]
    out_ref[2 * rows :, :] = plane_sweep(start, start, beside, keep_ref[...], spread_ref[...])


def second_step_kernel(*refs):
    start_ref, keep_ref, spread_ref, field_ref, term_ref, direct_ref = refs[7:]
    place_ref, across_ref, along_ref, sent_ref, cond_ref = refs[0], refs[1], refs[2], refs[3], refs[5]
    rows = cond_ref.shape[1]
    for p, value in enumerate(two_sweeps(*refs[:7])):
        field_ref[p * rows : (p + 1) * rows, :] = value
    tail = slice(2 * rows, 2 * rows + PLANE)
    beside = across_ref[tail, :] + along_ref[tail, :]
    direct = plane_sweep(sent_ref[tail, :], start_ref[...], beside, keep_ref[...], spread_ref[...])
    direct_ref[...] = direct
    term_ref[...] = restricted(field_ref, rows) - jnp.where(place_ref[3] == 1, 0.0, direct)


def step_call(kernel, shapes, place, *operands):
    in_vmem = pl.BlockSpec(memory_space=pltpu.VMEM)
    return pl.pallas_call(
        kernel,
        out_shape=[jax.ShapeDtypeStruct(shape, jnp.float32) for shape in shapes],
        in_specs=[pl.BlockSpec(memory_space=pltpu.SMEM)] + [in_vmem] * len(operands),
        out_specs=[in_vmem] * len(shapes),
        compiler_params=params(),
    )(place, *operands)


def sweep_rows(source, start, keep, spread, target, first, last, low_end, high_end):
    shape = (SLABS, 128)
    low, z = lanes_of(shape)
    x = lax.broadcasted_iota(jnp.int32, shape, 0)
    zero = jnp.zeros(shape, jnp.float32)

    def swapped(q):
        return pltpu.roll(source[q], 64, 1) if low_end <= q < high_end else zero

    earlier, here = swapped(first - 1), swapped(first)
    for q in range(first, last):
        later = swapped(q + 1)
        value = source[q]
        total = here + jnp.where(low, earlier, later) + beside_z(value, z)
        total = total + jnp.where(x == 0, 0.0, pltpu.roll(value, 1, 0))
        total = total + jnp.where(x == SLABS - 1, 0.0, pltpu.roll(value, SLABS - 1, 0))
        target[q] = keep[q] * start[q] + spread[q] * total
        earlier, here = here, later


def coarse_step(fields, keep, spread, at, low_end, high_end):
    start, middle, result = fields.at[at], fields.at[2], fields.at[1 - at]
    sweep_rows(start, start, keep, spread, middle, low_end, high_end, low_end, high_end)
    sweep_rows(middle, start, keep, spread, result, low_end + 1, high_end - 1, low_end, high_end)
    return 1 - at


def first_links_kernel(c4_ref, c3_ref, c2_ref, c1_ref, keep_ref, spread_ref, out_ref, fields):
    rows = c4_ref.shape[0]
    fields[0] = c4_ref[...]
    at, low_end, high_end = 0, 0, rows
    for added in (c3_ref, c2_ref, c1_ref, None):
        at = coarse_step(fields, keep_ref, spread_ref, at, low_end, high_end)
        low_end, high_end = low_end + 1, high_end - 1
        if added is not None:
            for q in range(low_end, high_end):
                fields[at, q] = fields[at, q] + added[q - low_end]
    out_ref[...] = fields[at, low_end:high_end]


def power_kernel(links, window_ref, base_ref, keep_ref, spread_ref, out_ref, fields):
    rows = window_ref.shape[0]
    fields[0] = window_ref[...]
    at = 0
    for link in range(links):
        at = coarse_step(fields, keep_ref, spread_ref, at, link, rows - link)
    out_ref[...] = base_ref[...] + fields[at, links : rows - links]


def chain_call(kernel, rows, *operands):
    return pl.pallas_call(
        kernel,
        out_shape=jax.ShapeDtypeStruct((BLOCK, SLABS, 128), jnp.float32),
        scratch_shapes=[pltpu.VMEM((3, rows, SLABS, 128), jnp.float32)],
        compiler_params=params(),
    )(*operands)


def snake(j):
    return j if j // 8 % 2 == 0 else j // 8 * 8 + 7 - j % 8


def snaked(value):
    return jnp.concatenate([jnp.flip(value[g : g + 8], 0) if g // 8 % 2 else value[g : g + 8] for g in range(0, SLABS, 8)])


def facing(distance, late):
    pairs = []
    for i in range(SLABS - distance):
        if (i // distance) % 2 == late:
            pairs += [(i, i + distance), (i + distance, i)]
    return pairs


def from_later(value, links, pairs):
    pairs = [(snake(i), snake(j)) for i, j in pairs]
    both = [((n + links) * SLABS + i, n * SLABS + j) for n in range(SLICES - links) for i, j in pairs]
    return lax.ppermute(value, ("tm", "space"), both)


def beside_later(value, links, distance, block):
    one = from_later(value, links, facing(distance, 0))
    other = from_later(value, links, facing(distance, 1))
    upper = (block // distance) % 2 == 1
    return jnp.where(upper, one, other), jnp.where(upper, other, one)


def windows(plane, reach):
    blocks = plane.reshape(SLABS, BLOCK, 128)
    padded = jnp.pad(blocks, ((reach, reach), (0, 0), (0, 0)))
    return jnp.concatenate([padded[i : i + SLABS] for i in range(2 * reach + 1)], axis=1)


def to_rows(parts):
    arrived = lax.all_to_all(parts, "space", 0, 0)
    return jnp.transpose(arrived, (1, 0, 2))


def per_device(end_state, cond, receivers, residuals):
    start_field = end_state[0]
    row_count, width_y, width_z = start_field.shape
    plane_size = width_y * width_z
    slab = lax.axis_index("space")
    slice_index = lax.axis_index("tm")
    odd = slab % 2 == 1
    is_final = slice_index == SLICES - 1

    def across_chips(value):
        return lax.ppermute(value, "space", facing(1, 1))

    def in_chip(value):
        return lax.ppermute(value, "space", facing(1, 0))

    def by_side(along, across):
        return jnp.where(odd, along, across), jnp.where(odd, across, along)

    ring = slice_index % 4
    quarter = width_y // 4
    share = lax.dynamic_slice_in_dim(cond, ring * quarter, quarter, axis=1)
    across = across_chips(jnp.where(odd, share[1], share[0]))
    along = in_chip(jnp.where(odd, share[0], share[1]))
    share = jnp.stack(by_side(along, across))
    for bit in (1, 2):
        upper = (ring // bit) % 2 == 1
        other = lax.ppermute(share, "tm", [(n, n ^ bit) for n in range(SLICES)])
        share = jnp.concatenate([jnp.where(upper, other, share), jnp.where(upper, share, other)], axis=1)

    local_row = receivers[0] // plane_size - slab * row_count + 1
    inside = (local_row >= 0) & (local_row < row_count + 2)
    wide_size = (row_count + 2) * plane_size
    target = jnp.where(inside, local_row * plane_size + receivers[0] % plane_size, wide_size)
    flat_source = jnp.zeros((wide_size,), jnp.float32).at[target].add(residuals[0], mode="drop")
    wide_source = flat_source.reshape(row_count + 2, width_y, width_z)
    place = jnp.stack([odd, slab > 0, slab < SLABS - 1, is_final]).astype(jnp.int32)

    coarse_cond = restrict(cond) / FINE_STEPS
    plane_spread = 1.0 / (coarse_cond + 1.5)
    plane_keep = coarse_cond * plane_spread
    plane_spread = 0.25 * plane_spread
    coarse_start = restrict(start_field)

    slab_rows = row_count * width_y
    start_rows = start_field.reshape(slab_rows, width_z)
    around = (share, cond, wide_source, coarse_start, plane_keep, plane_spread)
    across, along = across_chips(start_rows), in_chip(start_rows)
    sent, = step_call(
        first_step_kernel, [(slab_rows + PLANE, 128)], place, across, along, start_rows, *around
    )
    across, along = across_chips(sent), in_chip(sent)
    field_now, term, direct = step_call(
        second_step_kernel, [(slab_rows, 128), (PLANE, 128), (PLANE, 128)], place, across, along, sent, *around
    )
    field_now = field_now.reshape(start_field.shape)

    bits = (ring % 2 == 1, ring // 2 == 1)
    quarters = [windows(coarse_cond, 2)[:, 5 * i : 5 * i + 5] for i in range(4)]
    pairs_of = [jnp.where(bits[0], quarters[i + 1], quarters[i]) for i in (0, 2)]
    cond_windows = jnp.where(bits[1], pairs_of[1], pairs_of[0])
    arrived = to_rows(snaked(jnp.concatenate([windows(term, 1), cond_windows], axis=1)))
    rows, own_cond = arrived[:12], arrived[12:]
    parts = [own_cond]
    for k in (1, 2, 3):
        parts.append(lax.ppermute(own_cond, "tm", [(n // 4 * 4 + (n + k) % 4, n) for n in range(SLICES)]))
    for away, bit in ((1, bits[0]), (2, bits[1])):
        parts = [jnp.where(bit, parts[(i - away) % 4], parts[i]) for i in range(4)]
    row_cond = jnp.concatenate(parts)
    later = [(i, i) for i in range(SLABS)]
    links = {k: from_later(rows[4 - k : 8 + k], k, later) for k in (1, 2, 3, 4)}
    group = slab // 8
    block = jnp.where(group % 2 == 1, 16 * group + 7 - slab, slab)
    row_place = (block - 2) * BLOCK + lax.broadcasted_iota(jnp.int32, row_cond.shape, 0)
    within = (row_place >= 0) & (row_place < PLANE)
    row_spread = jnp.where(within, 1.0 / (row_cond + 1.5), 0.0)
    row_keep = row_cond * row_spread
    row_spread = 0.25 * row_spread

    inner = slice(BLOCK, 4 * BLOCK)
    total = chain_call(
        first_links_kernel, 12, *(links[k] for k in (4, 3, 2, 1)), row_keep[inner], row_spread[inner]
    )

    centre = from_later(total, 4, later)
    before, after = beside_later(total, 4, 1, block)
    window = jnp.concatenate([before, centre, after])
    total = chain_call(
        lambda *refs: power_kernel(4, *refs), 12, window, total, row_keep[inner], row_spread[inner]
    )

    centre = from_later(total, 8, later)
    near = from_later(total, 8, facing(1, 1))
    outward = [(j - 2, j) for j in range(2, SLABS, 2)] + [(j + 2, j) for j in range(1, SLABS - 2, 2)]
    far = from_later(total, 8, outward)
    swapped = from_later(jnp.stack([centre, near]), 0, facing(1, 0))
    window = jnp.where(
        block % 2 == 1,
        jnp.concatenate([swapped[1], swapped[0], centre, near, far]),
        jnp.concatenate([far, near, centre, swapped[0], swapped[1]]),
    )
    total = chain_call(lambda *refs: power_kernel(8, *refs), 20, window, total, row_keep, row_spread)

    back = lax.all_to_all(jnp.transpose(total, (1, 0, 2)), "space", 0, 0)
    propagated = jnp.where(is_final, direct, snaked(back).reshape(PLANE, 128))
    return prolong_add(propagated - direct, field_now)[None]


def solution(mesh):
    in_specs = (P("tm", "space", None, None), P("space", None, None), P("tm", None), P("tm", None))
    out_specs = P("tm", "space", None, None)
    return jax.shard_map(
        per_device, mesh=mesh, in_specs=in_specs, out_specs=out_specs, check_vma=False
    )
```

```python
import jax
import jax.numpy as jnp
from jax import lax
from jax.experimental import pallas as pl
from jax.experimental.pallas import tpu as pltpu
from jax.sharding import PartitionSpec as P

FINE_STEPS = 2
SWEEPS = 2
SLABS = 32
SLICES = 16
PLANE = 128
BLOCK = 4
EXACT = lax.Precision.HIGHEST


def params():
    return pltpu.CompilerParams(vmem_limit_bytes=16 * 1024 * 1024)


def halving(half):
    row = lax.broadcasted_iota(jnp.int32, (128, 128), 0)
    lane = lax.broadcasted_iota(jnp.int32, (128, 128), 1)
    return jnp.where(lane == row // 2 + 64 * half, 0.125, 0.0).astype(jnp.float32)


def restricted(ref, rows):
    total = jnp.zeros((PLANE, 128), jnp.float32)
    for half in range(2):
        parts = [ref[pl.ds(p * rows + 2 * half + r, PLANE, stride=4), :] for p in range(2) for r in range(2)]
        summed = (parts[0] + parts[1]) + (parts[2] + parts[3])
        total = total + jnp.dot(summed, halving(half), precision=EXACT, preferred_element_type=jnp.float32)
    return total


def restrict_kernel(field_ref, out_ref):
    out_ref[...] = restricted(field_ref, field_ref.shape[0] // 2)


def restrict(field):
    return pl.pallas_call(
        restrict_kernel,
        out_shape=jax.ShapeDtypeStruct((PLANE, 128), jnp.float32),
        compiler_params=params(),
    )(field.reshape(-1, 128))


def prolong_add_kernel(delta_ref, field_ref, out_ref):
    row = lax.broadcasted_iota(jnp.int32, (128, 128), 0)
    lane = lax.broadcasted_iota(jnp.int32, (128, 128), 1)
    delta = delta_ref[...]
    for half in range(2):
        spread = jnp.where(row == lane // 2 + 64 * half, 1.0, 0.0).astype(jnp.float32)
        wide = jnp.dot(delta, spread, precision=EXACT, preferred_element_type=jnp.float32)
        for plane in range(2):
            for r in range(2):
                rows = pl.ds(2 * half + r, PLANE, stride=4)
                out_ref[plane, rows, :] = field_ref[plane, rows, :] + wide


def prolong_add(delta, field):
    return pl.pallas_call(
        prolong_add_kernel,
        out_shape=jax.ShapeDtypeStruct(field.shape, jnp.float32),
        compiler_params=params(),
    )(delta, field)


def lanes_of(shape):
    lane = lax.broadcasted_iota(jnp.int32, shape, len(shape) - 1)
    return lane < 64, lane % 64


def beside_z(value, z):
    before = jnp.where(z == 0, 0.0, pltpu.roll(value, 1, 1))
    after = jnp.where(z == 63, 0.0, pltpu.roll(value, 127, 1))
    return before + after


def beside_in_plane(value):
    rows = value.shape[0]
    row = lax.broadcasted_iota(jnp.int32, value.shape, 0)
    lane = lax.broadcasted_iota(jnp.int32, value.shape, 1)
    above = jnp.where(row == 0, 0.0, pltpu.roll(value, 1, 0))
    below = jnp.where(row == rows - 1, 0.0, pltpu.roll(value, rows - 1, 0))
    before = jnp.where(lane == 0, 0.0, pltpu.roll(value, 1, 1))
    after = jnp.where(lane == 127, 0.0, pltpu.roll(value, 127, 1))
    return above + below + before + after


def two_sweeps(place_ref, across_ref, along_ref, field_ref, share_ref, cond_ref, source_ref):
    odd = place_ref[0] == 1
    rows = cond_ref.shape[1]

    def plane(ref, p):
        return ref[p * rows : (p + 1) * rows, :]

    planes = [jnp.where(odd, plane(along_ref, p), plane(across_ref, p)) for p in range(2)]
    planes += [plane(field_ref, p) for p in range(2)]
    planes += [jnp.where(odd, plane(across_ref, p), plane(along_ref, p)) for p in range(2)]
    conds = [share_ref[0], cond_ref[0], cond_ref[1], share_ref[1]]
    terms, inverses, wide = [], [], []
    for i in range(4):
        value = planes[i + 1]
        terms.append(conds[i] * value + source_ref[i])
        inverses.append(1.0 / (conds[i] + 6.0))
        total = planes[i] + planes[i + 2] + beside_in_plane(value)
        wide.append((terms[i] + total) * inverses[i])
    wide[0] = jnp.where(place_ref[1] == 1, wide[0], 0.0)
    wide[3] = jnp.where(place_ref[2] == 1, wide[3], 0.0)
    swept = []
    for p in range(2):
        total = wide[p] + wide[p + 2] + beside_in_plane(wide[p + 1])
        swept.append((terms[p + 1] + total) * inverses[p + 1])
    return swept


def plane_sweep(value, start, beside, keep, spread):
    low, z = lanes_of(value.shape)
    row = lax.broadcasted_iota(jnp.int32, value.shape, 0)
    swapped = pltpu.roll(value, 64, 1)
    earlier = jnp.where(row == 0, 0.0, pltpu.roll(swapped, 1, 0))
    later = jnp.where(row == PLANE - 1, 0.0, pltpu.roll(swapped, PLANE - 1, 0))
    total = beside + swapped + jnp.where(low, earlier, later) + beside_z(value, z)
    return keep * start + spread * total


def first_step_kernel(*refs):
    start_ref, keep_ref, spread_ref, out_ref = refs[7:]
    across_ref, along_ref, cond_ref = refs[1], refs[2], refs[5]
    rows = cond_ref.shape[1]
    for p, value in enumerate(two_sweeps(*refs[:7])):
        out_ref[p * rows : (p + 1) * rows, :] = value
    beside = restricted(across_ref, rows) + restricted(along_ref, rows)
    start = start_ref[...]
    out_ref[2 * rows :, :] = plane_sweep(start, start, beside, keep_ref[...], spread_ref[...])


def second_step_kernel(*refs):
    start_ref, keep_ref, spread_ref, field_ref, term_ref, direct_ref = refs[7:]
    place_ref, across_ref, along_ref, sent_ref, cond_ref = refs[0], refs[1], refs[2], refs[3], refs[5]
    rows = cond_ref.shape[1]
    for p, value in enumerate(two_sweeps(*refs[:7])):
        field_ref[p * rows : (p + 1) * rows, :] = value
    tail = slice(2 * rows, 2 * rows + PLANE)
    beside = across_ref[tail, :] + along_ref[tail, :]
    direct = plane_sweep(sent_ref[tail, :], start_ref[...], beside, keep_ref[...], spread_ref[...])
    direct_ref[...] = direct
    term_ref[...] = restricted(field_ref, rows) - jnp.where(place_ref[3] == 1, 0.0, direct)


def step_call(kernel, shapes, place, *operands):
    in_vmem = pl.BlockSpec(memory_space=pltpu.VMEM)
    return pl.pallas_call(
        kernel,
        out_shape=[jax.ShapeDtypeStruct(shape, jnp.float32) for shape in shapes],
        in_specs=[pl.BlockSpec(memory_space=pltpu.SMEM)] + [in_vmem] * len(operands),
        out_specs=[in_vmem] * len(shapes),
        compiler_params=params(),
    )(place, *operands)


def sweep_rows(source, start, keep, spread, target, first, last, low_end, high_end):
    shape = (SLABS, 128)
    low, z = lanes_of(shape)
    x = lax.broadcasted_iota(jnp.int32, shape, 0)
    zero = jnp.zeros(shape, jnp.float32)

    def swapped(q):
        return pltpu.roll(source[q], 64, 1) if low_end <= q < high_end else zero

    earlier, here = swapped(first - 1), swapped(first)
    for q in range(first, last):
        later = swapped(q + 1)
        value = source[q]
        total = here + jnp.where(low, earlier, later) + beside_z(value, z)
        total = total + jnp.where(x == 0, 0.0, pltpu.roll(value, 1, 0))
        total = total + jnp.where(x == SLABS - 1, 0.0, pltpu.roll(value, SLABS - 1, 0))
        target[q] = keep[q] * start[q] + spread[q] * total
        earlier, here = here, later


def coarse_step(fields, keep, spread, at, low_end, high_end):
    start, middle, result = fields.at[at], fields.at[2], fields.at[1 - at]
    sweep_rows(start, start, keep, spread, middle, low_end, high_end, low_end, high_end)
    sweep_rows(middle, start, keep, spread, result, low_end + 1, high_end - 1, low_end, high_end)
    return 1 - at


def first_links_kernel(c4_ref, c3_ref, c2_ref, c1_ref, keep_ref, spread_ref, out_ref, fields):
    rows = c4_ref.shape[0]
    fields[0] = c4_ref[...]
    at, low_end, high_end = 0, 0, rows
    for added in (c3_ref, c2_ref, c1_ref, None):
        at = coarse_step(fields, keep_ref, spread_ref, at, low_end, high_end)
        low_end, high_end = low_end + 1, high_end - 1
        if added is not None:
            for q in range(low_end, high_end):
                fields[at, q] = fields[at, q] + added[q - low_end]
    out_ref[...] = fields[at, low_end:high_end]


def power_kernel(links, window_ref, base_ref, keep_ref, spread_ref, out_ref, fields):
    rows = window_ref.shape[0]
    fields[0] = window_ref[...]
    at = 0
    for link in range(links):
        at = coarse_step(fields, keep_ref, spread_ref, at, link, rows - link)
    out_ref[...] = base_ref[...] + fields[at, links : rows - links]


def chain_call(kernel, rows, *operands):
    return pl.pallas_call(
        kernel,
        out_shape=jax.ShapeDtypeStruct((BLOCK, SLABS, 128), jnp.float32),
        scratch_shapes=[pltpu.VMEM((3, rows, SLABS, 128), jnp.float32)],
        compiler_params=params(),
    )(*operands)


def snake(j):
    return j if j // 8 % 2 == 0 else j // 8 * 8 + 7 - j % 8


def snaked(value):
    return jnp.concatenate([jnp.flip(value[g : g + 8], 0) if g // 8 % 2 else value[g : g + 8] for g in range(0, SLABS, 8)])


def facing(distance, late):
    pairs = []
    for i in range(SLABS - distance):
        if (i // distance) % 2 == late:
            pairs += [(i, i + distance), (i + distance, i)]
    return pairs


def from_later(value, links, pairs):
    pairs = [(snake(i), snake(j)) for i, j in pairs]
    both = [((n + links) * SLABS + i, n * SLABS + j) for n in range(SLICES - links) for i, j in pairs]
    return lax.ppermute(value, ("tm", "space"), both)


def beside_later(value, links, distance, block):
    one = from_later(value, links, facing(distance, 0))
    other = from_later(value, links, facing(distance, 1))
    upper = (block // distance) % 2 == 1
    return jnp.where(upper, one, other), jnp.where(upper, other, one)


def windows(plane, reach):
    blocks = plane.reshape(SLABS, BLOCK, 128)
    padded = jnp.pad(blocks, ((reach, reach), (0, 0), (0, 0)))
    return jnp.concatenate([padded[i : i + SLABS] for i in range(2 * reach + 1)], axis=1)


def to_rows(parts):
    arrived = lax.all_to_all(parts, "space", 0, 0)
    return jnp.transpose(arrived, (1, 0, 2))


def per_device(end_state, cond, receivers, residuals):
    start_field = end_state[0]
    row_count, width_y, width_z = start_field.shape
    plane_size = width_y * width_z
    slab = lax.axis_index("space")
    slice_index = lax.axis_index("tm")
    odd = slab % 2 == 1
    is_final = slice_index == SLICES - 1

    def across_chips(value):
        return lax.ppermute(value, "space", facing(1, 1))

    def in_chip(value):
        return lax.ppermute(value, "space", facing(1, 0))

    def by_side(along, across):
        return jnp.where(odd, along, across), jnp.where(odd, across, along)

    ring = slice_index % 4
    quarter = width_y // 4
    share = lax.dynamic_slice_in_dim(cond, ring * quarter, quarter, axis=1)
    across = across_chips(jnp.where(odd, share[1], share[0]))
    along = in_chip(jnp.where(odd, share[0], share[1]))
    share = jnp.stack(by_side(along, across))
    for bit in (1, 2):
        upper = (ring // bit) % 2 == 1
        other = lax.ppermute(share, "tm", [(n, n ^ bit) for n in range(SLICES)])
        share = jnp.concatenate([jnp.where(upper, other, share), jnp.where(upper, share, other)], axis=1)

    local_row = receivers[0] // plane_size - slab * row_count + 1
    inside = (local_row >= 0) & (local_row < row_count + 2)
    wide_size = (row_count + 2) * plane_size
    target = jnp.where(inside, local_row * plane_size + receivers[0] % plane_size, wide_size)
    flat_source = jnp.zeros((wide_size,), jnp.float32).at[target].add(residuals[0], mode="drop")
    wide_source = flat_source.reshape(row_count + 2, width_y, width_z)
    place = jnp.stack([odd, slab > 0, slab < SLABS - 1, is_final]).astype(jnp.int32)

    coarse_cond = restrict(cond) / FINE_STEPS
    plane_spread = 1.0 / (coarse_cond + 1.5)
    plane_keep = coarse_cond * plane_spread
    plane_spread = 0.25 * plane_spread
    coarse_start = restrict(start_field)

    slab_rows = row_count * width_y
    start_rows = start_field.reshape(slab_rows, width_z)
    around = (share, cond, wide_source, coarse_start, plane_keep, plane_spread)
    across, along = across_chips(start_rows), in_chip(start_rows)
    sent, = step_call(
        first_step_kernel, [(slab_rows + PLANE, 128)], place, across, along, start_rows, *around
    )
    across, along = across_chips(sent), in_chip(sent)
    field_now, term, direct = step_call(
        second_step_kernel, [(slab_rows, 128), (PLANE, 128), (PLANE, 128)], place, across, along, sent, *around
    )
    field_now = field_now.reshape(start_field.shape)

    second_half = slice_index % 2 == 1
    cond_windows = windows(coarse_cond, 2)
    cond_windows = jnp.where(second_half, cond_windows[:, 10:], cond_windows[:, :10])
    arrived = to_rows(snaked(jnp.concatenate([windows(term, 1), cond_windows], axis=1)))
    rows, own_cond = arrived[:12], arrived[12:]
    other_cond = lax.ppermute(own_cond, "tm", [(n, n ^ 1) for n in range(SLICES)])
    row_cond = jnp.concatenate(
        [jnp.where(second_half, other_cond, own_cond), jnp.where(second_half, own_cond, other_cond)]
    )
    later = [(i, i) for i in range(SLABS)]
    links = {k: from_later(rows[4 - k : 8 + k], k, later) for k in (1, 2, 3, 4)}
    group = slab // 8
    block = jnp.where(group % 2 == 1, 16 * group + 7 - slab, slab)
    row_place = (block - 2) * BLOCK + lax.broadcasted_iota(jnp.int32, row_cond.shape, 0)
    within = (row_place >= 0) & (row_place < PLANE)
    row_spread = jnp.where(within, 1.0 / (row_cond + 1.5), 0.0)
    row_keep = row_cond * row_spread
    row_spread = 0.25 * row_spread

    inner = slice(BLOCK, 4 * BLOCK)
    total = chain_call(
        first_links_kernel, 12, *(links[k] for k in (4, 3, 2, 1)), row_keep[inner], row_spread[inner]
    )

    centre = from_later(total, 4, later)
    before, after = beside_later(total, 4, 1, block)
    window = jnp.concatenate([before, centre, after])
    total = chain_call(
        lambda *refs: power_kernel(4, *refs), 12, window, total, row_keep[inner], row_spread[inner]
    )

    centre = from_later(total, 8, later)
    near = from_later(total, 8, facing(1, 1))
    outward = [(j - 2, j) for j in range(2, SLABS, 2)] + [(j + 2, j) for j in range(1, SLABS - 2, 2)]
    far = from_later(total, 8, outward)
    swapped = from_later(jnp.stack([centre, near]), 0, facing(1, 0))
    window = jnp.where(
        block % 2 == 1,
        jnp.concatenate([swapped[1], swapped[0], centre, near, far]),
        jnp.concatenate([far, near, centre, swapped[0], swapped[1]]),
    )
    total = chain_call(lambda *refs: power_kernel(8, *refs), 20, window, total, row_keep, row_spread)

    back = lax.all_to_all(jnp.transpose(total, (1, 0, 2)), "space", 0, 0)
    propagated = jnp.where(is_final, direct, snaked(back).reshape(PLANE, 128))
    return prolong_add(propagated - direct, field_now)[None]


def solution(mesh):
    in_specs = (P("tm", "space", None, None), P("space", None, None), P("tm", None), P("tm", None))
    out_specs = P("tm", "space", None, None)
    return jax.shard_map(
        per_device, mesh=mesh, in_specs=in_specs, out_specs=out_specs, check_vma=False
    )
```
